32 devices in a mesh: videos: 8 (over z, x), heads: 4 (over y, core).
Axes of the slice: x: 2, y: 2, z: 4, core: 2. Of those that a mesh axis runs over, the one named last changes fastest.
Arguments:
- frames: bfloat16 [8, 8, 328, 768], P('videos', None, 'heads'), may hold values from -6 to 6
- out_grad: bfloat16 [8, 8, 328, 768], P('videos', None, 'heads'), may hold values from -6 to 6
- frame_tokens: int32 [8], P('videos'), may hold values from 197 to 325, as said below
- frame_count: int32 [8], P('videos'), may hold values from 2 to 8, as said below
- msg_fc_w: bfloat16 [768, 768], P(None, 'heads'), may hold values from -0.21875 to 0.21875
- msg_fc_b: bfloat16 [768], P('heads'), may hold values from -2 to 2
- msg_norm_g: bfloat16 [768], replicated, may hold values from 0.5 to 1.5
- msg_norm_b: bfloat16 [768], replicated, may hold values from -2 to 2
- msg_qkv_w: bfloat16 [3, 768, 768], P(None, None, 'heads'), may hold values from -0.21875 to 0.21875
- msg_qkv_b: bfloat16 [2, 768], P(None, 'heads'), may hold values from -2 to 2
- msg_out_w: bfloat16 [768, 768], P('heads'), may hold values from -0.4375 to 0.4375
- msg_out_b: bfloat16 [768], replicated, may hold values from -2 to 2
- norm1_g: bfloat16 [768], replicated, may hold values from 0.5 to 1.5
- norm1_b: bfloat16 [768], replicated, may hold values from -2 to 2
- attn_qkv_w: bfloat16 [3, 768, 768], P(None, None, 'heads'), may hold values from -0.21875 to 0.21875
- attn_qkv_b: bfloat16 [2, 768], P(None, 'heads'), may hold values from -2 to 2
- attn_out_w: bfloat16 [768, 768], P('heads'), may hold values from -1.75 to 1.75
- attn_out_b: bfloat16 [768], replicated, may hold values from -2 to 2
- norm2_g: bfloat16 [768], replicated, may hold values from 0.5 to 1.5
- norm2_b: bfloat16 [768], replicated, may hold values from -2 to 2
- fc1_w: bfloat16 [768, 3072], P(None, 'heads'), may hold values from -0.21875 to 0.21875
- fc1_b: bfloat16 [3072], P('heads'), may hold values from -2 to 2
- fc2_w: bfloat16 [3072, 768], P('heads'), may hold values from -0.109375 to 0.109375
- fc2_b: bfloat16 [768], replicated, may hold values from -2 to 2
Outputs:
- mixed_out: bfloat16 [8, 8, 328, 768], P('videos', None, 'heads')
- frames_grad: float32 [8, 8, 328, 768], P('videos', None, 'heads')
- msg_fc_w_grad: float32 [768, 768], P(None, 'heads')
- msg_fc_b_grad: float32 [768], P('heads')
- msg_norm_g_grad: float32 [768], P('heads')
- msg_norm_b_grad: float32 [768], P('heads')
- msg_qkv_w_grad: float32 [3, 768, 768], P(None, None, 'heads')
- msg_qkv_b_grad: float32 [2, 768], P(None, 'heads')
- msg_out_w_grad: float32 [768, 768], P('heads')
- msg_out_b_grad: float32 [768], P('heads')
- norm1_g_grad: float32 [768], P('heads')
- norm1_b_grad: float32 [768], P('heads')
- attn_qkv_w_grad: float32 [3, 768, 768], P(None, None, 'heads')
- attn_qkv_b_grad: float32 [2, 768], P(None, 'heads')
- attn_out_w_grad: float32 [768, 768], P('heads')
- attn_out_b_grad: float32 [768], P('heads')
- norm2_g_grad: float32 [768], P('heads')
- norm2_b_grad: float32 [768], P('heads')
- fc1_w_grad: float32 [768, 3072], P(None, 'heads')
- fc1_b_grad: float32 [3072], P('heads')
- fc2_w_grad: float32 [3072, 768], P('heads')
- fc2_b_grad: float32 [768], P('heads')
The draws below stay inside these ranges and needn't reach their ends.
Inputs may be any that keep to these rules, and one draw needn't show every extreme that they name: `frame_tokens`: each video has 197 or 325 tokens a frame, and some video has 325. `frame_count`: some video has 8.
All inputs are finite; a program needn't handle non-finite values.
Results may differ from the reference program's by a relative error of at most 0.025.
Values may be sent and summed in bfloat16 or wider, within the bound.
No kernel may reach another device: no remote copies, remote signals or barrier semaphores. Data moves between devices by JAX's collectives and lax.ppermute only.
A program may use at most 192 MiB of HBM per device.

```python
import jax
import jax.numpy as jnp
from jax import lax

HEAD_DIM = 64
FF = 3072
D = 768
FRAMES = 8
ROWS = 328
BIG_TOK = 325
SMALL_TOK = 197
VIDEOS = 8


def draw_frame_tokens(key, part):
    key = jax.random.fold_in(key, 11)
    pick_key, place_key = jax.random.split(key)
    picks = jax.random.randint(pick_key, (VIDEOS,), 0, 2)
    forced = jax.random.randint(place_key, (), 0, VIDEOS)
    picks = jnp.where(jnp.arange(VIDEOS) == forced, 1, picks)
    return jnp.where(picks == 1, BIG_TOK, SMALL_TOK).astype(jnp.int32)


def draw_frame_count(key, part):
    key = jax.random.fold_in(key, 23)
    pick_key, place_key = jax.random.split(key)
    counts = jax.random.randint(pick_key, (VIDEOS,), 2, FRAMES + 1)
    forced = jax.random.randint(place_key, (), 0, VIDEOS)
    counts = jnp.where(jnp.arange(VIDEOS) == forced, FRAMES, counts)
    return counts.astype(jnp.int32)


def levels(rng, dims, cuts, low, high):
    def one(position, shards_of):
        steps = jax.random.uniform(jax.random.fold_in(jax.random.fold_in(rng, 6), position), (shards_of,), jnp.float32, low / len(cuts), high / len(cuts))
        return jnp.repeat(jnp.exp(steps), dims[position] // shards_of).reshape((-1,) + (1,) * (len(dims) - position - 1))

    gain = one(*cuts[0])
    for cut in cuts[1:]:
        gain = gain * one(*cut)
    return gain


def centred(stream_key, shape, deviation, bound, pieces=(), dtype=jnp.bfloat16):
    factor_of = levels(stream_key, shape, pieces, -0.22, 0.18) if pieces else 1.0
    result = jax.random.normal(stream_key, shape, jnp.float32) * deviation * factor_of
    return jnp.minimum(jnp.maximum(result, -bound), bound).astype(dtype)


def setup_inputs(seed: int = 0) -> dict:
    arg_keys = jax.random.split(jax.random.key(seed), 25)
    return {
        "frames": centred(arg_keys[0], (VIDEOS, FRAMES, ROWS, D), 1.0, 6.0, ((0, 8), (2, 4))),
        "out_grad": centred(arg_keys[1], (VIDEOS, FRAMES, ROWS, D), 1.0, 6.0, ((0, 8), (2, 4))),
        "frame_tokens": draw_frame_tokens(jax.random.fold_in(arg_keys[24], 71), 0),
        "frame_count": draw_frame_count(jax.random.fold_in(arg_keys[24], 71), 0),
        "msg_fc_w": centred(arg_keys[4], (D, D), D ** -0.5, 0.21875, ((1, 4),)),
        "msg_fc_b": centred(arg_keys[5], (D,), 0.3, 2.0, ((0, 4),)),
        "msg_norm_g": jnp.clip(1.0 + 0.1 * jax.random.normal(arg_keys[6], (D,), jnp.float32), 0.5, 1.5).astype(jnp.bfloat16),
        "msg_norm_b": centred(arg_keys[7], (D,), 0.3, 2.0),
        "msg_qkv_w": centred(arg_keys[8], (3, D, D), D ** -0.5, 0.21875, ((2, 4),)),
        "msg_qkv_b": centred(arg_keys[9], (2, D), 0.3, 2.0, ((1, 4),)),
        "msg_out_w": centred(arg_keys[10], (D, D), (D // 4) ** -0.5, 0.4375, ((0, 4),)),
        "msg_out_b": centred(arg_keys[11], (D,), 0.3, 2.0),
        "norm1_g": jnp.clip(1.0 + 0.1 * jax.random.normal(arg_keys[12], (D,), jnp.float32), 0.5, 1.5).astype(jnp.bfloat16),
        "norm1_b": centred(arg_keys[13], (D,), 0.3, 2.0),
        "attn_qkv_w": centred(arg_keys[14], (3, D, D), D ** -0.5, 0.21875, ((2, 4),)),
        "attn_qkv_b": centred(arg_keys[15], (2, D), 0.3, 2.0, ((1, 4),)),
        "attn_out_w": centred(arg_keys[16], (D, D), (D // 64) ** -0.5, 1.75, ((0, 4),)),
        "attn_out_b": centred(arg_keys[17], (D,), 0.3, 2.0),
        "norm2_g": jnp.clip(1.0 + 0.1 * jax.random.normal(arg_keys[18], (D,), jnp.float32), 0.5, 1.5).astype(jnp.bfloat16),
        "norm2_b": centred(arg_keys[19], (D,), 0.3, 2.0),
        "fc1_w": centred(arg_keys[20], (D, FF), D ** -0.5, 0.21875, ((1, 4),)),
        "fc1_b": centred(arg_keys[21], (FF,), 0.3, 2.0, ((0, 4),)),
        "fc2_w": centred(arg_keys[22], (FF, D), FF ** -0.5, 0.109375, ((0, 4),)),
        "fc2_b": centred(arg_keys[23], (D,), 0.3, 2.0),
    }


@jax.custom_vjp
def low(v):
    return lax.optimization_barrier(v.astype(jnp.bfloat16)).astype(jnp.float32)

@jax.custom_vjp
def low_back(v):
    return v

def low_keep(v):
    return (low(v), None)

def low_pass(kept, grad):
    return (grad,)

def back_keep(v):
    return (v, None)

def back_low(kept, grad):
    return (low(grad),)
low.defvjp(low_keep, low_pass)
low_back.defvjp(back_keep, back_low)
highest = lax.Precision.HIGHEST
epsilon = 1e-05

def both_ways(value):
    return low(low_back(value))

def normalize(value, gains, offset):
    average = lax.optimization_barrier(jnp.mean(value, -1, keepdims=True))
    centered = value - average
    spread = lax.optimization_barrier(jnp.mean(centered * centered, -1, keepdims=True))
    return centered * lax.rsqrt(spread + epsilon) * gains + offset

def attend(normed, weight, biases, keymask):
    batches, length, features = normed.shape
    queries = both_ways(jnp.einsum('bld,de->ble', normed, weight[0], precision=highest) + biases[0])
    key_rows = both_ways(jnp.einsum('bld,de->ble', normed, weight[1], precision=highest))
    values = both_ways(jnp.einsum('bld,de->ble', normed, weight[2], precision=highest) + biases[1])
    split_shape = (batches, length, features // HEAD_DIM, HEAD_DIM)
    queries = queries.reshape(split_shape)
    key_rows = key_rows.reshape(split_shape)
    values = values.reshape(split_shape)
    scores = low_back(jnp.einsum('bqhe,bkhe->bhqk', queries, key_rows, precision=highest) * HEAD_DIM ** (-0.5))
    scores = jnp.where(keymask, scores, -1e+30)
    largest = lax.optimization_barrier(jnp.max(scores, -1, keepdims=True))
    exponent = jnp.exp(scores - largest)
    chances = exponent / lax.optimization_barrier(jnp.sum(exponent, -1, keepdims=True))
    output = jnp.einsum('bhqk,bkhe->bqhe', low(chances), values, precision=highest)
    return both_ways(output).reshape(batches, length, features)

def one_video(frame_block, params, tokens, count):
    msg_fc_w, msg_fc_b, msg_norm_g, msg_norm_b, msg_qkv_w, msg_qkv_b, msg_out_w, msg_out_b, norm1_g, norm1_b, attn_qkv_w, attn_qkv_b, attn_out_w, attn_out_b, norm2_g, norm2_b, fc1_w, fc1_b, fc2_w, fc2_b = params
    message = low_back(jnp.dot(frame_block[:, 0, :], msg_fc_w, precision=highest) + msg_fc_b)
    msg_normed = low(normalize(message, msg_norm_g, msg_norm_b))
    frame_keys = (jnp.arange(FRAMES) < count)[None, None, None, :]
    msg_heads = attend(msg_normed[None], msg_qkv_w, msg_qkv_b, frame_keys)[0]
    carried = message + low_back(jnp.dot(msg_heads, msg_out_w, precision=highest) + msg_out_b)
    joined = jnp.concatenate([frame_block, carried[:, None, :]], 1)
    normed = low(normalize(joined, norm1_g, norm1_b))
    places = jnp.arange(ROWS + 1)
    row_keys = ((places < tokens) | (places == ROWS))[None, None, None, :]
    heads_out = attend(normed, attn_qkv_w, attn_qkv_b, row_keys)
    attn_branch = low_back(jnp.dot(heads_out, attn_out_w, precision=highest) + attn_out_b)
    mixed_rows = (joined + attn_branch)[:, :ROWS]
    normed_two = low(normalize(mixed_rows, norm2_g, norm2_b))
    hidden = low_back(jnp.dot(normed_two, fc1_w, precision=highest) + fc1_b)
    active = low(hidden * jax.nn.sigmoid(1.702 * hidden))
    return mixed_rows + low_back(jnp.dot(active, fc2_w, precision=highest) + fc2_b)

def reference(frames, out_grad, frame_tokens, frame_count, msg_fc_w, msg_fc_b, msg_norm_g, msg_norm_b, msg_qkv_w, msg_qkv_b, msg_out_w, msg_out_b, norm1_g, norm1_b, attn_qkv_w, attn_qkv_b, attn_out_w, attn_out_b, norm2_g, norm2_b, fc1_w, fc1_b, fc2_w, fc2_b):
    params = tuple((weight.astype(jnp.float32) for weight in (msg_fc_w, msg_fc_b, msg_norm_g, msg_norm_b, msg_qkv_w, msg_qkv_b, msg_out_w, msg_out_b, norm1_g, norm1_b, attn_qkv_w, attn_qkv_b, attn_out_w, attn_out_b, norm2_g, norm2_b, fc1_w, fc1_b, fc2_w, fc2_b)))

    def forward(inputs, weights):

        def per_video(element):
            frame_block, tokens, count = element
            return jax.checkpoint(one_video)(frame_block, weights, tokens, count)
        return lax.map(per_video, (inputs, frame_tokens, frame_count))
    mixed_rows, pullback = jax.vjp(forward, frames.astype(jnp.float32), params)
    frames_grad, grads = pullback(out_grad.astype(jnp.float32))
    return (mixed_rows.astype(jnp.bfloat16), frames_grad, grads[0], grads[1], grads[2], grads[3], grads[4], grads[5], grads[6], grads[7], grads[8], grads[9], grads[10], grads[11], grads[12], grads[13], grads[14], grads[15], grads[16], grads[17], grads[18], grads[19])
```

```python
import jax
import jax.numpy as jnp
from jax import lax
from jax.sharding import PartitionSpec as P

HEAD_DIM = 64


epsilon = 1e-05


def norm_forward(value, gains, offset):
    average = jnp.mean(value, -1, keepdims=True)
    centered = value - average
    spread = jnp.mean(centered * centered, -1, keepdims=True)
    inverse = lax.rsqrt(spread + epsilon)
    unit = centered * inverse
    return (unit * gains.astype(jnp.float32) + offset.astype(jnp.float32), unit, inverse)


def norm_backward(gradient, unit, inverse, gains):
    scaled = gradient * gains.astype(jnp.float32)
    average = jnp.mean(scaled, -1, keepdims=True)
    second = jnp.mean(scaled * unit, -1, keepdims=True)
    return inverse * (scaled - average - unit * second)


def split_heads(tensors):
    return tuple(
        (
            tensor.reshape(tensor.shape[:-1] + (tensor.shape[-1] // HEAD_DIM, HEAD_DIM))
            for tensor in tensors
        )
    )


def project(normed, weight, biases):
    stacked = jnp.einsum("...d,cde->c...e", normed, weight, preferred_element_type=jnp.float32)
    return (
        (stacked[0] + biases[0]).astype(jnp.bfloat16),
        stacked[1].astype(jnp.bfloat16),
        (stacked[2] + biases[1]).astype(jnp.bfloat16),
    )


def attend_forward(queries, key_rows, values, keymask):
    scale_factor = HEAD_DIM ** (-0.5)
    scores = (
        jnp.einsum("bqhe,bkhe->bhqk", queries, key_rows, preferred_element_type=jnp.float32)
        * scale_factor
    )
    scores = jnp.where(keymask, scores, -1e30)
    largest = jnp.max(scores, -1, keepdims=True)
    exponent = jnp.exp(scores - largest)
    totals = jnp.sum(exponent, -1, keepdims=True)
    chances = exponent / totals
    output = jnp.einsum(
        "bhqk,bkhe->bqhe", chances.astype(jnp.bfloat16), values, preferred_element_type=jnp.float32
    )
    return (output.astype(jnp.bfloat16), largest + jnp.log(totals))


def attend_backward(queries, key_rows, values, keymask, log_total, grad_heads):
    scale_factor = HEAD_DIM ** (-0.5)
    scores = (
        jnp.einsum("bqhe,bkhe->bhqk", queries, key_rows, preferred_element_type=jnp.float32)
        * scale_factor
    )
    scores = jnp.where(keymask, scores, -1e30)
    chances = jnp.exp(scores - log_total)
    grad_chances = jnp.einsum(
        "bqhe,bkhe->bhqk", grad_heads, values, preferred_element_type=jnp.float32
    )
    deltas = jnp.sum(chances * grad_chances, -1, keepdims=True)
    grad_scores = (chances * (grad_chances - deltas)).astype(jnp.bfloat16)
    grad_query = (
        jnp.einsum("bhqk,bkhe->bqhe", grad_scores, key_rows, preferred_element_type=jnp.float32)
        * scale_factor
    ).astype(jnp.bfloat16)
    grad_key = (
        jnp.einsum("bhqk,bqhe->bkhe", grad_scores, queries, preferred_element_type=jnp.float32)
        * scale_factor
    ).astype(jnp.bfloat16)
    grad_value = jnp.einsum(
        "bhqk,bqhe->bkhe",
        chances.astype(jnp.bfloat16),
        grad_heads,
        preferred_element_type=jnp.float32,
    ).astype(jnp.bfloat16)
    return (grad_query, grad_key, grad_value)


def swap(value, axis, offset):
    size = lax.axis_size(axis)
    return lax.ppermute(value, axis, [(place, place ^ offset) for place in range(size)])


def pick(value, index, count):
    return lax.dynamic_slice_in_dim(value, index * count, count, 0)


def scatter_frames(frames, here, groups):
    slots, rows, features = frames.shape
    mine = slots // groups
    return [
        swap(pick(frames, here ^ offset, mine), "heads", offset)
        if offset
        else pick(frames, here, mine)
        for offset in range(groups)
    ]


def return_frames(value, here, groups, rows):
    mine, _, features = value.shape
    pieces = []
    for offset in range(groups):
        piece = value[:, offset * rows : (offset + 1) * rows]
        pieces.append(swap(piece, "heads", offset) if offset else piece)
    stacked = jnp.stack(pieces)
    order = jnp.arange(groups) ^ here
    return jnp.concatenate(
        [lax.dynamic_index_in_dim(stacked, here ^ place, 0, False) for place in range(groups)], 0
    )


def gather_blocks(block, groups):
    blocks = [block]
    offset = groups // 2
    found = {0: block}
    while offset:
        for known in list(found):
            found[known ^ offset] = swap(found[known], "heads", offset)
        offset //= 2
    return [found[place] for place in range(groups)]


def on_device(
    frames,
    out_grad,
    frame_tokens,
    frame_count,
    msg_fc_w,
    msg_fc_b,
    msg_norm_g,
    msg_norm_b,
    msg_qkv_w,
    msg_qkv_b,
    msg_out_w,
    msg_out_b,
    norm1_g,
    norm1_b,
    attn_qkv_w,
    attn_qkv_b,
    attn_out_w,
    attn_out_b,
    norm2_g,
    norm2_b,
    fc1_w,
    fc1_b,
    fc2_w,
    fc2_b,
):
    low = jnp.bfloat16
    full = jnp.float32
    _, slots, rows, features = frames.shape
    groups = lax.axis_size("heads")
    here = lax.axis_index("heads")
    mine = slots // groups
    all_rows = rows * groups
    padded = -(-(all_rows + 1) // 16) * 16
    width = msg_fc_w.shape[1]
    hidden_width = fc1_w.shape[1]
    frames = frames[0]
    out_grad = out_grad[0]

    row_blocks = scatter_frames(frames, here, groups)
    attn_pack = jnp.concatenate(
        [attn_qkv_w.transpose(0, 2, 1).reshape(3 * width, features), attn_out_w], 0
    )
    attn_packs = gather_blocks(attn_pack, groups)
    small_bias = jnp.concatenate([attn_qkv_b.reshape(-1), fc1_b])
    small_packs = lax.all_gather(small_bias, "heads")
    small_packs = [
        lax.dynamic_index_in_dim(small_packs, here ^ offset, 0, False) for offset in range(groups)
    ]
    fc_pack = jnp.stack([fc1_w, fc2_w])
    fc_packs = gather_blocks(fc_pack, groups)
    grad_blocks = scatter_frames(out_grad, here, groups)

    leading = lax.all_gather(frames[:, 0, :], "heads")[0]
    fc_part = jnp.dot(leading, msg_fc_w, preferred_element_type=full) + msg_fc_b
    message = lax.all_gather(fc_part, "heads", axis=1, tiled=True)
    msg_normed, msg_unit, msg_inverse = norm_forward(message, msg_norm_g, msg_norm_b)
    msg_in = msg_normed.astype(low)
    frame_mask = (jnp.arange(slots) < frame_count[0])[None, None, None, :]
    msg_query, msg_key, msg_value = split_heads(project(msg_in[None], msg_qkv_w, msg_qkv_b))
    msg_heads, msg_lse = attend_forward(msg_query, msg_key, msg_value, frame_mask)
    msg_flat = msg_heads.reshape(slots, width)
    msg_part = jnp.dot(msg_flat, msg_out_w, preferred_element_type=full)
    carried = message + jnp.sum(lax.all_gather(msg_part, "heads"), 0) + msg_out_b
    carried = pick(carried, here, mine)

    places = jnp.concatenate(
        [(here ^ offset) * rows + jnp.arange(rows) for offset in range(groups)]
    )
    tail = padded - all_rows
    row_mask = jnp.concatenate([places < frame_tokens[0], jnp.arange(tail) == 0])
    row_mask = row_mask[None, None, None, :]
    joined = jnp.concatenate(
        row_blocks
        + [carried[:, None, :].astype(low), jnp.zeros((mine, tail - 1, features), low)],
        1,
    ).astype(full)
    normed, unit, inverse = norm_forward(joined, norm1_g, norm1_b)
    normed = normed.astype(low)
    qkv_w = [
        jnp.concatenate([pack[part * width : (part + 1) * width] for pack in attn_packs], 0)
        for part in range(4)
    ]
    q_bias = jnp.concatenate([pack[:width] for pack in small_packs])
    v_bias = jnp.concatenate([pack[width : 2 * width] for pack in small_packs])
    fc1_bias = jnp.concatenate([pack[2 * width :] for pack in small_packs])

    def against(value, weight):
        return jnp.einsum("frd,ed->fre", value, weight, preferred_element_type=full)

    queries = (against(normed, qkv_w[0]) + q_bias).astype(low)
    key_rows = against(normed, qkv_w[1]).astype(low)
    values = (against(normed, qkv_w[2]) + v_bias).astype(low)
    queries, key_rows, values = split_heads((queries, key_rows, values))
    attn_heads, attn_lse = attend_forward(queries, key_rows, values, row_mask)
    attn_flat = attn_heads.reshape(mine, padded, features)
    attn_rows = attn_flat[:, :all_rows]
    mixed = (
        joined[:, :all_rows]
        + jnp.einsum("fre,ed->frd", attn_rows, qkv_w[3], preferred_element_type=full)
        + attn_out_b
    )

    normed_two, unit_two, inverse_two = norm_forward(mixed, norm2_g, norm2_b)
    mlp_in = normed_two.astype(low)
    fc1_full = jnp.concatenate([pack[0] for pack in fc_packs], 1)
    fc2_full = jnp.concatenate([pack[1] for pack in fc_packs], 0)
    hidden = jnp.einsum("frd,dk->frk", mlp_in, fc1_full, preferred_element_type=full) + fc1_bias
    gate = jax.nn.sigmoid(1.702 * hidden)
    active = (hidden * gate).astype(low)
    mixed_out = (
        mixed + jnp.einsum("frk,kd->frd", active, fc2_full, preferred_element_type=full) + fc2_b
    ).astype(low)
    mixed_out = return_frames(mixed_out, here, groups, rows)

    grad_low = jnp.concatenate(grad_blocks, 1)
    grad_top = grad_low.astype(full)
    grad_active = jnp.einsum("frd,kd->frk", grad_low, fc2_full, preferred_element_type=full)
    grad_hidden = (grad_active * (gate + 1.702 * hidden * gate * (1.0 - gate))).astype(low)
    grad_normed_two = jnp.einsum("frk,dk->frd", grad_hidden, fc1_full, preferred_element_type=full)
    grad_mixed = grad_top + norm_backward(grad_normed_two, unit_two, inverse_two, norm2_g)
    grad_attn = grad_mixed.astype(low)

    def by_block(value, axis):
        return jnp.split(value, groups, axis)

    active_blocks = by_block(active, 2)
    hidden_blocks = by_block(grad_hidden, 2)

    def fc_grads(block):
        return jnp.stack(
            [
                jnp.einsum("frd,frk->dk", mlp_in, hidden_blocks[block], preferred_element_type=full),
                jnp.einsum("frk,frd->kd", active_blocks[block], grad_low, preferred_element_type=full),
            ]
        ).astype(low)

    def collect(blocks):
        blocks = dict(enumerate(blocks))
        offset = 1
        while offset < groups:
            for place in [place for place in blocks if place & offset]:
                came = swap(blocks.pop(place), "heads", offset)
                kept = place ^ offset
                blocks[kept] = (blocks[kept].astype(full) + came.astype(full)).astype(low)
            offset *= 2
        return blocks[0]

    fc_total = collect([fc_grads(block) for block in range(groups)])
    fc_total = lax.psum(fc_total, "videos").astype(full)

    grad_o = jnp.einsum("frd,ed->fre", grad_attn, qkv_w[3], preferred_element_type=full).astype(low)
    grad_o = jnp.concatenate([grad_o, jnp.zeros((mine, tail, features), low)], 1)
    grad_query, grad_key, grad_value = attend_backward(
        queries, key_rows, values, row_mask, attn_lse, split_heads((grad_o,))[0]
    )
    parts = [part.reshape(mine, padded, features) for part in (grad_query, grad_key, grad_value)]
    grad_normed = sum(
        jnp.einsum("fre,ed->frd", part, weight, preferred_element_type=full)
        for part, weight in zip(parts, qkv_w)
    )
    grad_joined = norm_backward(grad_normed, unit, inverse, norm1_g)

    def total(value):
        return jnp.sum(value.astype(full), tuple(range(value.ndim - 1)))

    wide = [total(grad_hidden)]
    narrow = [
        total(grad_normed * unit),
        total(grad_normed),
        total(grad_attn),
        total(grad_normed_two * unit_two),
        total(grad_normed_two),
        total(grad_top),
    ]
    part_blocks = [by_block(part, 2) for part in parts]
    flat_blocks = by_block(attn_rows, 2)
    wide_blocks = by_block(wide[0], 0)
    q_sums = by_block(total(parts[0]), 0)
    v_sums = by_block(total(parts[2]), 0)
    narrow_all = jnp.stack([vector.reshape(groups, width) for vector in narrow], 1)

    def attn_grads(block):
        pieces = [
            jnp.einsum("fre,frd->ed", part[block], normed, preferred_element_type=full)
            for part in part_blocks
        ]
        pieces.append(
            jnp.einsum("fre,frd->ed", flat_blocks[block], grad_attn, preferred_element_type=full)
        )
        vectors = jnp.concatenate(
            [
                wide_blocks[block],
                q_sums[block],
                v_sums[block],
                lax.dynamic_index_in_dim(narrow_all, here ^ block, 0, False).reshape(-1),
            ]
        )
        count = vectors.shape[0]
        lines = -(-count // (16 * features)) * 16
        vectors = jnp.pad(vectors, (0, lines * features - count)).reshape(lines, features)
        return jnp.concatenate(pieces + [vectors], 0).astype(low)

    attn_total = collect([attn_grads(block) for block in range(groups)])
    attn_total = lax.psum(attn_total, "videos").astype(full)

    grad_carried = grad_joined[:, all_rows, :]
    grad_message = lax.all_gather(grad_carried, "heads", axis=0, tiled=True)
    grad_msg_low = grad_message.astype(low)
    msg_heads_grad = jnp.einsum("fd,ed->fe", grad_msg_low, msg_out_w, preferred_element_type=full)
    msg_gq, msg_gk, msg_gv = attend_backward(
        msg_query,
        msg_key,
        msg_value,
        frame_mask,
        msg_lse,
        split_heads((msg_heads_grad.astype(low)[None],))[0],
    )
    msg_stacked = jnp.stack([msg_gq, msg_gk, msg_gv]).reshape(3, slots, width)
    msg_norm_part = jnp.einsum("cfe,cde->fd", msg_stacked, msg_qkv_w, preferred_element_type=full)
    grad_msg_normed = jnp.sum(lax.all_gather(msg_norm_part, "heads"), 0)
    grad_fc = grad_message + norm_backward(grad_msg_normed, msg_unit, msg_inverse, msg_norm_g)
    grad_fc_cols = lax.dynamic_slice_in_dim(grad_fc, here * width, width, 1).astype(low)
    leading_part = jnp.einsum("fe,de->fd", grad_fc_cols, msg_fc_w, preferred_element_type=full)
    leading_grad = jnp.sum(lax.all_gather(leading_part, "heads"), 0)

    cut = lambda value: lax.dynamic_slice_in_dim(value, here * width, width, value.ndim - 1)
    operands = jnp.concatenate(
        [
            msg_in,
            msg_stacked[0],
            msg_stacked[1],
            msg_stacked[2],
            msg_flat,
            grad_msg_low,
            leading,
            grad_fc_cols,
        ],
        1,
    )
    operands = lax.all_gather(operands, "videos", axis=0, tiled=True)
    norm_sums = jnp.stack(
        [jnp.sum(cut(grad_msg_normed * msg_unit), 0), jnp.sum(cut(grad_msg_normed), 0)]
    )
    norm_sums = jnp.sum(lax.all_gather(norm_sums, "videos"), 0)
    marks = [0]
    for size in (features, width, width, width, width, features, features, width):
        marks.append(marks[-1] + size)
    all_in, all_q, all_k, all_v, all_flat, all_grad, all_lead, all_cols = [
        operands[:, begin:end] for begin, end in zip(marks[:-1], marks[1:])
    ]

    def outer(left, right):
        return jnp.einsum("rd,re->de", left, right, preferred_element_type=full)

    msg_qkv_w_grad = jnp.stack([outer(all_in, part) for part in (all_q, all_k, all_v)])
    msg_qkv_b_grad = jnp.stack([total(all_q), total(all_v)])
    msg_out_w_grad = outer(all_flat, all_grad)
    msg_out_b_grad = total(cut(all_grad))
    msg_fc_w_grad = outer(all_lead, all_cols)
    msg_fc_b_grad = total(all_cols)

    grad_frames = grad_mixed + grad_joined[:, :all_rows]
    frames_grad = return_frames(grad_frames.astype(low), here, groups, rows).astype(full)
    owner = (here == 0).astype(full)
    frames_grad = frames_grad.at[:, 0, :].add(leading_grad * owner)

    attn_w_total = attn_total[: 4 * width].reshape(4, width, features)
    sums = attn_total[4 * width :].reshape(-1)
    fc1_b_grad = sums[:hidden_width]
    sums = sums[hidden_width : hidden_width + 8 * width].reshape(8, width)
    return (
        mixed_out[None],
        frames_grad[None],
        msg_fc_w_grad,
        msg_fc_b_grad,
        norm_sums[0],
        norm_sums[1],
        msg_qkv_w_grad,
        msg_qkv_b_grad,
        msg_out_w_grad,
        msg_out_b_grad,
        sums[2],
        sums[3],
        attn_w_total[:3].transpose(0, 2, 1),
        sums[:2],
        attn_w_total[3],
        sums[4],
        sums[5],
        sums[6],
        fc_total[0],
        fc1_b_grad,
        fc_total[1],
        sums[7],
    )


def solution(mesh):
    placed = (
        P("videos", None, "heads", None),
        P("videos", None, "heads", None),
        P("videos"),
        P("videos"),
        P(None, "heads"),
        P("heads"),
        P(),
        P(),
        P(None, None, "heads"),
        P(None, "heads"),
        P("heads", None),
        P(),
        P(),
        P(),
        P(None, None, "heads"),
        P(None, "heads"),
        P("heads", None),
        P(),
        P(),
        P(),
        P(None, "heads"),
        P("heads"),
        P("heads", None),
        P(),
    )
    return jax.shard_map(
        on_device,
        mesh=mesh,
        in_specs=placed,
        out_specs=(
            P("videos", None, "heads", None),
            P("videos", None, "heads", None),
            P(None, "heads"),
            P("heads"),
            P("heads"),
            P("heads"),
            P(None, None, "heads"),
            P(None, "heads"),
            P("heads", None),
            P("heads"),
            P("heads"),
            P("heads"),
            P(None, None, "heads"),
            P(None, "heads"),
            P("heads", None),
            P("heads"),
            P("heads"),
            P("heads"),
            P(None, "heads"),
            P("heads"),
            P("heads", None),
            P("heads"),
        ),
        check_vma=False,
    )
```

```python
import jax
import jax.numpy as jnp
from jax import lax
from jax.experimental import pallas as pl
from jax.experimental.pallas import tpu as pltpu
from jax.sharding import PartitionSpec as P

HEAD_DIM = 64


epsilon = 1e-05

low = jnp.bfloat16
full = jnp.float32
VMEM_LIMIT = 48 * 1024 * 1024

RATE = 1e9


def norm_forward(value, gains, offset):
    average = jnp.mean(value, -1, keepdims=True)
    centered = value - average
    spread = jnp.mean(centered * centered, -1, keepdims=True)
    inverse = lax.rsqrt(spread + epsilon)
    unit = centered * inverse
    return (unit * gains.astype(jnp.float32) + offset.astype(jnp.float32), unit, inverse)


def norm_backward(gradient, unit, inverse, gains):
    scaled = gradient * gains.astype(jnp.float32)
    average = jnp.mean(scaled, -1, keepdims=True)
    second = jnp.mean(scaled * unit, -1, keepdims=True)
    return inverse * (scaled - average - unit * second)


def split_heads(tensors):
    return tuple(
        (
            tensor.reshape(tensor.shape[:-1] + (tensor.shape[-1] // HEAD_DIM, HEAD_DIM))
            for tensor in tensors
        )
    )


def project(normed, weight, biases):
    stacked = jnp.einsum("...d,cde->c...e", normed, weight, preferred_element_type=jnp.float32)
    return (
        (stacked[0] + biases[0]).astype(jnp.bfloat16),
        stacked[1].astype(jnp.bfloat16),
        (stacked[2] + biases[1]).astype(jnp.bfloat16),
    )


def attend_forward(queries, key_rows, values, keymask):
    scale_factor = HEAD_DIM ** (-0.5)
    scores = (
        jnp.einsum("bqhe,bkhe->bhqk", queries, key_rows, preferred_element_type=jnp.float32)
        * scale_factor
    )
    scores = jnp.where(keymask, scores, -1e30)
    largest = jnp.max(scores, -1, keepdims=True)
    exponent = jnp.exp(scores - largest)
    totals = jnp.sum(exponent, -1, keepdims=True)
    chances = exponent / totals
    output = jnp.einsum(
        "bhqk,bkhe->bqhe", chances.astype(jnp.bfloat16), values, preferred_element_type=jnp.float32
    )
    return (output.astype(jnp.bfloat16), largest + jnp.log(totals))


def attend_backward(queries, key_rows, values, keymask, log_total, grad_heads):
    scale_factor = HEAD_DIM ** (-0.5)
    scores = (
        jnp.einsum("bqhe,bkhe->bhqk", queries, key_rows, preferred_element_type=jnp.float32)
        * scale_factor
    )
    scores = jnp.where(keymask, scores, -1e30)
    chances = jnp.exp(scores - log_total)
    grad_chances = jnp.einsum(
        "bqhe,bkhe->bhqk", grad_heads, values, preferred_element_type=jnp.float32
    )
    deltas = jnp.sum(chances * grad_chances, -1, keepdims=True)
    grad_scores = (chances * (grad_chances - deltas)).astype(jnp.bfloat16)
    grad_query = (
        jnp.einsum("bhqk,bkhe->bqhe", grad_scores, key_rows, preferred_element_type=jnp.float32)
        * scale_factor
    ).astype(jnp.bfloat16)
    grad_key = (
        jnp.einsum("bhqk,bqhe->bkhe", grad_scores, queries, preferred_element_type=jnp.float32)
        * scale_factor
    ).astype(jnp.bfloat16)
    grad_value = jnp.einsum(
        "bhqk,bqhe->bkhe",
        chances.astype(jnp.bfloat16),
        grad_heads,
        preferred_element_type=jnp.float32,
    ).astype(jnp.bfloat16)
    return (grad_query, grad_key, grad_value)


def dot(left, right, left_dim=1, right_dim=0):
    return lax.dot_general(
        left, right, (((left_dim,), (right_dim,)), ((), ())), preferred_element_type=full
    )


def unit_of(value):
    centered = value - jnp.mean(value, -1, keepdims=True)
    inverse = lax.rsqrt(jnp.mean(centered * centered, -1, keepdims=True) + epsilon)
    return centered * inverse, inverse


def unit_backward(scaled, unit, inverse):
    average = jnp.mean(scaled, -1, keepdims=True)
    second = jnp.mean(scaled * unit, -1, keepdims=True)
    return inverse * (scaled - average - unit * second)


def row_sum(value):
    return jnp.sum(value, 0, keepdims=True)


def lane_mask(width, head):
    lane = lax.broadcasted_iota(jnp.int32, (1, width), 1)
    return (lane >= head * HEAD_DIM) & (lane < (head + 1) * HEAD_DIM)


def call_kernel(body, inputs, outputs, scratch, name, specs=None, micros=3):
    def kernel(*refs):
        queue = list(refs)
        body(lambda count: [queue.pop(0) for _ in range(count)])

    return list(
        pl.pallas_call(
            kernel,
            out_shape=[jax.ShapeDtypeStruct(*each) for each in outputs],
            scratch_shapes=scratch,
            **({} if specs is None else {"in_specs": specs}),
            compiler_params=pltpu.CompilerParams(vmem_limit_bytes=VMEM_LIMIT),
            cost_estimate=pl.CostEstimate(
                flops=int(micros * RATE), bytes_accessed=1024, transcendentals=0
            ),
            name=name,
        )(*inputs)
    )


def combine(*outputs):
    terms = [term for output in outputs for slot in output for term in slot]
    marks = jnp.stack([jnp.asarray(index, jnp.int32) for _, index in terms])
    _, rows, features = terms[0][0].shape
    chunk = rows // 2 if rows >= 192 else rows

    def kernel(_, *refs):
        queue = list(refs)
        sums = [
            [sum(queue.pop(0)[0].astype(full) for _ in slot) for slot in output]
            for output in outputs
        ]
        for out, values in zip(queue, sums):
            for k, value in enumerate(values):
                out[k] = value.astype(low)

    return pl.pallas_call(
        kernel,
        grid_spec=pltpu.PrefetchScalarGridSpec(
            num_scalar_prefetch=1,
            grid=(rows // chunk,),
            in_specs=[
                pl.BlockSpec((1, chunk, features), lambda c, s, k=k: (s[k], c, 0))
                for k in range(len(terms))
            ],
            out_specs=[
                pl.BlockSpec((len(output), chunk, features), lambda c, s: (0, c, 0))
                for output in outputs
            ],
        ),
        out_shape=[jax.ShapeDtypeStruct((len(each), rows, features), low) for each in outputs],
        compiler_params=pltpu.CompilerParams(vmem_limit_bytes=VMEM_LIMIT),
        name="combine",
    )(marks, *[array for array, _ in terms])


def spread(pieces, bit, pair_bit, split):
    _, rows, features = pieces[0].shape
    marks = jnp.stack([bit, pair_bit]).astype(jnp.int32)

    def body(take):
        (mark_ref,) = take(1)
        piece_refs = take(4)
        first_ref, second_ref = take(2)
        for k, piece in enumerate(piece_refs):
            outer, inner = mark_ref[0] ^ (k // 2), mark_ref[1] ^ (k % 2)
            begin = pl.multiple_of((outer * 2 + inner) * rows, 8)
            first_ref[pl.ds(begin, rows)] = piece[0].astype(full)
            if not split:
                second_ref[pl.ds(begin, rows)] = piece[1].astype(full)
            else:

                @pl.when(outer == 0)
                def _(piece=piece, begin=begin):
                    first_ref[pl.ds(4 * rows + begin, rows)] = piece[1].astype(full)

                @pl.when(outer == 1)
                def _(piece=piece, inner=inner):
                    at = pl.ds(pl.multiple_of(inner * rows, 8), rows)
                    second_ref[at] = piece[1].astype(full)

    sizes = (6, 2) if split else (4, 4)
    outputs = [((size * rows, features), full) for size in sizes]
    specs = [pl.BlockSpec(memory_space=pltpu.VMEM)] * 5
    specs[0] = pl.BlockSpec(memory_space=pltpu.SMEM)
    return call_kernel(body, [marks, *pieces], outputs, [], "spread", specs)


def prepare(bit, qkv, out, extra, fc1, fc2):
    width, features = out.shape
    units = fc2.shape[0]
    half = units // 2
    size = 4 * width + extra.shape[0]

    def body(take):
        bit_ref, qkv_ref, out_ref, extra_ref, fc1_ref, fc2_ref = take(6)
        pack_ref, half_ref, fcs_ref, send_ref = take(4)
        pack_ref[: 3 * width] = qkv_ref[...]
        pack_ref[3 * width : 4 * width] = out_ref[...]
        pack_ref[4 * width :] = extra_ref[...]
        for k in range(2):
            fcs_ref[2 * k] = fc1_ref[:, k * half : (k + 1) * half].T
            fcs_ref[2 * k + 1] = fc2_ref[k * half : (k + 1) * half]
        here = bit_ref[0]
        half_ref[...] = pack_ref[pl.ds(pl.multiple_of(here * (size // 2), 16), size // 2)]
        send_ref[...] = fcs_ref[pl.ds(2 * here, 2)]

    outputs = [((size, features), low), ((size // 2, features), low)]
    outputs += [((4, half, features), low), ((2, half, features), low)]
    specs = [pl.BlockSpec(memory_space=pltpu.VMEM)] * 6
    specs[0] = pl.BlockSpec(memory_space=pltpu.SMEM)
    inputs = [bit, qkv, out, extra, fc1, fc2]
    return call_kernel(body, inputs, outputs, [], "prepare", specs)


def message_forward(message, norm, qkv, out, bias, key_row):
    slots, features = message.shape
    width = out.shape[0]

    def body(take):
        message_ref, norm_ref, qkv_ref, out_ref, bias_ref, key_ref = take(6)
        normed_ref, saved_ref, part_ref = take(3)
        unit, _ = unit_of(message_ref[...])
        normed = (unit * norm_ref[0:1] + norm_ref[1:2]).astype(low)
        normed_ref[...] = normed.astype(full)
        query, key, value = [
            dot(normed, qkv_ref[k * width : (k + 1) * width], 1, 1) for k in range(3)
        ]
        query = (query + bias_ref[0:1]).astype(low)
        key = key.astype(low)
        value = (value + bias_ref[1:2]).astype(low)
        result = jnp.zeros((slots, width), full)
        for j in range(width // HEAD_DIM):
            mask = lane_mask(width, j)
            scaled = query.astype(full) * HEAD_DIM ** (-0.5)
            one = jnp.where(mask, scaled, jnp.zeros_like(scaled)).astype(low)
            scores = dot(one, key, 1, 1) + key_ref[...]
            exponent = jnp.exp(scores - jnp.max(scores, -1, keepdims=True))
            chances = exponent / jnp.sum(exponent, -1, keepdims=True)
            result = jnp.where(mask, dot(chances.astype(low), value), result)
        result = result.astype(low)
        for k, each in enumerate((query, key, value, result)):
            saved_ref[k] = each.astype(full)
        part_ref[...] = dot(result, out_ref[...])

    outputs = [((slots, features), full), ((4, slots, width), full), ((slots, features), full)]
    inputs = [message, norm, qkv, out, bias, key_row]
    return call_kernel(body, inputs, outputs, [], "message_forward")


def message_backward(grad_message, saved, qkv, out, key_row):
    slots, features = grad_message.shape
    width = out.shape[0]

    def body(take):
        grad_ref, saved_ref, qkv_ref, out_ref, key_ref = take(5)
        stacked_ref, part_ref = take(2)
        grad_o = dot(grad_ref[...].astype(low), out_ref[...], 1, 1).astype(low).astype(full)
        scaled = saved_ref[0] * HEAD_DIM ** (-0.5)
        key, value = saved_ref[1].astype(low), saved_ref[2].astype(low)
        grad_q = grad_k = grad_v = jnp.zeros((slots, width), full)
        for j in range(width // HEAD_DIM):
            mask = lane_mask(width, j)
            one_query = jnp.where(mask, scaled, jnp.zeros_like(scaled)).astype(low)
            one_grad = jnp.where(mask, grad_o, jnp.zeros_like(grad_o)).astype(low)
            scores = dot(one_query, key, 1, 1) + key_ref[...]
            exponent = jnp.exp(scores - jnp.max(scores, -1, keepdims=True))
            chances = exponent / jnp.sum(exponent, -1, keepdims=True)
            grad_p = dot(one_grad, value, 1, 1)
            grad_s = chances * (grad_p - jnp.sum(chances * grad_p, -1, keepdims=True))
            grad_s = grad_s.astype(low)
            grad_v += dot(chances.astype(low), one_grad, 0, 0)
            grad_k += dot(grad_s, one_query, 0, 0)
            grad_q = jnp.where(mask, dot(grad_s, key), grad_q)
        grads = [each.astype(low) for each in (grad_q * HEAD_DIM ** (-0.5), grad_k, grad_v)]
        for k, each in enumerate(grads):
            stacked_ref[k] = each.astype(full)
        part_ref[...] = sum(
            dot(each, qkv_ref[k * width : (k + 1) * width]) for k, each in enumerate(grads)
        )

    outputs = [((3, slots, width), full), ((slots, features), full)]
    return call_kernel(
        body, [grad_message, saved, qkv, out, key_row], outputs, [], "message_backward"
    )


def message_weights(operands, features, width, field, count):
    rows, total = operands.shape
    slots = rows // count
    starts = [k * features for k in range(3)] + [3 * features + k * field for k in range(5)]
    last = 3 * features + 5 * field

    def body(take):
        (rows_ref,) = take(1)
        qkv_ref, out_ref, fc_ref, heads_ref, grad_ref, cols_ref, own_ref = take(7)
        wide = [rows_ref[:, at : at + features] for at in starts[:3]]
        thin = [rows_ref[:, at : at + width] for at in starts[3:]]
        for k in range(3):
            qkv_ref[k * width : (k + 1) * width] = dot(thin[k], wide[0], 0, 0)
        out_ref[...] = dot(thin[3], wide[1], 0, 0)
        fc_ref[...] = dot(thin[4], wide[2], 0, 0)
        heads_ref[...] = jnp.concatenate(
            [row_sum(thin[0].astype(full)), row_sum(thin[2].astype(full))], 0
        )
        grad_ref[...] = row_sum(wide[1].astype(full))
        cols_ref[...] = row_sum(thin[4].astype(full))
        own = rows_ref[:, last:].astype(full)
        own_ref[...] = sum(own[k * slots : (k + 1) * slots] for k in range(count))

    outputs = [
        ((3 * width, features), full),
        ((width, features), full),
        ((width, features), full),
        ((2, width), full),
        ((1, features), full),
        ((1, width), full),
        ((slots, total - last), full),
    ]
    return call_kernel(body, [operands], outputs, [], "message_weights")


def attn_forward(rows_in, total, norm, carried, bit, key_row, packs, mine, all_rows):
    first = total is None
    rows, features = rows_in.shape
    span = rows // mine
    width = features // 4
    count = len(packs)
    edge = all_rows // 16 * 16

    def body(take):
        if first:
            rows_ref, norm_ref, carried_ref = take(3)
        else:
            rows_ref, total_in, bit_ref = take(3)
        (key_ref,) = take(1)
        if first:
            pack_refs = take(count)
            normed_ref, joined_ref = take(2)
        else:
            own_refs, other_refs = take(count), take(count)
            pack_refs = take(count)
            normed_ref = rows_ref
        (total_ref,) = take(1)
        saved_refs = take(count)
        q_refs, k_refs, v_refs, o_refs = [[each.at[k] for each in saved_refs] for k in range(4)]
        if first:
            joined_ref[...] = rows_ref[...]
            place = lax.broadcasted_iota(jnp.int32, (span - edge, 1), 0)
            for f in range(mine):
                at = slice(f * span + edge, (f + 1) * span)
                joined_ref[at] = jnp.where(
                    place == all_rows - edge,
                    carried_ref[f : f + 1],
                    rows_ref[at].astype(full),
                ).astype(low)
            unit, _ = unit_of(joined_ref[...].astype(full))
            normed_ref[...] = (unit * norm_ref[0:1] + norm_ref[1:2]).astype(low)
        else:
            half = own_refs[0].shape[0]
            here = bit_ref[0]
            for own, other, pack in zip(own_refs, other_refs, pack_refs):
                pack[pl.ds(pl.multiple_of(here * half, 16), half)] = own[...]
                pack[pl.ds(pl.multiple_of((1 - here) * half, 16), half)] = other[...]
        normed = normed_ref[...]
        key_bias = key_ref[...]
        for b in range(count):
            pack = pack_refs[b]
            extra = pack[4 * width : 4 * width + 16].astype(full)
            q_refs[b][...] = (dot(normed, pack[:width], 1, 1) + extra[0:1, :width]).astype(low)
            k_refs[b][...] = dot(normed, pack[width : 2 * width], 1, 1).astype(low)
            v_refs[b][...] = (
                dot(normed, pack[2 * width : 3 * width], 1, 1) + extra[1:2, :width]
            ).astype(low)
            for f in range(mine):
                at = slice(f * span, (f + 1) * span)
                query = q_refs[b][at] * jnp.asarray(HEAD_DIM ** (-0.5), low)
                key, value = k_refs[b][at], v_refs[b][at]
                out = jnp.zeros((span, width), full)
                for j in range(width // HEAD_DIM):
                    mask = lane_mask(width, j)
                    scores = dot(jnp.where(mask, query, jnp.zeros_like(query)), key, 1, 1)
                    scores = scores + key_bias
                    exponent = jnp.exp(scores - jnp.max(scores, -1, keepdims=True))
                    share = 1.0 / jnp.sum(exponent, -1, keepdims=True)
                    out = jnp.where(mask, dot(exponent.astype(low), value) * share, out)
                o_refs[b][at] = out.astype(low)
            part = dot(o_refs[b][...], pack[3 * width : 4 * width])
            if b:
                total_ref[...] += part
            else:
                total_ref[...] = part if first else total_in[...] + part

    small = ((rows, features), low)
    if first:
        inputs = [rows_in, norm, carried, key_row, *packs]
        outputs = [small, small]
        specs = None
    else:
        inputs = [rows_in, total, bit, key_row]
        inputs += [own for own, _ in packs] + [other for _, other in packs]
        outputs = [((2 * own.shape[0], features), low) for own, _ in packs]
        specs = [pl.BlockSpec(memory_space=pltpu.VMEM)] * len(inputs)
        specs[2] = pl.BlockSpec(memory_space=pltpu.SMEM)
    lead = len(outputs) + 1
    outputs += [((rows, features), full)] + [((4, rows, width), low)] * count
    results = call_kernel(body, inputs, outputs, [], "attn_forward", specs, 9)
    return results[: lead - 1], results[lead - 1], results[lead:]


def mlp_step(start, carry, grad, consts, weights, biases, last):
    first = carry is None
    rows, features = grad.shape
    count = len(weights)
    lengths = [[each.shape[0] for each in group] for group in weights]

    def body(take):
        joined_ref, total_ref, const_ref = take(3)
        if not first:
            normed_ref, y_in, d_in = take(3)
        (grad_ref,) = take(1)
        fc_refs = [
            [ref.at[k] for size in group for ref in take(1) for k in range(size)]
            for group in lengths
        ]
        bias_refs = take(count)
        if last:
            out_ref, mixed_ref, attn_ref, sums_ref = take(4)
        else:
            y_ref, d_ref = take(2)
        if first:
            (normed_ref,) = take(1)
        w_refs, b_refs = take(count), take(count)
        if last:
            y_ref, d_ref = take(2)

        def mixed():
            return joined_ref[...].astype(full) + total_ref[...] + const_ref[0:1]

        if first:
            unit, _ = unit_of(mixed())
            normed_ref[...] = (unit * const_ref[1:2] + const_ref[2:3]).astype(low)
        normed = normed_ref[...]
        grad = grad_ref[...]
        fresh = True
        for b in range(count):
            for c in range(len(fc_refs[b]) // 2):
                fc1, fc2 = fc_refs[b][2 * c][...], fc_refs[b][2 * c + 1][...]
                pre = dot(normed, fc1, 1, 1) + bias_refs[b][c : c + 1]
                gate = jax.nn.sigmoid(1.702 * pre)
                active = (pre * gate).astype(low)
                back = dot(grad, fc2, 1, 1) * (gate + 1.702 * pre * gate * (1.0 - gate))
                back = back.astype(low)
                b_refs[b][c : c + 1] = row_sum(back.astype(full))
                y_part = dot(active, fc2)
                d_part = dot(back, fc1)
                if not fresh:
                    y_ref[...] += y_part
                    d_ref[...] += d_part
                else:
                    y_ref[...] = y_part if first else y_in[...] + y_part
                    d_ref[...] = d_part if first else d_in[...] + d_part
                fresh = False
                w_refs[b][2 * c] = dot(back, normed, 0, 0).astype(low)
                w_refs[b][2 * c + 1] = dot(active, grad, 0, 0).astype(low)
        if last:
            value = mixed()
            unit, inverse = unit_of(value)
            out_ref[...] = (value + y_ref[...] + const_ref[3:4]).astype(low)
            grad_normed = d_ref[...]
            top = grad.astype(full)
            grad_mixed = top + unit_backward(grad_normed * const_ref[1:2], unit, inverse)
            mixed_ref[...] = grad_mixed
            grad_attn = grad_mixed.astype(low)
            attn_ref[...] = grad_attn
            sums_ref[...] = jnp.concatenate(
                [
                    row_sum(grad_attn.astype(full)),
                    row_sum(grad_normed * unit),
                    row_sum(grad_normed),
                    row_sum(top),
                ],
                0,
            )

    big = ((rows, features), full)
    small = ((rows, features), low)
    inputs = [*start, consts] + ([] if first else list(carry)) + [grad]
    inputs += [each for group in weights for each in group] + list(biases)
    outputs = [small, big, small, ((4, features), full)] if last else [big, big]
    outputs += [small] if first else []
    lead = len(outputs)
    outputs += [((sum(size), *group[0].shape[1:]), low) for size, group in zip(lengths, weights)]
    outputs += [(each.shape, full) for each in biases]
    scratch = [pltpu.VMEM((rows, features), full)] * 2 if last else []
    results = call_kernel(body, inputs, outputs, scratch, "mlp_step", None, 12)
    return results[:lead], results[lead : lead + count], results[lead + count :]


def attn_backward(normed, grad, key_column, total, packs, saved, mine, all_rows, ending):
    rows, features = normed.shape
    span = rows // mine
    width = features // 4
    count = len(packs)
    first = total is None
    last = ending is not None

    def body(take):
        normed_ref, grad_ref, key_ref = take(3)
        if not first:
            (total_in,) = take(1)
        if last:
            joined_ref, mixed_ref, norm_ref = take(3)
        pack_refs = take(count)
        saved_refs = take(count)
        q_refs, k_refs, v_refs, o_refs = [[each.at[k] for each in saved_refs] for k in range(4)]
        if last:
            rows_ref, carried_ref, sums_ref = take(3)
        else:
            (total_ref,) = take(1)
        w_refs, b_refs = take(count), take(count)
        dq_ref, dk_ref, dv_ref, do_ref = take(4)
        if last:
            (total_ref,) = take(1)
        normed = normed_ref[...]
        grad = grad_ref[...]
        key_bias = key_ref[...]
        scale = HEAD_DIM ** (-0.5)
        for b in range(count):
            pack = pack_refs[b]
            do_ref[...] = dot(grad, pack[3 * width : 4 * width], 1, 1).astype(low)
            for f in range(mine):
                at = slice(f * span, (f + 1) * span)
                query = q_refs[b][at] * jnp.asarray(scale, low)
                key, value, grad_o = k_refs[b][at], v_refs[b][at], do_ref[at]
                grad_q = grad_k = grad_v = jnp.zeros((span, width), full)
                for j in range(width // HEAD_DIM):
                    mask = lane_mask(width, j)
                    one_query = jnp.where(mask, query, jnp.zeros_like(query))
                    one_grad = jnp.where(mask, grad_o, jnp.zeros_like(grad_o))
                    scores = dot(key, one_query, 1, 1) + key_bias
                    exponent = jnp.exp(scores - jnp.max(scores, 0, keepdims=True))
                    chances = exponent * (1.0 / row_sum(exponent))
                    grad_p = dot(value, one_grad, 1, 1)
                    grad_s = (chances * (grad_p - row_sum(chances * grad_p))).astype(low)
                    grad_v += dot(chances.astype(low), one_grad)
                    grad_k += dot(grad_s, one_query)
                    grad_q = jnp.where(mask, dot(grad_s, key, 0, 0), grad_q)
                dq_ref[at] = (grad_q * scale).astype(low)
                dk_ref[at] = grad_k.astype(low)
                dv_ref[at] = grad_v.astype(low)
            grads = (dq_ref[...], dk_ref[...], dv_ref[...])
            part = sum(dot(each, pack[k * width : (k + 1) * width]) for k, each in enumerate(grads))
            if b:
                total_ref[...] += part
            else:
                total_ref[...] = part if first else total_in[...] + part
            for k, each in enumerate(grads):
                w_refs[b][k] = dot(each, normed, 0, 0).astype(low)
            w_refs[b][3] = dot(o_refs[b][...], grad, 0, 0).astype(low)
            b_refs[b][...] = jnp.concatenate(
                [row_sum(grads[0].astype(full)), row_sum(grads[2].astype(full))], 0
            )
        if last:
            unit, inverse = unit_of(joined_ref[...].astype(full))
            grad_normed = total_ref[...]
            grad_joined = unit_backward(grad_normed * norm_ref[0:1], unit, inverse)
            rows_ref[...] = (mixed_ref[...] + grad_joined).astype(low)
            carried_ref[...] = jnp.concatenate(
                [grad_joined[f * span + all_rows : f * span + all_rows + 1] for f in range(mine)],
                0,
            )
            sums_ref[...] = jnp.concatenate(
                [row_sum(grad_normed * unit), row_sum(grad_normed)], 0
            )

    inputs = [normed, grad, key_column] + ([] if first else [total]) + list(ending or ())
    inputs += [*packs, *saved]
    if last:
        outputs = [((rows, features), low), ((mine, features), full), ((2, features), full)]
    else:
        outputs = [((rows, features), full)]
    lead = len(outputs)
    outputs += [((4, width, features), low)] * count + [((2, width), full)] * count
    scratch = [pltpu.VMEM((rows, width), low)] * 4
    scratch += [pltpu.VMEM((rows, features), full)] if last else []
    results = call_kernel(body, inputs, outputs, scratch, "attn_backward", None, 9)
    grads = [(results[lead + b], results[lead + count + b]) for b in range(count)]
    return results[:lead], grads


def swap(value, axis, offset):
    size = lax.axis_size(axis)
    return lax.ppermute(value, axis, [(place, place ^ offset) for place in range(size)])


def pick(value, index, count, dimension=0):
    return lax.dynamic_slice_in_dim(value, index * count, count, dimension)


def add(*values):
    return sum(value.astype(full) for value in values).astype(low)


def hold(*values):
    return lax.optimization_barrier(values)


def after(value, *others):
    return lax.optimization_barrier((value, *others))[0]


def everyone(value):
    size = lax.axis_size("heads")
    return [value] + [swap(value, "heads", k) for k in range(1, size)]


def by_place(pieces, here):
    stacked = jnp.stack(pieces)
    return [lax.dynamic_index_in_dim(stacked, here ^ k, 0, False) for k in range(len(pieces))]


def frame_pieces(frames, here, groups):
    mine = frames.shape[0] // groups
    return [pick(frames, here ^ k, mine) for k in range(groups)]


def send_each(pieces):
    return [swap(piece, "heads", k) if k else piece for k, piece in enumerate(pieces)]


def far_frames(frames, here):
    return pick(frames, (here // 2) ^ 1, frames.shape[0] // 2)


def near_frames(frames, came, here):
    mine = came.shape[0] // 2
    return jnp.concatenate([pick(frames, here ^ 1, mine), pick(came, 1 - here % 2, mine)], 0)


def own_frames(frames, came, near, here):
    mine = came.shape[0] // 2
    return [pick(frames, here, mine), near[:mine], pick(came, here % 2, mine), near[mine:]]


def on_device(
    frames,
    out_grad,
    frame_tokens,
    frame_count,
    msg_fc_w,
    msg_fc_b,
    msg_norm_g,
    msg_norm_b,
    msg_qkv_w,
    msg_qkv_b,
    msg_out_w,
    msg_out_b,
    norm1_g,
    norm1_b,
    attn_qkv_w,
    attn_qkv_b,
    attn_out_w,
    attn_out_b,
    norm2_g,
    norm2_b,
    fc1_w,
    fc1_b,
    fc2_w,
    fc2_b,
):
    _, slots, rows, features = frames.shape
    groups = lax.axis_size("heads")
    videos = lax.axis_size("videos")
    here = lax.axis_index("heads")
    video = lax.axis_index("videos")
    bit = video % 2
    far = groups // 2
    mine = slots // groups
    all_rows = rows * groups
    span = -(-(all_rows + 1) // 16) * 16
    tail = span - all_rows
    width = msg_fc_w.shape[1]
    units = fc1_w.shape[1]
    half = units // 2
    quick = videos == 8
    frames = frames[0]
    out_grad = out_grad[0]
    mark = bit[None].astype(jnp.int32)
    stack = lambda *vectors: jnp.stack(vectors).astype(full)
    flat = lambda pieces: jnp.concatenate(pieces, 1).reshape(mine * span, features)
    unflat = lambda value: value.reshape(mine, span, features)[:, :all_rows]
    pair_bit = (video // 2) % 2
    blank = jnp.zeros((mine, tail, features), low)

    link = lambda value: swap(value, "heads", far)
    side = lambda value: swap(value, "heads", 1)
    pair = lambda value: swap(value, "videos", 1)

    lead = frames[:, 0, :]
    leads = everyone(lead)
    wide = lambda value: jnp.pad(value, ((0, 0), (0, features - value.shape[1])))
    extra = jnp.concatenate(
        [wide(attn_qkv_b), wide(fc1_b[None]), jnp.zeros((29, features), low)], 0
    )
    pack, pack_send, fcs, fc_send = prepare(
        mark,
        after(attn_qkv_w, lead).transpose(0, 2, 1).reshape(3 * width, features),
        attn_out_w,
        extra,
        fc1_w,
        fc2_w,
    )
    leads = hold(*leads, pack)[:groups]
    leading = lax.dynamic_index_in_dim(jnp.stack(leads), here, 0, False)
    fc_part = jnp.dot(leading, msg_fc_w, preferred_element_type=full) + msg_fc_b
    columns = everyone(fc_part)
    frames = after(frames, fc_part)
    row_send = far_frames(frames, here)
    row_came = link(row_send)
    columns = hold(*columns, row_send)[:groups]
    message = jnp.concatenate(by_place(columns, here), 1)
    msg_norm = stack(msg_norm_g, msg_norm_b)
    msg_key = jnp.where(jnp.arange(slots) < frame_count[0], 0.0, -1e30).astype(full)[None]
    msg_qkv = msg_qkv_w.transpose(0, 2, 1).reshape(3 * width, features)
    msg_in, msg_saved, msg_part = message_forward(
        message, msg_norm, msg_qkv, msg_out_w, msg_qkv_b.astype(full), msg_key
    )
    msg_pieces = frame_pieces(msg_part, here, groups)
    msg_rows = send_each(msg_pieces)
    pack_send, *_ = hold(pack_send, *msg_pieces)
    pack_own = link(pack_send)
    row_came, pack = hold(row_came, pack, pack_send)[:2]
    row_next = near_frames(frames, row_came, here)
    row_near = side(row_next)
    pack_near = side(after(pack, row_next))
    grad_send = far_frames(after(out_grad, row_next), here)
    base = flat(own_frames(frames, row_came, after(row_near, grad_send), here) + [blank])
    msg_rows = hold(*msg_rows, base)[:groups]
    carried = pick(message + msg_out_b, here, mine) + sum(msg_rows)

    places = jnp.concatenate([(here ^ k) * rows + jnp.arange(rows) for k in range(groups)])
    seen = jnp.concatenate([places < frame_tokens[0], jnp.arange(tail) == 0])
    key_bias = jnp.where(seen, 0.0, -1e30).astype(full)
    norm = stack(norm1_g, norm1_b)
    base, carried, pack_near, pack_own, grad_send, fc_send = hold(
        base, carried, pack_near, pack_own, grad_send, fc_send
    )
    pack_other, pack_own_3 = pair(pack_own), side(pack_own)
    grad_came = link(grad_send)
    (normed, joined), total, saved = attn_forward(
        base, None, norm, carried, None, key_bias[None], [pack, pack_near], mine, all_rows
    )
    pack_other, total, grad_came, pack_own_3, fc_send, fcs = hold(
        pack_other, total, grad_came, pack_own_3, fc_send, fcs
    )
    fc_own_1 = link(fc_send[:1])
    pack_other_3 = side(pack_other)
    grad_next = near_frames(out_grad, grad_came, here)
    grad_near = side(grad_next)
    fc_near = side(after(fcs, grad_next))
    total, pack_other_3, _ = hold(total, pack_other_3, grad_next)
    far_packs, total, rest = attn_forward(
        normed,
        total,
        None,
        None,
        mark,
        key_bias[None],
        [(pack_own, pack_other), (pack_own_3, pack_other_3)],
        mine,
        all_rows,
    )
    saved += rest
    packs = [pack, pack_near, *far_packs]
    total, grad_near, fc_own_1, fc_send = hold(total, grad_near, fc_own_1, fc_send)
    fc_own_2, fc_other_1, fc_own_31 = link(fc_send[1:]), pair(fc_own_1), side(fc_own_1)
    grad_top = flat(own_frames(out_grad, grad_came, grad_near, here) + [blank])

    consts = stack(attn_out_b, norm2_g, norm2_b, fc2_b)
    bias = [each[4 * width + 2].reshape(2, half).astype(full) for each in packs]
    order = lambda value: jnp.concatenate([pick(value, bit, 1), pick(value, 1 - bit, 1)], 0)
    bias = bias[:2] + [order(each) for each in bias[2:]]
    parts = [[each[:1] for each in bias[:1:-1]], [each[1:] for each in bias[:1:-1]]]
    start = (joined, total)
    (y_sum, d_sum, normed_two), (w_0,), (b_0,) = mlp_step(
        start, None, grad_top, consts, [[fcs]], bias[:1], False
    )
    y_sum, fc_own_2, fc_other_1, fc_own_31, fc_near = hold(
        y_sum, fc_own_2, fc_other_1, fc_own_31, fc_near
    )
    fc_other_2, fc_own_32, fc_other_31 = pair(fc_own_2), side(fc_own_2), side(fc_other_1)
    carry = (normed_two, y_sum, d_sum)
    (y_sum, d_sum), (w_1,), (b_1,) = mlp_step(
        start, carry, grad_top, consts, [[fc_near]], bias[1:2], False
    )
    y_sum, fc_other_2, fc_own_32, fc_other_31, w_1 = hold(
        y_sum, fc_other_2, fc_own_32, fc_other_31, w_1
    )
    fc_other_32, w_1 = side(fc_other_2), side(w_1)
    carry = (normed_two, y_sum, d_sum)
    units_own = [[fc_own_31, fc_own_32], [fc_own_1, fc_own_2]]
    (y_sum, d_sum), (w_3a, w_2a), (b_3a, b_2a) = mlp_step(
        start, carry, grad_top, consts, units_own, parts[0], False
    )
    y_sum, fc_other_32, w_1, w_3a = hold(y_sum, fc_other_32, w_1, w_3a)
    w_3a = side(w_3a)

    near = lambda k, weight: [(w_0, 2 * k + weight), (w_1, 2 * k + weight)]
    if quick:
        (send_2a,) = combine([near(1 - bit, 1)])
        came_2a = pair(send_2a)
        y_sum, _ = hold(y_sum, send_2a)
    carry = (normed_two, y_sum, d_sum)
    units_other = [[fc_other_31, fc_other_32], [fc_other_1, fc_other_2]]
    ends, (w_3b, w_2b), (b_3b, b_2b) = mlp_step(
        start, carry, grad_top, consts, units_other, parts[1], True
    )
    out_rows, grad_mixed, grad_attn, two_sums = ends
    column = key_bias[:, None]
    ending = (joined, grad_mixed, norm)

    def back(block, grad, total, last):
        results, ((weights, sums),) = attn_backward(
            normed,
            grad,
            column,
            total,
            [packs[block]],
            [saved[block]],
            mine,
            all_rows,
            ending if last else None,
        )
        return results, weights, sums

    grad_attn, w_3a, w_3b, out_rows = hold(grad_attn, w_3a, w_3b, out_rows)
    w_3b = side(w_3b)
    if quick:
        (send_1a,) = combine([[(w_2a, 0), (w_3a, 0)]])
        came_1a = link(send_1a)
        grad_attn, came_2a, _ = hold(grad_attn, came_2a, send_1a)
    (d_total,), g_1, s_1 = back(1, grad_attn, None, False)
    d_total, w_3b, w_2b, g_1 = hold(d_total, w_3b, w_2b, g_1)
    g_1 = side(g_1)
    if quick:
        send_1b, send_2b = combine([[(w_2b, 0), (w_3b, 0)]], [[(w_2b, 1), (w_3b, 1)]])
        came_1b, came_2b = link(send_1b), pair(send_2b)
        d_total, came_1a, _, _ = hold(d_total, came_1a, send_1b, send_2b)
    (d_total,), g_3, s_3 = back(3, grad_attn, d_total, False)
    d_total, g_3, g_1 = hold(d_total, g_3, g_1)
    g_3 = side(g_3)
    quarters = lambda value: value.reshape(2 * value.shape[0], -1, features)
    at = lambda terms, k: [(array, index + k) for array, index in terms]
    if quick:
        d_total, came_1b, came_2b = hold(d_total, came_1b, came_2b)
        send_1c, send_2c, keep = combine(
            [near(1 - bit, 0) + [(came_1b, 0)]],
            [[(w_2a, 1), (w_3a, 1), (came_2b, 0)]],
            [near(bit, 0) + [(came_1a, 0)], near(bit, 1) + [(came_2a, 0)]],
        )
        came_1c, came_2c = pair(send_1c), link(send_2c)
        d_total, _, _, _ = hold(d_total, send_1c, send_2c, keep)
    (d_total,), g_2, s_2 = back(2, grad_attn, d_total, False)
    if quick:
        d_total, came_1c, came_2c, g_3, g_2 = hold(d_total, came_1c, came_2c, g_3, g_2)
        fc_parts = [[(quarters(keep), 2 * k), (quarters(came), 0)] for k, came in enumerate((came_1c, came_2c))]
        fc_send, far_send, fc_keep = combine(
            [at(part, 1 - pair_bit) for part in fc_parts],
            [[(g_2, 0), (g_3, 0)], [(g_2, 1), (g_3, 1)]],
            [at(part, pair_bit) for part in fc_parts],
        )
        fc_came, far_came = swap(fc_send, "videos", 2), link(far_send)
        d_total, _, _, _ = hold(d_total, fc_send, far_send, fc_keep)
    (grad_rows, grad_carried, one_sums), g_0, s_0 = back(0, grad_attn, d_total, True)

    if quick:
        g_0, fc_came, grad_carried, far_came = hold(g_0, fc_came, grad_carried, far_came)
        fc_quarter, send_b = combine(
            [[(fc_keep, 0), (fc_came, 0)], [(fc_keep, 1), (fc_came, 1)]],
            [[(g_0, 3 - bit), (g_1, 3 - bit)], [(g_2, 3 - bit), (g_3, 3 - bit)]],
        )
        fc_came, came_b = swap(fc_quarter, "videos", 4), pair(send_b)
        grad_carried, _, _ = hold(grad_carried, fc_quarter, send_b)
    grad_message = lax.all_gather(grad_carried, "heads", axis=0, tiled=True)
    msg_stacked, msg_norm_part = message_backward(
        grad_message, msg_saved, msg_qkv, msg_out_w, msg_key
    )
    sums = jnp.concatenate([one_sums, two_sums], 0).reshape(6, groups, width)
    whole = lambda own, other: order(jnp.concatenate([own, other], 0)).reshape(1, -1)
    hidden_sums = [b_0.reshape(1, -1), b_1.reshape(1, -1), whole(b_2a, b_2b), whole(b_3a, b_3b)]
    hidden_sums = by_place(hidden_sums, here)
    head_sums = by_place([each.reshape(1, -1) for each in (s_0, s_1, s_2, s_3)], here)
    vectors = jnp.concatenate(
        [
            sums.transpose(1, 0, 2).reshape(groups, -1),
            jnp.concatenate(hidden_sums, 0),
            jnp.concatenate(head_sums, 0),
        ],
        1,
    ).reshape(-1, features)
    bundle = jnp.concatenate([msg_norm_part, vectors], 0)
    bundle = jnp.sum(lax.all_gather(bundle, "heads"), 0)
    grad_rows = unflat(grad_rows)
    out_rows = unflat(out_rows)
    by_rows = lambda value: [value[:, k * rows : (k + 1) * rows] for k in range(groups)]
    if quick:
        came_b, bundle = hold(came_b, bundle)
        send_a, send_bc, attn_keep = combine(
            [[(g_0, 1 - bit), (g_1, 1 - bit), (far_came, 1 - bit)]],
            [[(g_2, 2 + bit), (g_3, 2 + bit), (came_b, 1)]],
            [
                [(g_0, bit), (g_1, bit), (far_came, bit)],
                [(g_0, 2 + bit), (g_1, 2 + bit), (came_b, 0)],
            ],
        )
        came_a, came_bc = pair(send_a), link(send_bc)
        bundle, grad_rows, out_rows = hold(bundle, grad_rows, out_rows, send_a, send_bc)[:3]
    grad_msg_normed = bundle[:slots]
    vectors = bundle[slots:].reshape(groups, -1)
    vectors = lax.dynamic_index_in_dim(vectors, here, 0, False)
    msg_unit, msg_inverse = unit_of(message)
    grad_fc = grad_message + norm_backward(grad_msg_normed, msg_unit, msg_inverse, msg_norm_g)
    cut = lambda value: lax.dynamic_slice_in_dim(value, here * width, width, value.ndim - 1)
    grad_fc_cols = cut(grad_fc).astype(low)

    field = -(-width // 128) * 128
    thin = lambda value: jnp.pad(value.astype(low), ((0, 0), (0, field - width)))
    own = jnp.concatenate(
        [
            vectors,
            jnp.sum(cut(grad_msg_normed * msg_unit), 0),
            jnp.sum(cut(grad_msg_normed), 0),
        ]
    )
    count = own.shape[0]
    own = jnp.pad(own, (0, -count % (slots * 128))).reshape(slots, -1).astype(low)
    operands = [msg_in.astype(low), grad_message.astype(low), leading]
    operands += [thin(each) for each in (*msg_stacked, msg_saved[3], grad_fc_cols)]
    operands = jnp.concatenate(operands + [own], 1)[None]
    row_parts = by_rows(grad_rows)
    out_parts = by_rows(out_rows)
    far_rows = jnp.stack(row_parts[2:] + out_parts[2:])
    if quick:
        came = pair(operands)
        far_rows = after(far_rows, operands)
    rows_came = link(far_rows)
    leading_part = jnp.einsum("fe,de->fd", grad_fc_cols, msg_fc_w, preferred_element_type=full)
    if quick:
        came_a, came_bc, came, leading_part, _ = hold(came_a, came_bc, came, leading_part, far_rows)
        operands = jnp.concatenate([operands, came], 0)
        came = swap(operands, "videos", 2)
        attn_parts = [[(quarters(attn_keep), 2 * k), (quarters(each), 0)] for k, each in enumerate((came_a, came_bc))]
        attn_send, attn_keep = combine(
            [at(part, 1 - pair_bit) for part in attn_parts],
            [at(part, pair_bit) for part in attn_parts],
        )
        attn_came = swap(attn_send, "videos", 2)
        fc_quarter, fc_came = hold(fc_quarter, fc_came, attn_send, operands)[:2]
        (fc_quarter,) = combine(
            [[(fc_quarter, 0), (fc_came, 0)], [(fc_quarter, 1), (fc_came, 1)]]
        )
        fc_second, fc_third = swap(fc_quarter, "videos", 2), pair(fc_quarter)
        came, attn_came = hold(came, attn_came, fc_quarter)[:2]
        operands = jnp.concatenate([operands, came], 0)
        came = swap(operands, "videos", 4)
        (attn_quarter,) = combine(
            [[(attn_keep, 0), (attn_came, 0)], [(attn_keep, 1), (attn_came, 1)]]
        )
        attn_came = swap(attn_quarter, "videos", 4)
        came, rows_came, leading_part = hold(came, rows_came, leading_part, attn_quarter)[:3]
        operands = jnp.concatenate([operands, came], 0)
    else:
        operands = lax.all_gather(operands, "videos", axis=0, tiled=True)
    near_rows = jnp.stack([row_parts[1], rows_came[1], out_parts[1], rows_came[3]])
    rows_near = side(near_rows)
    leading_grad = jnp.sum(lax.all_gather(after(leading_part, near_rows), "heads"), 0)
    weights = message_weights(
        after(operands, leading_grad).reshape(-1, operands.shape[2]), features, width, field, videos
    )
    qkv_msg, msg_out_w_grad, fc_msg, msg_qkv_b_grad, all_grad, all_cols, own = weights
    own = own.reshape(-1)[:count]

    if quick:
        fc_second, fc_third, attn_came, own = hold(fc_second, fc_third, attn_came, own)
        fc_fourth = pair(fc_second)
        (attn_quarter,) = combine(
            [[(attn_quarter, 0), (attn_came, 0)], [(attn_quarter, 1), (attn_came, 1)]]
        )
        attn_second, attn_third = swap(attn_quarter, "videos", 2), pair(attn_quarter)
        rows_near = after(rows_near, attn_quarter)
    arrange = lambda pieces: jnp.concatenate(by_place(pieces, here), 0)
    mixed_out = arrange([out_parts[0], rows_near[2], rows_came[2], rows_near[3]])
    frames_grad = arrange([row_parts[0], rows_near[0], rows_came[0], rows_near[1]]).astype(full)
    owner = (here == 0).astype(full)
    frames_grad = frames_grad.at[:, 0, :].add(leading_grad * owner)
    if quick:
        attn_second, attn_third, fc_fourth, frames_grad = hold(
            attn_second, attn_third, fc_fourth, frames_grad
        )
        attn_fourth = pair(attn_second)
        fc1_total, fc2_total = spread(
            [fc_quarter, fc_second, fc_third, fc_fourth], bit, pair_bit, False
        )
        attn_fourth = hold(attn_fourth, fc2_total)[0]
        qkv_total, out_total = spread(
            [attn_quarter, attn_second, attn_third, attn_fourth], bit, pair_bit, True
        )
    else:
        w_2 = order(jnp.stack([w_2a, w_2b])).reshape(w_0.shape)
        w_3 = order(jnp.stack([w_3a, w_3b])).reshape(w_0.shape)
        fc_total = add(w_0, w_1, link(add(w_2, w_3)))
        attn_total = add(g_0, g_1, link(add(g_2, g_3)))
        fc_total, attn_total = lax.psum((fc_total, attn_total), "videos")
        fc1_total, fc2_total = [
            fc_total[k::2].reshape(units, features).astype(full) for k in range(2)
        ]
        attn_total = attn_total.astype(full)
        qkv_total, out_total = attn_total[:3].reshape(-1, features), attn_total[3]

    six = own[: 6 * width].reshape(6, width)
    own = own[6 * width :]
    turn = lambda value: value.reshape(3, width, features).transpose(0, 2, 1)
    return (
        mixed_out[None],
        frames_grad[None],
        fc_msg.T,
        all_cols[0],
        own[units + 2 * width : units + 3 * width],
        own[units + 3 * width :],
        turn(qkv_msg),
        msg_qkv_b_grad,
        msg_out_w_grad,
        cut(all_grad)[0],
        six[0],
        six[1],
        turn(qkv_total),
        own[units : units + 2 * width].reshape(2, width),
        out_total,
        six[2],
        six[3],
        six[4],
        fc1_total.T,
        own[:units],
        fc2_total,
        six[5],
    )


def solution(mesh):
    placed = (
        P("videos", None, "heads", None),
        P("videos", None, "heads", None),
        P("videos"),
        P("videos"),
        P(None, "heads"),
        P("heads"),
        P(),
        P(),
        P(None, None, "heads"),
        P(None, "heads"),
        P("heads", None),
        P(),
        P(),
        P(),
        P(None, None, "heads"),
        P(None, "heads"),
        P("heads", None),
        P(),
        P(),
        P(),
        P(None, "heads"),
        P("heads"),
        P("heads", None),
        P(),
    )
    return jax.shard_map(
        on_device,
        mesh=mesh,
        in_specs=placed,
        out_specs=(
            P("videos", None, "heads", None),
            P("videos", None, "heads", None),
            P(None, "heads"),
            P("heads"),
            P("heads"),
            P("heads"),
            P(None, None, "heads"),
            P(None, "heads"),
            P("heads", None),
            P("heads"),
            P("heads"),
            P("heads"),
            P(None, None, "heads"),
            P(None, "heads"),
            P("heads", None),
            P("heads"),
            P("heads"),
            P("heads"),
            P(None, "heads"),
            P("heads"),
            P("heads", None),
            P("heads"),
        ),
        check_vma=False,
    )
```

```python
import math

import jax
import jax.numpy as jnp
from jax import lax
from jax.experimental import pallas as pl
from jax.experimental.pallas import tpu as pltpu
from jax.sharding import PartitionSpec as P

HEAD_DIM = 64


epsilon = 1e-05

low = jnp.bfloat16
full = jnp.float32
VMEM_LIMIT = 40 * 1024 * 1024

RATE = 6e9


def norm_forward(value, gains, offset):
    average = jnp.mean(value, -1, keepdims=True)
    centered = value - average
    spread = jnp.mean(centered * centered, -1, keepdims=True)
    inverse = lax.rsqrt(spread + epsilon)
    unit = centered * inverse
    return (unit * gains.astype(jnp.float32) + offset.astype(jnp.float32), unit, inverse)


def norm_backward(gradient, unit, inverse, gains):
    scaled = gradient * gains.astype(jnp.float32)
    average = jnp.mean(scaled, -1, keepdims=True)
    second = jnp.mean(scaled * unit, -1, keepdims=True)
    return inverse * (scaled - average - unit * second)


def split_heads(tensors):
    return tuple(
        (
            tensor.reshape(tensor.shape[:-1] + (tensor.shape[-1] // HEAD_DIM, HEAD_DIM))
            for tensor in tensors
        )
    )


def project(normed, weight, biases):
    stacked = jnp.einsum("...d,cde->c...e", normed, weight, preferred_element_type=jnp.float32)
    return (
        (stacked[0] + biases[0]).astype(jnp.bfloat16),
        stacked[1].astype(jnp.bfloat16),
        (stacked[2] + biases[1]).astype(jnp.bfloat16),
    )


def attend_forward(queries, key_rows, values, keymask):
    scale_factor = HEAD_DIM ** (-0.5)
    scores = (
        jnp.einsum("bqhe,bkhe->bhqk", queries, key_rows, preferred_element_type=jnp.float32)
        * scale_factor
    )
    scores = jnp.where(keymask, scores, -1e30)
    largest = jnp.max(scores, -1, keepdims=True)
    exponent = jnp.exp(scores - largest)
    totals = jnp.sum(exponent, -1, keepdims=True)
    chances = exponent / totals
    output = jnp.einsum(
        "bhqk,bkhe->bqhe", chances.astype(jnp.bfloat16), values, preferred_element_type=jnp.float32
    )
    return (output.astype(jnp.bfloat16), largest + jnp.log(totals))


def attend_backward(queries, key_rows, values, keymask, log_total, grad_heads):
    scale_factor = HEAD_DIM ** (-0.5)
    scores = (
        jnp.einsum("bqhe,bkhe->bhqk", queries, key_rows, preferred_element_type=jnp.float32)
        * scale_factor
    )
    scores = jnp.where(keymask, scores, -1e30)
    chances = jnp.exp(scores - log_total)
    grad_chances = jnp.einsum(
        "bqhe,bkhe->bhqk", grad_heads, values, preferred_element_type=jnp.float32
    )
    deltas = jnp.sum(chances * grad_chances, -1, keepdims=True)
    grad_scores = (chances * (grad_chances - deltas)).astype(jnp.bfloat16)
    grad_query = (
        jnp.einsum("bhqk,bkhe->bqhe", grad_scores, key_rows, preferred_element_type=jnp.float32)
        * scale_factor
    ).astype(jnp.bfloat16)
    grad_key = (
        jnp.einsum("bhqk,bqhe->bkhe", grad_scores, queries, preferred_element_type=jnp.float32)
        * scale_factor
    ).astype(jnp.bfloat16)
    grad_value = jnp.einsum(
        "bhqk,bqhe->bkhe",
        chances.astype(jnp.bfloat16),
        grad_heads,
        preferred_element_type=jnp.float32,
    ).astype(jnp.bfloat16)
    return (grad_query, grad_key, grad_value)


def dot(left, right, left_dim=1, right_dim=0):
    return lax.dot_general(
        left, right, (((left_dim,), (right_dim,)), ((), ())), preferred_element_type=full
    )


def unit_of(value):
    centered = value - jnp.mean(value, -1, keepdims=True)
    inverse = lax.rsqrt(jnp.mean(centered * centered, -1, keepdims=True) + epsilon)
    return centered * inverse, inverse


def unit_backward(scaled, unit, inverse):
    average = jnp.mean(scaled, -1, keepdims=True)
    second = jnp.mean(scaled * unit, -1, keepdims=True)
    return inverse * (scaled - average - unit * second)


def row_sum(value):
    return jnp.sum(value, 0, keepdims=True)


def lane_mask(width, head):
    lane = lax.broadcasted_iota(jnp.int32, (1, width), 1)
    return (lane >= head * HEAD_DIM) & (lane < (head + 1) * HEAD_DIM)


def call_kernel(body, inputs, outputs, scratch, name, scalars=(), micros=3, loose=None, extras=()):
    def large(shape, dtype):
        if loose == 0 or (len(shape) == 2 and shape[0] == loose):
            return False
        return jnp.dtype(dtype).itemsize * math.prod(shape) > 2**17

    big_in = [large(each.shape, each.dtype) for each in inputs]
    big_out = [large(*each) for each in outputs]
    count = len(inputs) + len(outputs)

    def kernel(*refs):
        refs = refs[: len(inputs)] + refs[len(inputs) + len(extras) :]
        outer, spare = refs[:count], list(refs[count:])
        queue, coming, going = [], {}, []
        in_marks, out_marks = spare[-2:]
        targets = {}
        for k, ref in enumerate(outer):
            is_input = k < len(inputs)
            n = k if is_input else k - len(inputs)
            if not (big_in[n] if is_input else big_out[n]):
                queue.append(ref)
                continue
            buffer = spare.pop(len(scratch))
            queue.append(buffer)
            if is_input:
                copy = pltpu.make_async_copy(ref, buffer, in_marks.at[n])
                copy.start()
                coming[id(buffer)] = copy
            else:
                targets[id(buffer)] = pltpu.make_async_copy(buffer, ref, out_marks.at[n])
        queue += spare[: len(scratch)]
        handed = list(queue)

        def wait(*each):
            for ref in each:
                copy = coming.pop(id(ref), None)
                if copy is not None:
                    copy.wait()

        def send(*each):
            for ref in each:
                copy = targets.pop(id(ref), None)
                if copy is not None:
                    copy.start()
                    going.append(copy)

        body(lambda k: [queue.pop(0) for _ in range(k)], wait, send)
        wait(*handed)
        send(*handed)
        for copy in going:
            copy.wait()

    def spec(big, k=None):
        if k in scalars:
            return pl.BlockSpec(memory_space=pltpu.SMEM)
        return pl.BlockSpec(memory_space=pltpu.HBM if big else pltpu.VMEM)

    buffers = [pltpu.VMEM(each.shape, each.dtype) for each, big in zip(inputs, big_in) if big]
    buffers += [pltpu.VMEM(*each) for each, big in zip(outputs, big_out) if big]
    marks = [pltpu.SemaphoreType.DMA((len(inputs),)), pltpu.SemaphoreType.DMA((len(outputs),))]
    return list(
        pl.pallas_call(
            kernel,
            out_shape=[jax.ShapeDtypeStruct(*each) for each in outputs],
            in_specs=[spec(big, k) for k, big in enumerate(big_in)]
            + [pl.BlockSpec(memory_space=pl.ANY)] * len(extras),
            out_specs=[spec(big) for big in big_out],
            scratch_shapes=list(scratch) + buffers + marks,
            compiler_params=pltpu.CompilerParams(vmem_limit_bytes=VMEM_LIMIT),
            cost_estimate=pl.CostEstimate(
                flops=int(micros * RATE), bytes_accessed=1024, transcendentals=0
            ),
            name=name,
        )(*inputs, *extras)
    )


def combine(marks, *outputs, extras=()):
    terms = [term for output in outputs for slot in output for term in slot]
    _, rows, features = terms[0][0].shape
    chunk = rows // 2 if rows >= 192 else rows

    def kernel(_, *refs):
        queue = list(refs)
        sums = [
            [sum(queue.pop(0)[0].astype(full) for _ in slot) for slot in output]
            for output in outputs
        ]
        for out, values in zip(queue[len(extras) :], sums):
            for k, value in enumerate(values):
                out[k] = value.astype(low)
        queue[-1][...] = jnp.zeros((8, 128), full)

    def place(_, base, *steps):
        return lambda c, s: (base + sum(step * s[k] for k, step in enumerate(steps) if step), c, 0)

    return pl.pallas_call(
        kernel,
        grid_spec=pltpu.PrefetchScalarGridSpec(
            num_scalar_prefetch=1,
            grid=(rows // chunk,),
            in_specs=[pl.BlockSpec((1, chunk, features), place(*term)) for term in terms]
            + [pl.BlockSpec(memory_space=pl.ANY)] * len(extras),
            out_specs=[
                pl.BlockSpec((len(output), chunk, features), lambda c, s: (0, c, 0))
                for output in outputs
            ]
            + [pl.BlockSpec((8, 128), lambda c, s: (0, 0))],
        ),
        out_shape=[jax.ShapeDtypeStruct((len(each), rows, features), low) for each in outputs]
        + [jax.ShapeDtypeStruct((8, 128), full)],
        compiler_params=pltpu.CompilerParams(vmem_limit_bytes=VMEM_LIMIT),
        name="combine",
    )(marks, *[term[0] for term in terms], *extras)


def spread(pieces, marks, split):
    _, rows, features = pieces[0].shape

    def body(take, wait, send):
        (mark_ref,) = take(1)
        piece_refs = take(4)
        first_ref, second_ref = take(2)
        for k, piece in enumerate(piece_refs):
            wait(piece)
            outer, inner = mark_ref[0] ^ (k // 2), mark_ref[1] ^ (k % 2)
            begin = pl.multiple_of((outer * 2 + inner) * rows, 8)
            first_ref[pl.ds(begin, rows)] = piece[0].astype(full)
            if not split:
                second_ref[pl.ds(begin, rows)] = piece[1].astype(full)
            else:

                @pl.when(outer == 0)
                def _(piece=piece, begin=begin):
                    first_ref[pl.ds(4 * rows + begin, rows)] = piece[1].astype(full)

                @pl.when(outer == 1)
                def _(piece=piece, inner=inner):
                    at = pl.ds(pl.multiple_of(inner * rows, 8), rows)
                    second_ref[at] = piece[1].astype(full)

    sizes = (6, 2) if split else (4, 4)
    outputs = [((size * rows, features), full) for size in sizes]
    return call_kernel(body, [marks, *pieces], outputs, [], "spread", (0,), 3, 0)


def prepare(marks, qkv, out, extra, fc1, fc2, extras):
    width, features = out.shape
    units = fc2.shape[0]
    half = units // 2
    size = 4 * width + extra.shape[0]

    def body(take, wait, send):
        mark_ref, qkv_ref, out_ref, extra_ref, fc1_ref, fc2_ref = take(6)
        pack_ref, half_ref, fcs_ref, first_ref, second_ref = take(5)
        wait(qkv_ref, out_ref, extra_ref)
        pack_ref[: 3 * width] = qkv_ref[...]
        pack_ref[3 * width : 4 * width] = out_ref[...]
        pack_ref[4 * width :] = extra_ref[...]
        here = mark_ref[0]
        half_ref[...] = pack_ref[pl.ds(pl.multiple_of(here * (size // 2), 16), size // 2)]
        send(pack_ref, half_ref)
        wait(fc1_ref, fc2_ref)
        for k in range(2):
            fcs_ref[2 * k] = fc1_ref[:, k * half : (k + 1) * half].T
            fcs_ref[2 * k + 1] = fc2_ref[k * half : (k + 1) * half]
        first_ref[0] = fcs_ref[2 * here]
        second_ref[0] = fcs_ref[2 * here + 1]

    outputs = [((size, features), low), ((size // 2, features), low)]
    outputs += [((4, half, features), low)] + [((1, half, features), low)] * 2
    inputs = [marks, qkv, out, extra, fc1, fc2]
    return call_kernel(body, inputs, outputs, [], "prepare", (0,), extras=extras)


def message_start(marks, leads, weight, bias, extras):
    slots, _ = leads[0].shape
    width = weight.shape[0]

    def body(take, wait, send):
        (mark_ref,) = take(1)
        lead_refs = take(len(leads))
        weight_ref, bias_ref = take(2)
        lead_ref, part_ref = take(2)
        here = mark_ref[2]
        lead = lead_refs[0][...].astype(full)
        for k in range(1, len(leads)):
            lead = jnp.where(here == k, lead_refs[k][...].astype(full), lead)
        lead_ref[...] = lead
        part_ref[...] = dot(lead.astype(low), weight_ref[...], 1, 1) + bias_ref[...]

    outputs = [(leads[0].shape, full), ((slots, width), full)]
    inputs = [marks, *leads, weight, bias]
    return call_kernel(body, inputs, outputs, [], "message_start", (0,), 3, 0, extras)


def message_forward(message, norm, qkv, out, bias, key_row, extras):
    slots, features = message.shape
    width = out.shape[0]

    def body(take, wait, send):
        message_ref, norm_ref, qkv_ref, out_ref, bias_ref, key_ref = take(6)
        normed_ref, saved_ref, part_ref = take(3)
        wait(message_ref, qkv_ref, out_ref)
        unit, _ = unit_of(message_ref[...])
        normed = (unit * norm_ref[0:1] + norm_ref[1:2]).astype(low)
        normed_ref[...] = normed.astype(full)
        query, key, value = [
            dot(normed, qkv_ref[k * width : (k + 1) * width], 1, 1) for k in range(3)
        ]
        query = (query + bias_ref[0:1]).astype(low)
        key = key.astype(low)
        value = (value + bias_ref[1:2]).astype(low)
        result = jnp.zeros((slots, width), full)
        for j in range(width // HEAD_DIM):
            mask = lane_mask(width, j)
            scaled = query.astype(full) * HEAD_DIM ** (-0.5)
            one = jnp.where(mask, scaled, jnp.zeros_like(scaled)).astype(low)
            scores = dot(one, key, 1, 1) + key_ref[...]
            exponent = jnp.exp(scores - jnp.max(scores, -1, keepdims=True))
            chances = exponent / jnp.sum(exponent, -1, keepdims=True)
            result = jnp.where(mask, dot(chances.astype(low), value), result)
        result = result.astype(low)
        for k, each in enumerate((query, key, value, result)):
            saved_ref[k] = each.astype(full)
        part_ref[...] = dot(result, out_ref[...])

    outputs = [((slots, features), full), ((4, slots, width), full), ((slots, features), full)]
    inputs = [message, norm, qkv, out, bias, key_row]
    return call_kernel(body, inputs, outputs, [], "message_forward", (), 3, 0, extras)


def message_backward(grad_message, saved, qkv, out, key_row, extras):
    slots, features = grad_message.shape
    width = out.shape[0]

    def body(take, wait, send):
        grad_ref, saved_ref, qkv_ref, out_ref, key_ref = take(5)
        stacked_ref, part_ref = take(2)
        wait(saved_ref, qkv_ref, out_ref)
        grad_o = dot(grad_ref[...].astype(low), out_ref[...], 1, 1).astype(low).astype(full)
        scaled = saved_ref[0] * HEAD_DIM ** (-0.5)
        key, value = saved_ref[1].astype(low), saved_ref[2].astype(low)
        grad_q = grad_k = grad_v = jnp.zeros((slots, width), full)
        for j in range(width // HEAD_DIM):
            mask = lane_mask(width, j)
            one_query = jnp.where(mask, scaled, jnp.zeros_like(scaled)).astype(low)
            one_grad = jnp.where(mask, grad_o, jnp.zeros_like(grad_o)).astype(low)
            scores = dot(one_query, key, 1, 1) + key_ref[...]
            exponent = jnp.exp(scores - jnp.max(scores, -1, keepdims=True))
            chances = exponent / jnp.sum(exponent, -1, keepdims=True)
            grad_p = dot(one_grad, value, 1, 1)
            grad_s = chances * (grad_p - jnp.sum(chances * grad_p, -1, keepdims=True))
            grad_s = grad_s.astype(low)
            grad_v += dot(chances.astype(low), one_grad, 0, 0)
            grad_k += dot(grad_s, one_query, 0, 0)
            grad_q = jnp.where(mask, dot(grad_s, key), grad_q)
        grads = [each.astype(low) for each in (grad_q * HEAD_DIM ** (-0.5), grad_k, grad_v)]
        for k, each in enumerate(grads):
            stacked_ref[k] = each.astype(full)
        part_ref[...] = sum(
            dot(each, qkv_ref[k * width : (k + 1) * width]) for k, each in enumerate(grads)
        )

    outputs = [((3, slots, width), full), ((slots, features), full)]
    inputs = [grad_message, saved, qkv, out, key_row]
    return call_kernel(body, inputs, outputs, [], "message_backward", (), 3, 0, extras)


def message_bundle(marks, part, one_sums, two_sums, hidden, heads):
    slots, features = part.shape
    width = heads[0].shape[1]
    half = features // 2

    def body(take, wait, send):
        mark_ref, part_ref, one_ref, two_ref = take(4)
        near_refs, far_refs, head_refs = take(2), take(4), take(4)
        (out_ref,) = take(1)
        out_ref[...] = jnp.zeros(out_ref.shape, full)
        out_ref[:slots] = part_ref[...]
        out_ref[slots : slots + 2] = one_ref[...]
        out_ref[slots + 2 : slots + 6] = two_ref[...]
        bit, here = mark_ref[0], mark_ref[2]
        for k in range(4):
            if k < 2:
                first, second = near_refs[k][0:1], near_refs[k][1:2]
            else:
                own, other = far_refs[2 * k - 4][...], far_refs[2 * k - 3][...]
                first, second = jnp.where(bit == 0, own, other), jnp.where(bit == 0, other, own)
            row = pl.ds(slots + 6 + (here ^ k), 1)
            out_ref[row, :half] = first
            out_ref[row, half:] = second
            row = pl.ds(slots + 10 + (here ^ k), 1)
            out_ref[row, :width] = head_refs[k][0:1]
            out_ref[row, 256 : 256 + width] = head_refs[k][1:2]

    inputs = [marks, part, one_sums, two_sums, *hidden, *heads]
    outputs = [((slots + 16, features), full)]
    return call_kernel(body, inputs, outputs, [], "message_bundle", (0,), 3, 0)[0]


def message_finish(marks, bundles, grad_message, message, norm, normed, lead, stacked, saved, weight, field, extras):
    slots, features = message.shape
    width = weight.shape[0]
    groups = features // width

    def body(take, wait, send):
        mark_ref, bundle_ref, grad_ref, message_ref, norm_ref, normed_ref = take(6)
        lead_ref, stacked_ref, saved_ref, weight_ref = take(4)
        out_ref, part_ref = take(2)
        here = mark_ref[2]
        bundle = sum(bundle_ref[k] for k in range(groups))

        def cut(value):
            result = value[:, :width]
            for k in range(1, groups):
                result = jnp.where(here == k, value[:, k * width : (k + 1) * width], result)
            return result

        def own_row(first):
            result = bundle[first : first + 1]
            for k in range(1, groups):
                result = jnp.where(here == k, bundle[first + k : first + k + 1], result)
            return result

        grad_normed = bundle[:slots]
        unit, inverse = unit_of(message_ref[...])
        grad = grad_ref[...]
        columns = cut(grad + unit_backward(grad_normed * norm_ref[0:1], unit, inverse)).astype(low)
        part_ref[...] = dot(columns, weight_ref[...])
        at = 0
        for value in (normed_ref[...], grad, lead_ref[...]):
            out_ref[:, at : at + features] = value
            at += features
        for value in (stacked_ref[0], stacked_ref[1], stacked_ref[2], saved_ref[3], columns):
            out_ref[:, at : at + field] = jnp.zeros((slots, field), full)
            out_ref[:, at : at + width] = value.astype(full)
            at += field
        out_ref[:, at:] = jnp.zeros((slots, 512), full)
        out_ref[0:6, at : at + width] = cut(bundle[slots : slots + 6])
        units, heads = own_row(slots + 6), own_row(slots + 10)
        half = features // 2
        out_ref[6:7, at : at + half] = units[:, :half]
        out_ref[7:8, at : at + half] = units[:, half:]
        side = at + 256
        out_ref[0:1, side : side + width] = cut(row_sum(grad_normed * unit))
        out_ref[1:2, side : side + width] = cut(row_sum(grad_normed))
        out_ref[2:3, side : side + width] = heads[:, :width]
        out_ref[3:4, side : side + width] = heads[:, 256 : 256 + width]

    inputs = [marks, bundles, grad_message, message, norm, normed, lead, stacked, saved, weight]
    outputs = [((slots, 3 * features + 5 * field + 512), full), ((slots, features), full)]
    return call_kernel(body, inputs, outputs, [], "message_finish", (0,), 3, 0, extras)


def message_weights(operands, features, width, field, count):
    rows, total = operands.shape
    slots = rows // count
    starts = [k * features for k in range(3)] + [3 * features + k * field for k in range(5)]
    last = 3 * features + 5 * field

    def body(take, wait, send):
        (rows_ref,) = take(1)
        wait(rows_ref)
        qkv_ref, out_ref, fc_ref, heads_ref, grad_ref, cols_ref, own_ref = take(7)
        wide = [rows_ref[:, at : at + features] for at in starts[:3]]
        thin = [rows_ref[:, at : at + width] for at in starts[3:]]
        for k in range(3):
            qkv_ref[k * width : (k + 1) * width] = dot(thin[k], wide[0], 0, 0)
        out_ref[...] = dot(thin[3], wide[1], 0, 0)
        fc_ref[...] = dot(thin[4], wide[2], 0, 0)
        heads_ref[...] = jnp.concatenate(
            [row_sum(thin[0].astype(full)), row_sum(thin[2].astype(full))], 0
        )
        grad_ref[...] = row_sum(wide[1].astype(full))
        cols_ref[...] = row_sum(thin[4].astype(full))
        own = rows_ref[:, last:].astype(full)
        own_ref[...] = sum(own[k * slots : (k + 1) * slots] for k in range(count))

    outputs = [
        ((3 * width, features), full),
        ((width, features), full),
        ((width, features), full),
        ((2, width), full),
        ((1, features), full),
        ((1, width), full),
        ((slots, total - last), full),
    ]
    return call_kernel(body, [operands], outputs, [], "message_weights", (), 3, 0)


def place_rows(target, value_of, mine, span, rows, near_count):
    for f in range(mine):
        for k in range(near_count):
            target[f * span + k * rows : f * span + (k + 1) * rows] = value_of(k, f).astype(full)


def frame_values(marks_ref, own_ref, came_ref, near_ref, mine):
    def value_of(k, f):
        if k == 0:
            return own_ref[marks_ref[2] * mine + f]
        if k == 2:
            return came_ref[(marks_ref[2] % 2) * mine + f]
        return near_ref[(k // 2) * mine + f]

    return value_of


def attn_heads(normed, pack, saved_ref, key_bias, mine):
    rows, _ = normed.shape
    span = rows // mine
    width = saved_ref.shape[2]
    extra = pack[4 * width : 4 * width + 16].astype(full)
    saved_ref[0] = (dot(normed, pack[:width], 1, 1) + extra[0:1, :width]).astype(low)
    saved_ref[1] = dot(normed, pack[width : 2 * width], 1, 1).astype(low)
    saved_ref[2] = (dot(normed, pack[2 * width : 3 * width], 1, 1) + extra[1:2, :width]).astype(low)
    for f in range(mine):
        at = slice(f * span, (f + 1) * span)
        query = saved_ref[0, at] * jnp.asarray(HEAD_DIM ** (-0.5), low)
        key, value = saved_ref[1, at], saved_ref[2, at]
        out = jnp.zeros((span, width), full)
        for j in range(width // HEAD_DIM):
            mask = lane_mask(width, j)
            scores = dot(jnp.where(mask, query, jnp.zeros_like(query)), key, 1, 1)
            scores = scores + key_bias
            exponent = jnp.exp(scores - jnp.max(scores, -1, keepdims=True))
            share = 1.0 / jnp.sum(exponent, -1, keepdims=True)
            out = jnp.where(mask, dot(exponent.astype(low), value) * share, out)
        saved_ref[3, at] = out.astype(low)
    return dot(saved_ref[3], pack[3 * width : 4 * width])


def attn_start(marks, frames, came, near, carried, norm, key_row, packs, mine, span, extras):
    _, rows, features = frames.shape
    width = features // 4
    groups = 4
    all_rows = groups * rows
    count = len(packs)

    def body(take, wait, send):
        marks_ref, own_ref, came_ref, near_ref, carried_ref, norm_ref, key_ref = take(7)
        pack_refs = take(count)
        joined_ref, normed_ref, total_ref, token_ref = take(4)
        saved_refs = take(count)
        token_ref[...] = jnp.zeros((8, 128), full)
        (joined,) = take(1)
        wait(own_ref, came_ref, near_ref)
        for f in range(mine):
            end = (f + 1) * span
            joined[f * span + all_rows : end] = jnp.zeros((span - all_rows, features), full)
            joined[f * span + all_rows : f * span + all_rows + 1] = carried_ref[f : f + 1]
        value_of = frame_values(marks_ref, own_ref, came_ref, near_ref, mine)
        place_rows(joined, value_of, mine, span, rows, groups)
        joined_ref[...] = joined[...].astype(low)
        unit, _ = unit_of(joined_ref[...].astype(full))
        normed_ref[...] = (unit * norm_ref[0:1] + norm_ref[1:2]).astype(low)
        send(joined_ref, normed_ref)
        for b in range(count):
            wait(pack_refs[b])
            part = attn_heads(normed_ref[...], pack_refs[b], saved_refs[b], key_ref[...], mine)
            send(saved_refs[b])
            total_ref[...] = total_ref[...] + part if b else part

    size = mine * span
    inputs = [marks, frames, came, near, carried, norm, key_row, *packs]
    outputs = [((size, features), low)] * 2 + [((size, features), full), ((8, 128), full)]
    outputs += [((4, size, width), low)] * count
    scratch = [pltpu.VMEM((size, features), full)]
    results = call_kernel(body, inputs, outputs, scratch, "attn_start", (0,), 9, size, extras)
    return results[:4], results[4:]


def attn_rest(marks, normed, total, key_row, halves, mine, extras):
    rows, features = normed.shape
    width = features // 4
    count = len(halves)

    def body(take, wait, send):
        marks_ref, normed_ref, total_in, key_ref = take(4)
        half_refs = [take(2) for _ in range(count)]
        total_ref, token_ref = take(2)
        pack_refs, saved_refs = take(count), take(count)
        token_ref[...] = jnp.zeros((8, 128), full)
        here = marks_ref[0]
        wait(normed_ref)
        for b in range(count):
            wait(*half_refs[b])
            size = half_refs[b][0].shape[0]
            for k, each in enumerate(half_refs[b]):
                pack_refs[b][pl.ds(pl.multiple_of((here ^ k) * size, 16), size)] = each[...]
            send(pack_refs[b])
            part = attn_heads(normed_ref[...], pack_refs[b], saved_refs[b], key_ref[...], mine)
            send(saved_refs[b])
            wait(total_in)
            total_ref[...] = (total_ref if b else total_in)[...] + part

    inputs = [marks, normed, total, key_row] + [each for pair in halves for each in pair]
    outputs = [((rows, features), full), ((8, 128), full)]
    outputs += [((2 * own.shape[0], features), low) for own, _ in halves]
    outputs += [((4, rows, width), low)] * count
    results = call_kernel(body, inputs, outputs, [], "attn_rest", (0,), 9, rows, extras)
    return results[:2], results[2 : 2 + count], results[2 + count :]


def out_blocks(own_ref, near_ref, far_ref, source, mine, span):
    rows = own_ref.shape[1]
    for f in range(mine):
        for k in range(4):
            value = source[f * span + k * rows : f * span + (k + 1) * rows].astype(low)
            if k < 2:
                (near_ref if k else own_ref)[f] = value
            else:
                far_ref[k - 2, f] = value


def mlp_step(start, carry, grad, consts, weights, biases, last, mine, rows, extras):
    first = carry is None
    total_rows, features = start[0].shape
    span = total_rows // mine
    size = biases[0].shape[1]
    count = len(weights)
    lengths = [[each.shape[0] for each in group] for group in weights]

    def body(take, wait, send):
        if first or last:
            joined_ref, total_ref, const_ref = take(3)
        if first:
            grad_sources = take(4)
        else:
            normed_ref, y_in, d_in, grad_ref = take(4)
        fc_bases = [take(len(group)) for group in lengths]
        fc_refs = [
            [ref.at[k] for ref, n in zip(refs, group) for k in range(n)]
            for refs, group in zip(fc_bases, lengths)
        ]
        bias_refs = take(count)
        if last:
            own_ref, near_ref, far_ref, mixed_ref, attn_ref, sums_ref = take(6)
        else:
            y_ref, d_ref = take(2)
        if first:
            normed_ref, grad_ref = take(2)
        w_refs, b_refs = take(count), take(count)
        if last:
            y_ref, d_ref = take(2)

        def mixed():
            return joined_ref[...].astype(full) + total_ref[...] + const_ref[0:1]

        if first:
            wait(*grad_sources)
            for f in range(mine):
                end = (f + 1) * span
                d_ref[f * span + 4 * rows : end] = jnp.zeros((span - 4 * rows, features), full)
            place_rows(d_ref, frame_values(*grad_sources, mine), mine, span, rows, 4)
            grad_ref[...] = d_ref[...].astype(low)
            wait(joined_ref, total_ref)
            unit, _ = unit_of(mixed())
            normed_ref[...] = (unit * const_ref[1:2] + const_ref[2:3]).astype(low)
            send(grad_ref, normed_ref)
        else:
            wait(normed_ref, grad_ref)
        normed = normed_ref[...]
        grad_rows = grad_ref[...]
        fresh = True
        for b in range(count):
            wait(*fc_bases[b])
            for c in range(len(fc_refs[b]) // 2):
                fc1, fc2 = fc_refs[b][2 * c][...], fc_refs[b][2 * c + 1][...]
                pre = dot(normed, fc1, 1, 1) + bias_refs[b][c : c + 1]
                gate = jax.nn.sigmoid(1.702 * pre)
                active = (pre * gate).astype(low)
                back = dot(grad_rows, fc2, 1, 1) * (gate + 1.702 * pre * gate * (1.0 - gate))
                back = back.astype(low)
                b_refs[b][c : c + 1] = row_sum(back.astype(full))
                y_part = dot(active, fc2)
                d_part = dot(back, fc1)
                if not fresh:
                    y_ref[...] += y_part
                    d_ref[...] += d_part
                elif first:
                    y_ref[...] = y_part
                    d_ref[...] = d_part
                else:
                    wait(y_in, d_in)
                    y_ref[...] = y_in[...] + y_part
                    d_ref[...] = d_in[...] + d_part
                fresh = False
                w_refs[b][2 * c] = dot(back, normed, 0, 0).astype(low)
                w_refs[b][2 * c + 1] = dot(active, grad_rows, 0, 0).astype(low)
            send(w_refs[b])
        if last:
            wait(joined_ref, total_ref)
            value = mixed()
            unit, inverse = unit_of(value)
            y_ref[...] = value + y_ref[...] + const_ref[3:4]
            out_blocks(own_ref, near_ref, far_ref, y_ref, mine, span)
            send(far_ref, near_ref, own_ref)
            grad_normed = d_ref[...]
            top = grad_rows.astype(full)
            grad_mixed = top + unit_backward(grad_normed * const_ref[1:2], unit, inverse)
            mixed_ref[...] = grad_mixed
            grad_attn = grad_mixed.astype(low)
            attn_ref[...] = grad_attn
            sums_ref[...] = jnp.concatenate(
                [
                    row_sum(grad_attn.astype(full)),
                    row_sum(grad_normed * unit),
                    row_sum(grad_normed),
                    row_sum(top),
                ],
                0,
            )

    big = ((total_rows, features), full)
    small = ((total_rows, features), low)
    inputs = [*start, consts] if first or last else []
    inputs += list(grad) if first else [*carry, grad]
    scalars = (3,) if first else ()
    inputs += [each for group in weights for each in group] + list(biases)
    if last:
        outputs = [((mine, rows, features), low)] * 2 + [((2, mine, rows, features), low)]
        outputs += [big, small, ((4, features), full)]
    else:
        outputs = [big, big]
    outputs += [small, small] if first else []
    lead = len(outputs)
    outputs += [((sum(group), size, features), low) for group in lengths]
    outputs += [(each.shape, full) for each in biases]
    scratch = [pltpu.VMEM((total_rows, features), full)] * 2 if last else []
    results = call_kernel(body, inputs, outputs, scratch, "mlp_step", scalars, 12, total_rows, extras)
    return results[:lead], results[lead : lead + count], results[lead + count :]


def attn_backward(normed, grad, key_column, total, packs, saved, mine, frame_rows, ending, extras):
    rows, features = normed.shape
    span = rows // mine
    width = features // 4
    count = len(packs)
    first = total is None
    last = ending is not None

    def body(take, wait, send):
        normed_ref, grad_ref, key_ref = take(3)
        if not first:
            (total_in,) = take(1)
        if last:
            joined_ref, mixed_ref, norm_ref = take(3)
        pack_refs = take(count)
        saved_refs = take(count)
        q_refs, k_refs, v_refs, o_refs = [[each.at[k] for each in saved_refs] for k in range(4)]
        if last:
            own_ref, near_ref, far_ref, carried_ref, sums_ref = take(5)
        else:
            (total_ref,) = take(1)
        w_refs, b_refs = take(count), take(count)
        dq_ref, dk_ref, dv_ref, do_ref = take(4)
        if last:
            (total_ref,) = take(1)
        wait(normed_ref, grad_ref, key_ref)
        normed = normed_ref[...]
        grad = grad_ref[...]
        key_bias = key_ref[...]
        scale = HEAD_DIM ** (-0.5)
        for b in range(count):
            pack = pack_refs[b]
            wait(pack, saved_refs[b])
            do_ref[...] = dot(grad, pack[3 * width : 4 * width], 1, 1).astype(low)
            for f in range(mine):
                at = slice(f * span, (f + 1) * span)
                query = q_refs[b][at] * jnp.asarray(scale, low)
                key, value, grad_o = k_refs[b][at], v_refs[b][at], do_ref[at]
                grad_q = grad_k = grad_v = jnp.zeros((span, width), full)
                for j in range(width // HEAD_DIM):
                    mask = lane_mask(width, j)
                    one_query = jnp.where(mask, query, jnp.zeros_like(query))
                    one_grad = jnp.where(mask, grad_o, jnp.zeros_like(grad_o))
                    scores = dot(key, one_query, 1, 1) + key_bias
                    exponent = jnp.exp(scores - jnp.max(scores, 0, keepdims=True))
                    chances = exponent * (1.0 / row_sum(exponent))
                    grad_p = dot(value, one_grad, 1, 1)
                    grad_s = (chances * (grad_p - row_sum(chances * grad_p))).astype(low)
                    grad_v += dot(chances.astype(low), one_grad)
                    grad_k += dot(grad_s, one_query)
                    grad_q = jnp.where(mask, dot(grad_s, key, 0, 0), grad_q)
                dq_ref[at] = (grad_q * scale).astype(low)
                dk_ref[at] = grad_k.astype(low)
                dv_ref[at] = grad_v.astype(low)
            grads = (dq_ref[...], dk_ref[...], dv_ref[...])
            part = sum(dot(each, pack[k * width : (k + 1) * width]) for k, each in enumerate(grads))
            if b:
                total_ref[...] += part
            else:
                if not first:
                    wait(total_in)
                total_ref[...] = part if first else total_in[...] + part
            for k, each in enumerate(grads):
                w_refs[b][k] = dot(each, normed, 0, 0).astype(low)
            w_refs[b][3] = dot(o_refs[b][...], grad, 0, 0).astype(low)
            send(w_refs[b])
            b_refs[b][...] = jnp.concatenate(
                [row_sum(grads[0].astype(full)), row_sum(grads[2].astype(full))], 0
            )
        if last:
            wait(joined_ref, mixed_ref)
            unit, inverse = unit_of(joined_ref[...].astype(full))
            grad_normed = total_ref[...]
            grad_joined = unit_backward(grad_normed * norm_ref[0:1], unit, inverse)
            total_ref[...] = mixed_ref[...] + grad_joined
            all_rows = 4 * frame_rows
            for f in range(mine):
                at = f * span + all_rows
                carried_ref[f : f + 1] = total_ref[at : at + 1]
            out_blocks(own_ref, near_ref, far_ref, total_ref, mine, span)
            send(far_ref, near_ref, own_ref)
            sums_ref[...] = jnp.concatenate(
                [row_sum(grad_normed * unit), row_sum(grad_normed)], 0
            )

    inputs = [normed, grad, key_column] + ([] if first else [total]) + list(ending or ())
    inputs += [*packs, *saved]
    if last:
        outputs = [((mine, frame_rows, features), low)] * 2
        outputs += [((2, mine, frame_rows, features), low)]
        outputs += [((mine, features), full), ((2, features), full)]
    else:
        outputs = [((rows, features), full)]
    lead = len(outputs)
    outputs += [((4, width, features), low)] * count + [((2, width), full)] * count
    scratch = [pltpu.VMEM((rows, width), low)] * 4
    scratch += [pltpu.VMEM((rows, features), full)] if last else []
    results = call_kernel(body, inputs, outputs, scratch, "attn_backward", (), 9, rows, extras)
    grads = [(results[lead + b], results[lead + count + b]) for b in range(count)]
    return results[:lead], grads


def swap(value, axis, offset):
    size = lax.axis_size(axis)
    return lax.ppermute(value, axis, [(place, place ^ offset) for place in range(size)])


def pick(value, index, count, dimension=0):
    return lax.dynamic_slice_in_dim(value, index * count, count, dimension)


def add(*values):
    return sum(value.astype(full) for value in values).astype(low)


def hold(*values):
    return lax.optimization_barrier(values)


def tie(value, token):
    return value + token[:1, :1]


def everyone(value):
    size = lax.axis_size("heads")
    return [value] + [swap(value, "heads", k) for k in range(1, size)]


def by_place(pieces, here):
    stacked = jnp.stack(pieces)
    return [lax.dynamic_index_in_dim(stacked, here ^ k, 0, False) for k in range(len(pieces))]


def frame_pieces(frames, here, groups):
    mine = frames.shape[0] // groups
    return [pick(frames, here ^ k, mine) for k in range(groups)]


def send_each(pieces):
    return [swap(piece, "heads", k) if k else piece for k, piece in enumerate(pieces)]


def on_device(
    frames,
    out_grad,
    frame_tokens,
    frame_count,
    msg_fc_w,
    msg_fc_b,
    msg_norm_g,
    msg_norm_b,
    msg_qkv_w,
    msg_qkv_b,
    msg_out_w,
    msg_out_b,
    norm1_g,
    norm1_b,
    attn_qkv_w,
    attn_qkv_b,
    attn_out_w,
    attn_out_b,
    norm2_g,
    norm2_b,
    fc1_w,
    fc1_b,
    fc2_w,
    fc2_b,
):
    _, slots, rows, features = frames.shape
    groups = lax.axis_size("heads")
    videos = lax.axis_size("videos")
    here = lax.axis_index("heads")
    video = lax.axis_index("videos")
    bit = video % 2
    far = groups // 2
    mine = slots // groups
    span = -(-(rows * groups + 1) // 16) * 16
    tail = span - rows * groups
    width = msg_fc_w.shape[1]
    units = fc1_w.shape[1]
    half = units // 2
    quick = videos == 8
    pair_bit = (video // 2) % 2
    frames = frames[0]
    out_grad = out_grad[0]
    marks = [bit, pair_bit, here, here ^ 1, here % 2, (here // 2) ^ 1]
    marks = jnp.stack(marks).astype(jnp.int32)
    stack = lambda *vectors: jnp.stack(vectors).astype(full)
    link = lambda value: swap(value, "heads", far)
    side = lambda value: swap(value, "heads", 1)
    pair = lambda value: swap(value, "videos", 1)
    two = range(mine)
    far_rows = lambda value: [[(value, k, 0, 0, 0, 0, 0, far * mine)] for k in range(far * mine)]
    near_rows = lambda value, came: [[(value, k, 0, 0, 0, mine)] for k in two] + [
        [(came, mine + k, 0, 0, 0, 0, -mine)] for k in two
    ]

    leads = everyone(frames[:, 0, :])
    row_send, _ = combine(marks, [each for each in far_rows(frames)])
    row_came = link(row_send)
    leading, fc_part = message_start(
        marks, leads, msg_fc_w.T, msg_fc_b[None].astype(full), [row_send]
    )
    columns = everyone(fc_part)
    wide = lambda value: jnp.pad(value, ((0, 0), (0, features - value.shape[1])))
    extra = jnp.concatenate(
        [wide(attn_qkv_b), wide(fc1_b[None]), jnp.zeros((29, features), low)], 0
    )
    pack, pack_send, fcs, fc_send_1, fc_send_2 = prepare(
        marks,
        attn_qkv_w.transpose(0, 2, 1).reshape(3 * width, features),
        attn_out_w,
        extra,
        fc1_w,
        fc2_w,
        [fc_part],
    )
    pack_own = link(pack_send)
    message = jnp.concatenate(by_place(columns, here), 1)
    msg_norm = stack(msg_norm_g, msg_norm_b)
    msg_key = jnp.where(jnp.arange(slots) < frame_count[0], 0.0, -1e30).astype(full)[None]
    msg_qkv = msg_qkv_w.transpose(0, 2, 1).reshape(3 * width, features)
    msg_in, msg_saved, msg_part = message_forward(
        message, msg_norm, msg_qkv, msg_out_w, msg_qkv_b.astype(full), msg_key, [pack_send]
    )
    msg_pieces = frame_pieces(msg_part, here, groups)
    msg_rows = send_each(msg_pieces)
    row_next, token = combine(marks, near_rows(frames, row_came), extras=msg_pieces)
    row_near = side(row_next)
    pack_near = side(pack)
    grad_send, token = combine(marks, far_rows(out_grad), extras=[token])
    carried = tie(pick(message + msg_out_b, here, mine) + sum(msg_rows), token)

    places = jnp.concatenate([(here ^ k) * rows + jnp.arange(rows) for k in range(groups)])
    seen = jnp.concatenate([places < frame_tokens[0], jnp.arange(tail) == 0])
    key_bias = jnp.where(seen, 0.0, -1e30).astype(full)
    norm = stack(norm1_g, norm1_b)
    pack_own, carried = hold(pack_own, carried)
    pack_other, pack_own_3 = pair(pack_own), side(pack_own)
    grad_came = link(grad_send)
    (joined, normed, total, token), saved = attn_start(
        marks,
        frames,
        row_came,
        row_near,
        carried,
        norm,
        key_bias[None],
        [pack, pack_near],
        mine,
        span,
        [pack_own],
    )
    fc_own_1 = link(fc_send_1)
    token, pack_other = hold(token, pack_other)
    pack_other_3 = side(pack_other)
    grad_next, _ = combine(marks, near_rows(out_grad, grad_came), extras=[token])
    grad_near = side(grad_next)
    fc_near = side(fcs)
    halves = [(pack_own, pack_other), (pack_own_3, pack_other_3)]
    (total, token), far_packs, rest = attn_rest(
        marks, normed, total, key_bias[None], halves, mine, [grad_next]
    )
    saved += rest
    packs = [pack, pack_near, *far_packs]
    token, fc_own_1 = hold(token, fc_own_1)
    fc_own_2, fc_other_1, fc_own_31 = link(fc_send_2), pair(fc_own_1), side(fc_own_1)

    consts = stack(attn_out_b, norm2_g, norm2_b, fc2_b)
    bias = [each[4 * width + 2].reshape(2, half).astype(full) for each in packs]
    order = lambda value: jnp.concatenate([pick(value, bit, 1), pick(value, 1 - bit, 1)], 0)
    bias = bias[:2] + [order(each) for each in bias[2:]]
    parts = [[each[:1] for each in bias[:1:-1]], [each[1:] for each in bias[:1:-1]]]
    start = (joined, total)
    sources = (marks, out_grad, grad_came, grad_near)
    (y_sum, d_sum, normed_two, grad_top), (w_0,), (b_0,) = mlp_step(
        start, None, sources, consts, [[fcs]], bias[:1], False, mine, rows, [token]
    )
    b_0, bias[1], fc_own_2, fc_other_1 = hold(b_0, bias[1], fc_own_2, fc_other_1)
    fc_other_2, fc_own_32 = pair(fc_own_2), side(fc_own_2)
    fc_other_31 = side(fc_other_1)
    carry = (normed_two, y_sum, d_sum)
    (y_sum, d_sum), (w_1,), (b_1,) = mlp_step(
        start, carry, grad_top, consts, [[fc_near]], bias[1:2], False, mine, rows, []
    )
    b_1, parts[0][0], fc_other_2 = hold(b_1, parts[0][0], fc_other_2)
    fc_other_32, w_1_came = side(fc_other_2), side(w_1)
    carry = (normed_two, y_sum, d_sum)
    units_own = [[fc_own_31, fc_own_32], [fc_own_1, fc_own_2]]
    (y_sum, d_sum), (w_3a, w_2a), (b_3a, b_2a) = mlp_step(
        start, carry, grad_top, consts, units_own, parts[0], False, mine, rows, []
    )
    w_3a_came = side(w_3a)

    near = lambda weight: [(w_0, weight, 2), (w_1_came, weight, 2)]
    near_other = lambda weight: [(w_0, 2 + weight, -2), (w_1_came, 2 + weight, -2)]
    sum_of = lambda index, *arrays: [(array, index) for array in arrays]
    by_bit = lambda index, *arrays: [(array, index, 1) for array in arrays]
    by_other = lambda index, *arrays: [(array, index + 1, -1) for array in arrays]
    token = w_3a
    if quick:
        send_2a, token = combine(marks, [near_other(1)], extras=[w_3a])
        came_2a = pair(send_2a)
    carry = (normed_two, y_sum, d_sum)
    units_other = [[fc_other_31, fc_other_32], [fc_other_1, fc_other_2]]
    ends, (w_3b, w_2b), (b_3b, b_2b) = mlp_step(
        start, carry, grad_top, consts, units_other, parts[1], True, mine, rows, [token]
    )
    out_own, out_near, out_far, grad_mixed, grad_attn, two_sums = ends
    column = key_bias[:, None]
    ending = (joined, grad_mixed, norm)

    def back(block, total, last, extras):
        results, ((weights, sums),) = attn_backward(
            normed,
            grad_attn,
            column,
            total,
            [packs[block]],
            [saved[block]],
            mine,
            rows,
            ending if last else None,
            extras,
        )
        return results, weights, sums

    w_3b_came = side(w_3b)
    token = w_3b
    extras = []
    if quick:
        send_1a, token = combine(marks, [sum_of(0, w_2a, w_3a_came)], extras=[w_3b])
        came_1a = link(send_1a)
        extras = [token, came_2a]
    out_came = link(out_far)
    (d_total,), g_1, s_1 = back(1, None, False, extras)
    g_1_came = side(g_1)
    if quick:
        send_1b, send_2b, token = combine(
            marks, [sum_of(0, w_2b, w_3b_came)], [sum_of(1, w_2b, w_3b_came)], extras=[g_1]
        )
        came_1b, came_2b = link(send_1b), pair(send_2b)
        extras = [token, came_1a]
    (d_total,), g_3, s_3 = back(3, d_total, False, extras)
    g_3_came = side(g_3)
    quarters = lambda value: value.reshape(2 * value.shape[0], -1, features)
    quarter = lambda pieces: [(quarters(array), 2 * k, 0, 1) for array, k in pieces]
    quarter_other = lambda pieces: [(quarters(array), 2 * k + 1, 0, -1) for array, k in pieces]
    if quick:
        send_1c, send_2c, keep, token = combine(
            marks,
            [near_other(0) + sum_of(0, came_1b)],
            [sum_of(1, w_2a, w_3a_came) + sum_of(0, came_2b)],
            [near(0) + sum_of(0, came_1a), near(1) + sum_of(0, came_2a)],
            extras=[g_3],
        )
        came_1c, came_2c = pair(send_1c), link(send_2c)
        extras = [token]
    (d_total,), g_2, s_2 = back(2, d_total, False, extras)
    if quick:
        far_a, far_b, token = combine(
            marks,
            [sum_of(0, g_2, g_3_came), sum_of(1, g_2, g_3_came)],
            [by_other(2, g_2, g_3_came)],
        )
        far_a_came, far_b_came = link(far_a), pair(far_b)
        fc_parts = [[(keep, 0), (came_1c, 0)], [(keep, 1), (came_2c, 0)]]
        fc_out, fc_keep, token = combine(
            marks,
            [quarter_other(part) for part in fc_parts],
            [quarter(part) for part in fc_parts],
            extras=[token],
        )
        fc_came = swap(fc_out, "videos", 2)
        extras = [token]
    ends, g_0, s_0 = back(0, d_total, True, extras)
    row_own, row_near, row_far, grad_carried, one_sums = ends

    token = jnp.zeros((8, 128), full)
    if quick:
        attn_out, far_b, attn_keep, token = combine(
            marks,
            [by_other(0, g_0, g_1_came, far_a_came), by_other(2, g_0, g_1_came)],
            [by_bit(2, g_2, g_3_came) + sum_of(0, far_b_came)],
            [by_bit(0, g_0, g_1_came, far_a_came), by_bit(2, g_0, g_1_came)],
        )
        attn_came, far_b_came = pair(attn_out), link(far_b)
        fc_quarter, token = combine(
            marks, [sum_of(0, fc_keep, fc_came), sum_of(1, fc_keep, fc_came)], extras=[token]
        )
        fc_came = swap(fc_quarter, "videos", 4)
    grad_message = lax.all_gather(tie(grad_carried, token), "heads", axis=0, tiled=True)
    msg_stacked, msg_norm_part = message_backward(
        grad_message, msg_saved, msg_qkv, msg_out_w, msg_key, []
    )
    bundle = message_bundle(
        marks,
        msg_norm_part,
        one_sums,
        two_sums,
        [b_0, b_1, b_2a, b_2b, b_3a, b_3b],
        [s_0, s_1, s_2, s_3],
    )
    bundles = lax.all_gather(bundle, "heads")
    by_blocks = lambda value: value.reshape(-1, rows, features)
    rows_out, token = combine(
        marks, [[(by_blocks(row_far), k)] for k in range(2 * mine)], extras=[bundles]
    )
    rows_came = link(rows_out.reshape(row_far.shape))
    if quick:
        attn_parts = [
            [(attn_keep, 0), (attn_came, 0)],
            [(attn_keep, 1), (attn_came, 1), (far_b_came, 0)],
        ]
        attn_out, attn_keep, token = combine(
            marks,
            [quarter_other(part) for part in attn_parts],
            [quarter(part) for part in attn_parts],
            extras=[token],
        )
        attn_came = swap(attn_out, "videos", 2)

    field = -(-width // 128) * 128
    operands, leading_part = message_finish(
        marks,
        bundles,
        grad_message,
        message,
        msg_norm,
        msg_in,
        leading,
        msg_stacked,
        msg_saved,
        msg_fc_w.T,
        field,
        [token],
    )
    operands = operands.astype(low)[None]
    if quick:
        came = pair(operands)
        attn_quarter, token = combine(
            marks,
            [sum_of(0, attn_keep, attn_came), sum_of(1, attn_keep, attn_came)],
            extras=[operands],
        )
        attn_came = swap(attn_quarter, "videos", 4)
        token, came = hold(token, came)
        operands = jnp.concatenate([operands, came], 0)
        came = swap(operands, "videos", 2)
        fc_quarter, token = combine(
            marks,
            [sum_of(0, fc_quarter, fc_came), sum_of(1, fc_quarter, fc_came)],
            extras=[token],
        )
        fc_second, fc_third = swap(fc_quarter, "videos", 2), pair(fc_quarter)
        token, came, leading_part = hold(token, came, leading_part)
        operands = jnp.concatenate([operands, came], 0)
        came = swap(operands, "videos", 4)
    else:
        operands = lax.all_gather(operands, "videos", axis=0, tiled=True)
    leading_grad = jnp.sum(lax.all_gather(leading_part, "heads"), 0)
    out_came, rows_came, leading_grad = hold(out_came, rows_came, leading_grad)
    rows_near = [side(each) for each in (row_near, rows_came[1], out_near, out_came[1])]
    if quick:
        attn_quarter, token = combine(
            marks,
            [sum_of(0, attn_quarter, attn_came), sum_of(1, attn_quarter, attn_came)],
            extras=[leading_grad],
        )
        attn_second, attn_third = swap(attn_quarter, "videos", 2), pair(attn_quarter)
        token, fc_second, came = hold(token, fc_second, came)
        fc_fourth = pair(fc_second)
        operands = jnp.concatenate([operands, came], 0)
    weights = message_weights(
        operands.reshape(-1, operands.shape[2]), features, width, field, videos
    )
    qkv_msg, msg_out_w_grad, fc_msg, msg_qkv_b_grad, all_grad, all_cols, own = weights

    arrange = lambda pieces: jnp.concatenate(by_place(pieces, here), 0)
    mixed_out = arrange([out_own, rows_near[2], out_came[0], rows_near[3]])
    frames_grad = arrange([row_own, rows_near[0], rows_came[0], rows_near[1]]).astype(full)
    owner = (here == 0).astype(full)
    frames_grad = frames_grad.at[:, 0, :].add(leading_grad * owner)
    if quick:
        attn_second, msg_out_w_grad = hold(attn_second, msg_out_w_grad)
        attn_fourth = pair(attn_second)
        fc1_total, fc2_total = spread(
            [fc_quarter, fc_second, fc_third, fc_fourth], marks, False
        )
        qkv_total, out_total = spread(
            [attn_quarter, attn_second, attn_third, attn_fourth], marks, True
        )
    else:
        w_2 = order(jnp.stack([w_2a, w_2b])).reshape(w_0.shape)
        w_3 = order(jnp.stack([w_3a_came, w_3b_came])).reshape(w_0.shape)
        fc_total = add(w_0, w_1_came, link(add(w_2, w_3)))
        attn_total = add(g_0, g_1_came, link(add(g_2, g_3_came)))
        fc_total, attn_total = lax.psum((fc_total, attn_total), "videos")
        fc1_total, fc2_total = [
            fc_total[k::2].reshape(units, features).astype(full) for k in range(2)
        ]
        attn_total = attn_total.astype(full)
        qkv_total, out_total = attn_total[:3].reshape(-1, features), attn_total[3]


    six = own[:6, :width]
    more = own[:4, 256 : 256 + width]
    cut = lambda value: lax.dynamic_slice_in_dim(value, here * width, width, value.ndim - 1)
    turn = lambda value: value.reshape(3, width, features).transpose(0, 2, 1)
    return (
        mixed_out[None],
        frames_grad[None],
        fc_msg.T,
        all_cols[0],
        more[0],
        more[1],
        turn(qkv_msg),
        msg_qkv_b_grad,
        msg_out_w_grad,
        cut(all_grad)[0],
        six[0],
        six[1],
        turn(qkv_total),
        more[2:],
        out_total,
        six[2],
        six[3],
        six[4],
        fc1_total.T,
        own[6:, :half].reshape(units),
        fc2_total,
        six[5],
    )


def solution(mesh):
    placed = (
        P("videos", None, "heads", None),
        P("videos", None, "heads", None),
        P("videos"),
        P("videos"),
        P(None, "heads"),
        P("heads"),
        P(),
        P(),
        P(None, None, "heads"),
        P(None, "heads"),
        P("heads", None),
        P(),
        P(),
        P(),
        P(None, None, "heads"),
        P(None, "heads"),
        P("heads", None),
        P(),
        P(),
        P(),
        P(None, "heads"),
        P("heads"),
        P("heads", None),
        P(),
    )
    return jax.shard_map(
        on_device,
        mesh=mesh,
        in_specs=placed,
        out_specs=(
            P("videos", None, "heads", None),
            P("videos", None, "heads", None),
            P(None, "heads"),
            P("heads"),
            P("heads"),
            P("heads"),
            P(None, None, "heads"),
            P(None, "heads"),
            P("heads", None),
            P("heads"),
            P("heads"),
            P("heads"),
            P(None, None, "heads"),
            P(None, "heads"),
            P("heads", None),
            P("heads"),
            P("heads"),
            P("heads"),
            P(None, "heads"),
            P("heads"),
            P("heads", None),
            P("heads"),
        ),
        check_vma=False,
    )
```

```python
import math

import jax
import jax.numpy as jnp
from jax import lax
from jax.experimental import pallas as pl
from jax.experimental.pallas import tpu as pltpu
from jax.sharding import PartitionSpec as P

HEAD_DIM = 64


epsilon = 1e-05

low = jnp.bfloat16
full = jnp.float32
VMEM_LIMIT = 30 * 1024 * 1024

RATE = 6e9


def norm_forward(value, gains, offset):
    average = jnp.mean(value, -1, keepdims=True)
    centered = value - average
    spread = jnp.mean(centered * centered, -1, keepdims=True)
    inverse = lax.rsqrt(spread + epsilon)
    unit = centered * inverse
    return (unit * gains.astype(jnp.float32) + offset.astype(jnp.float32), unit, inverse)


def norm_backward(gradient, unit, inverse, gains):
    scaled = gradient * gains.astype(jnp.float32)
    average = jnp.mean(scaled, -1, keepdims=True)
    second = jnp.mean(scaled * unit, -1, keepdims=True)
    return inverse * (scaled - average - unit * second)


def split_heads(tensors):
    return tuple(
        (
            tensor.reshape(tensor.shape[:-1] + (tensor.shape[-1] // HEAD_DIM, HEAD_DIM))
            for tensor in tensors
        )
    )


def project(normed, weight, biases):
    stacked = jnp.einsum("...d,cde->c...e", normed, weight, preferred_element_type=jnp.float32)
    return (
        (stacked[0] + biases[0]).astype(jnp.bfloat16),
        stacked[1].astype(jnp.bfloat16),
        (stacked[2] + biases[1]).astype(jnp.bfloat16),
    )


def attend_forward(queries, key_rows, values, keymask):
    scale_factor = HEAD_DIM ** (-0.5)
    scores = (
        jnp.einsum("bqhe,bkhe->bhqk", queries, key_rows, preferred_element_type=jnp.float32)
        * scale_factor
    )
    scores = jnp.where(keymask, scores, -1e30)
    largest = jnp.max(scores, -1, keepdims=True)
    exponent = jnp.exp(scores - largest)
    totals = jnp.sum(exponent, -1, keepdims=True)
    chances = exponent / totals
    output = jnp.einsum(
        "bhqk,bkhe->bqhe", chances.astype(jnp.bfloat16), values, preferred_element_type=jnp.float32
    )
    return (output.astype(jnp.bfloat16), largest + jnp.log(totals))


def attend_backward(queries, key_rows, values, keymask, log_total, grad_heads):
    scale_factor = HEAD_DIM ** (-0.5)
    scores = (
        jnp.einsum("bqhe,bkhe->bhqk", queries, key_rows, preferred_element_type=jnp.float32)
        * scale_factor
    )
    scores = jnp.where(keymask, scores, -1e30)
    chances = jnp.exp(scores - log_total)
    grad_chances = jnp.einsum(
        "bqhe,bkhe->bhqk", grad_heads, values, preferred_element_type=jnp.float32
    )
    deltas = jnp.sum(chances * grad_chances, -1, keepdims=True)
    grad_scores = (chances * (grad_chances - deltas)).astype(jnp.bfloat16)
    grad_query = (
        jnp.einsum("bhqk,bkhe->bqhe", grad_scores, key_rows, preferred_element_type=jnp.float32)
        * scale_factor
    ).astype(jnp.bfloat16)
    grad_key = (
        jnp.einsum("bhqk,bqhe->bkhe", grad_scores, queries, preferred_element_type=jnp.float32)
        * scale_factor
    ).astype(jnp.bfloat16)
    grad_value = jnp.einsum(
        "bhqk,bqhe->bkhe",
        chances.astype(jnp.bfloat16),
        grad_heads,
        preferred_element_type=jnp.float32,
    ).astype(jnp.bfloat16)
    return (grad_query, grad_key, grad_value)


PINNED = True


def dot(left, right, left_dim=1, right_dim=0):
    return lax.dot_general(
        left, right, (((left_dim,), (right_dim,)), ((), ())), preferred_element_type=full
    )


def unit_of(value):
    centered = value - jnp.mean(value, -1, keepdims=True)
    inverse = lax.rsqrt(jnp.mean(centered * centered, -1, keepdims=True) + epsilon)
    return centered * inverse, inverse


def unit_backward(scaled, unit, inverse):
    average = jnp.mean(scaled, -1, keepdims=True)
    second = jnp.mean(scaled * unit, -1, keepdims=True)
    return inverse * (scaled - average - unit * second)


def row_sum(value):
    return jnp.sum(value, 0, keepdims=True)


def lane_mask(width, head):
    lane = lax.broadcasted_iota(jnp.int32, (1, width), 1)
    return (lane >= head * HEAD_DIM) & (lane < (head + 1) * HEAD_DIM)


def call_kernel(body, inputs, outputs, scratch, name, scalars=(), micros=3, loose=None, extras=(), pinned=True):
    def large(shape, dtype):
        if loose == 0 or (len(shape) == 2 and shape[0] == loose):
            return False
        return jnp.dtype(dtype).itemsize * math.prod(shape) > 2**17

    big_in = [pinned and large(each.shape, each.dtype) for each in inputs]
    big_out = [large(*each) for each in outputs]
    count = len(inputs) + len(outputs)

    def kernel(*refs):
        refs = refs[: len(inputs)] + refs[len(inputs) + len(extras) :]
        outer, spare = refs[:count], list(refs[count:])
        queue, coming, going = [], {}, []
        in_marks, out_marks = spare[-2:]
        targets = {}
        for k, ref in enumerate(outer):
            is_input = k < len(inputs)
            n = k if is_input else k - len(inputs)
            if not (big_in[n] if is_input else big_out[n]):
                queue.append(ref)
                continue
            buffer = spare.pop(len(scratch))
            queue.append(buffer)
            if is_input:
                copy = pltpu.make_async_copy(ref, buffer, in_marks.at[n])
                copy.start()
                coming[id(buffer)] = copy
            else:
                targets[id(buffer)] = pltpu.make_async_copy(buffer, ref, out_marks.at[n])
        queue += spare[: len(scratch)]
        handed = list(queue)

        def wait(*each):
            for ref in each:
                copy = coming.pop(id(ref), None)
                if copy is not None:
                    copy.wait()

        def send(*each):
            for ref in each:
                copy = targets.pop(id(ref), None)
                if copy is not None:
                    copy.start()
                    going.append(copy)

        body(lambda k: [queue.pop(0) for _ in range(k)], wait, send)
        wait(*handed)
        send(*handed)
        for copy in going:
            copy.wait()

    def spec(big, k=None):
        if k in scalars:
            return pl.BlockSpec(memory_space=pltpu.SMEM)
        return pl.BlockSpec(memory_space=pltpu.HBM if big else pltpu.VMEM)

    buffers = [pltpu.VMEM(each.shape, each.dtype) for each, big in zip(inputs, big_in) if big]
    buffers += [pltpu.VMEM(*each) for each, big in zip(outputs, big_out) if big]
    marks = [pltpu.SemaphoreType.DMA((len(inputs),)), pltpu.SemaphoreType.DMA((len(outputs),))]
    return list(
        pl.pallas_call(
            kernel,
            out_shape=[jax.ShapeDtypeStruct(*each) for each in outputs],
            in_specs=[spec(big, k) for k, big in enumerate(big_in)]
            + [pl.BlockSpec(memory_space=pl.ANY)] * len(extras),
            out_specs=[spec(big) for big in big_out],
            scratch_shapes=list(scratch) + buffers + marks,
            compiler_params=pltpu.CompilerParams(vmem_limit_bytes=VMEM_LIMIT),
            cost_estimate=pl.CostEstimate(
                flops=int(micros * RATE), bytes_accessed=1024, transcendentals=0
            ),
            name=name,
        )(*inputs, *extras)
    )


def combine(marks, *outputs, extras=()):
    terms = [term for output in outputs for slot in output for term in slot]
    _, rows, features = terms[0][0].shape
    chunk = rows // 2 if rows >= 192 else rows

    def kernel(_, *refs):
        queue = list(refs)
        sums = [
            [sum(queue.pop(0)[0].astype(full) for _ in slot) for slot in output]
            for output in outputs
        ]
        for out, values in zip(queue[len(extras) :], sums):
            for k, value in enumerate(values):
                out[k] = value.astype(low)
        queue[-1][...] = jnp.zeros((8, 128), full)

    def place(_, base, *steps):
        return lambda c, s: (base + sum(step * s[k] for k, step in enumerate(steps) if step), c, 0)

    return pl.pallas_call(
        kernel,
        grid_spec=pltpu.PrefetchScalarGridSpec(
            num_scalar_prefetch=1,
            grid=(rows // chunk,),
            in_specs=[pl.BlockSpec((1, chunk, features), place(*term)) for term in terms]
            + [pl.BlockSpec(memory_space=pl.ANY)] * len(extras),
            out_specs=[
                pl.BlockSpec((len(output), chunk, features), lambda c, s: (0, c, 0))
                for output in outputs
            ]
            + [pl.BlockSpec((8, 128), lambda c, s: (0, 0))],
        ),
        out_shape=[jax.ShapeDtypeStruct((len(each), rows, features), low) for each in outputs]
        + [jax.ShapeDtypeStruct((8, 128), full)],
        compiler_params=pltpu.CompilerParams(vmem_limit_bytes=VMEM_LIMIT),
        cost_estimate=pl.CostEstimate(flops=1024, bytes_accessed=1024, transcendentals=0),
        name="combine",
    )(marks, *[term[0] for term in terms], *extras)


def spread(pieces, marks, split):
    _, rows, features = pieces[0].shape

    def body(take, wait, send):
        (mark_ref,) = take(1)
        piece_refs = take(4)
        first_ref, second_ref = take(2)
        for k, piece in enumerate(piece_refs):
            wait(piece)
            outer, inner = mark_ref[0] ^ (k // 2), mark_ref[1] ^ (k % 2)
            begin = pl.multiple_of((outer * 2 + inner) * rows, 8)
            first_ref[pl.ds(begin, rows)] = piece[0].astype(full)
            if not split:
                second_ref[pl.ds(begin, rows)] = piece[1].astype(full)
            else:

                @pl.when(outer == 0)
                def _(piece=piece, begin=begin):
                    first_ref[pl.ds(4 * rows + begin, rows)] = piece[1].astype(full)

                @pl.when(outer == 1)
                def _(piece=piece, inner=inner):
                    at = pl.ds(pl.multiple_of(inner * rows, 8), rows)
                    second_ref[at] = piece[1].astype(full)

    sizes = (6, 2) if split else (4, 4)
    outputs = [((size * rows, features), full) for size in sizes]
    return call_kernel(body, [marks, *pieces], outputs, [], "spread", (0,), 0.01, 0)


def prepare(marks, qkv, out, extra, fc1, fc2, extras):
    width, features = out.shape
    units = fc2.shape[0]
    half = units // 2
    size = 4 * width + extra.shape[0]

    def body(take, wait, send):
        mark_ref, qkv_ref, out_ref, extra_ref, fc1_ref, fc2_ref = take(6)
        pack_ref, half_ref, fcs_ref, first_ref, second_ref = take(5)
        wait(qkv_ref, out_ref, extra_ref)
        pack_ref[: 3 * width] = qkv_ref[...]
        pack_ref[3 * width : 4 * width] = out_ref[...]
        pack_ref[4 * width :] = extra_ref[...]
        here = mark_ref[0]
        half_ref[...] = pack_ref[pl.ds(pl.multiple_of(here * (size // 2), 16), size // 2)]
        send(pack_ref, half_ref)
        wait(fc1_ref, fc2_ref)
        for k in range(2):
            fcs_ref[2 * k] = fc1_ref[:, k * half : (k + 1) * half].T
            fcs_ref[2 * k + 1] = fc2_ref[k * half : (k + 1) * half]
        first_ref[0] = fcs_ref[2 * here]
        second_ref[0] = fcs_ref[2 * here + 1]

    outputs = [((size, features), low), ((size // 2, features), low)]
    outputs += [((4, half, features), low)] + [((1, half, features), low)] * 2
    inputs = [marks, qkv, out, extra, fc1, fc2]
    return call_kernel(body, inputs, outputs, [], "prepare", (0,), extras=extras)


def message_start(marks, leads, weight, bias, extras):
    slots, _ = leads[0].shape
    width = weight.shape[0]

    def body(take, wait, send):
        (mark_ref,) = take(1)
        lead_refs = take(len(leads))
        weight_ref, bias_ref = take(2)
        lead_ref, part_ref = take(2)
        here = mark_ref[2]
        lead = lead_refs[0][...].astype(full)
        for k in range(1, len(leads)):
            lead = jnp.where(here == k, lead_refs[k][...].astype(full), lead)
        lead_ref[...] = lead
        part_ref[...] = dot(lead.astype(low), weight_ref[...], 1, 1) + bias_ref[...]

    outputs = [(leads[0].shape, full), ((slots, width), full)]
    inputs = [marks, *leads, weight, bias]
    return call_kernel(body, inputs, outputs, [], "message_start", (0,), 0.01, 0, extras)


def message_forward(message, norm, qkv, out, bias, key_row, extras):
    slots, features = message.shape
    width = out.shape[0]

    def body(take, wait, send):
        message_ref, norm_ref, qkv_ref, out_ref, bias_ref, key_ref = take(6)
        normed_ref, saved_ref, part_ref = take(3)
        wait(message_ref, qkv_ref, out_ref)
        unit, _ = unit_of(message_ref[...])
        normed = (unit * norm_ref[0:1] + norm_ref[1:2]).astype(low)
        normed_ref[...] = normed.astype(full)
        query, key, value = [
            dot(normed, qkv_ref[k * width : (k + 1) * width], 1, 1) for k in range(3)
        ]
        query = (query + bias_ref[0:1]).astype(low)
        key = key.astype(low)
        value = (value + bias_ref[1:2]).astype(low)
        result = jnp.zeros((slots, width), full)
        for j in range(width // HEAD_DIM):
            mask = lane_mask(width, j)
            scaled = query.astype(full) * HEAD_DIM ** (-0.5)
            one = jnp.where(mask, scaled, jnp.zeros_like(scaled)).astype(low)
            scores = dot(one, key, 1, 1) + key_ref[...]
            exponent = jnp.exp(scores - jnp.max(scores, -1, keepdims=True))
            chances = exponent / jnp.sum(exponent, -1, keepdims=True)
            result = jnp.where(mask, dot(chances.astype(low), value), result)
        result = result.astype(low)
        for k, each in enumerate((query, key, value, result)):
            saved_ref[k] = each.astype(full)
        part_ref[...] = dot(result, out_ref[...])

    outputs = [((slots, features), full), ((4, slots, width), full), ((slots, features), full)]
    inputs = [message, norm, qkv, out, bias, key_row]
    return call_kernel(body, inputs, outputs, [], "message_forward", (), 0.01, 0, extras)


def message_backward(grad_message, saved, qkv, out, key_row, extras):
    slots, features = grad_message.shape
    width = out.shape[0]

    def body(take, wait, send):
        grad_ref, saved_ref, qkv_ref, out_ref, key_ref = take(5)
        stacked_ref, part_ref = take(2)
        wait(saved_ref, qkv_ref, out_ref)
        grad_o = dot(grad_ref[...].astype(low), out_ref[...], 1, 1).astype(low).astype(full)
        scaled = saved_ref[0] * HEAD_DIM ** (-0.5)
        key, value = saved_ref[1].astype(low), saved_ref[2].astype(low)
        grad_q = grad_k = grad_v = jnp.zeros((slots, width), full)
        for j in range(width // HEAD_DIM):
            mask = lane_mask(width, j)
            one_query = jnp.where(mask, scaled, jnp.zeros_like(scaled)).astype(low)
            one_grad = jnp.where(mask, grad_o, jnp.zeros_like(grad_o)).astype(low)
            scores = dot(one_query, key, 1, 1) + key_ref[...]
            exponent = jnp.exp(scores - jnp.max(scores, -1, keepdims=True))
            chances = exponent / jnp.sum(exponent, -1, keepdims=True)
            grad_p = dot(one_grad, value, 1, 1)
            grad_s = chances * (grad_p - jnp.sum(chances * grad_p, -1, keepdims=True))
            grad_s = grad_s.astype(low)
            grad_v += dot(chances.astype(low), one_grad, 0, 0)
            grad_k += dot(grad_s, one_query, 0, 0)
            grad_q = jnp.where(mask, dot(grad_s, key), grad_q)
        grads = [each.astype(low) for each in (grad_q * HEAD_DIM ** (-0.5), grad_k, grad_v)]
        for k, each in enumerate(grads):
            stacked_ref[k] = each.astype(full)
        part_ref[...] = sum(
            dot(each, qkv_ref[k * width : (k + 1) * width]) for k, each in enumerate(grads)
        )

    outputs = [((3, slots, width), full), ((slots, features), full)]
    inputs = [grad_message, saved, qkv, out, key_row]
    return call_kernel(body, inputs, outputs, [], "message_backward", (), 0.01, 0, extras)


def message_bundle(marks, part, one_sums, two_sums, hidden, heads):
    slots, features = part.shape
    width = heads[0].shape[1]
    half = features // 2

    def body(take, wait, send):
        mark_ref, part_ref, one_ref, two_ref = take(4)
        near_refs, far_refs, head_refs = take(2), take(4), take(4)
        (out_ref,) = take(1)
        out_ref[...] = jnp.zeros(out_ref.shape, full)
        out_ref[:slots] = part_ref[...]
        out_ref[slots : slots + 2] = one_ref[...]
        out_ref[slots + 2 : slots + 6] = two_ref[...]
        bit, here = mark_ref[0], mark_ref[2]
        for k in range(4):
            if k < 2:
                first, second = near_refs[k][0:1], near_refs[k][1:2]
            else:
                own, other = far_refs[2 * k - 4][...], far_refs[2 * k - 3][...]
                first, second = jnp.where(bit == 0, own, other), jnp.where(bit == 0, other, own)
            row = pl.ds(slots + 6 + (here ^ k), 1)
            out_ref[row, :half] = first
            out_ref[row, half:] = second
            row = pl.ds(slots + 10 + (here ^ k), 1)
            out_ref[row, :width] = head_refs[k][0:1]
            out_ref[row, 256 : 256 + width] = head_refs[k][1:2]

    inputs = [marks, part, one_sums, two_sums, *hidden, *heads]
    outputs = [((slots + 16, features), full)]
    return call_kernel(body, inputs, outputs, [], "message_bundle", (0,), 0.01, 0)[0]


def message_finish(marks, bundles, grad_message, message, norm, normed, lead, stacked, saved, weight, field, extras):
    slots, features = message.shape
    width = weight.shape[0]
    groups = features // width

    def body(take, wait, send):
        mark_ref, bundle_ref, grad_ref, message_ref, norm_ref, normed_ref = take(6)
        lead_ref, stacked_ref, saved_ref, weight_ref = take(4)
        out_ref, part_ref = take(2)
        here = mark_ref[2]
        bundle = sum(bundle_ref[k] for k in range(groups))

        def cut(value):
            result = value[:, :width]
            for k in range(1, groups):
                result = jnp.where(here == k, value[:, k * width : (k + 1) * width], result)
            return result

        def own_row(first):
            result = bundle[first : first + 1]
            for k in range(1, groups):
                result = jnp.where(here == k, bundle[first + k : first + k + 1], result)
            return result

        grad_normed = bundle[:slots]
        unit, inverse = unit_of(message_ref[...])
        grad = grad_ref[...]
        columns = cut(grad + unit_backward(grad_normed * norm_ref[0:1], unit, inverse)).astype(low)
        part_ref[...] = dot(columns, weight_ref[...])
        at = 0
        for value in (normed_ref[...], grad, lead_ref[...]):
            out_ref[:, at : at + features] = value
            at += features
        for value in (stacked_ref[0], stacked_ref[1], stacked_ref[2], saved_ref[3], columns):
            out_ref[:, at : at + field] = jnp.zeros((slots, field), full)
            out_ref[:, at : at + width] = value.astype(full)
            at += field
        out_ref[:, at:] = jnp.zeros((slots, 512), full)
        out_ref[0:6, at : at + width] = cut(bundle[slots : slots + 6])
        units, heads = own_row(slots + 6), own_row(slots + 10)
        half = features // 2
        out_ref[6:7, at : at + half] = units[:, :half]
        out_ref[7:8, at : at + half] = units[:, half:]
        side = at + 256
        out_ref[0:1, side : side + width] = cut(row_sum(grad_normed * unit))
        out_ref[1:2, side : side + width] = cut(row_sum(grad_normed))
        out_ref[2:3, side : side + width] = heads[:, :width]
        out_ref[3:4, side : side + width] = heads[:, 256 : 256 + width]

    inputs = [marks, bundles, grad_message, message, norm, normed, lead, stacked, saved, weight]
    outputs = [((slots, 3 * features + 5 * field + 512), full), ((slots, features), full)]
    return call_kernel(body, inputs, outputs, [], "message_finish", (0,), 0.01, 0, extras)


def message_weights(operands, features, width, field, count):
    rows, total = operands.shape
    slots = rows // count
    starts = [k * features for k in range(3)] + [3 * features + k * field for k in range(5)]
    last = 3 * features + 5 * field

    def body(take, wait, send):
        (rows_ref,) = take(1)
        wait(rows_ref)
        qkv_ref, out_ref, fc_ref, heads_ref, grad_ref, cols_ref, own_ref = take(7)
        wide = [rows_ref[:, at : at + features] for at in starts[:3]]
        thin = [rows_ref[:, at : at + width] for at in starts[3:]]
        for k in range(3):
            qkv_ref[k * width : (k + 1) * width] = dot(thin[k], wide[0], 0, 0)
        out_ref[...] = dot(thin[3], wide[1], 0, 0)
        fc_ref[...] = dot(thin[4], wide[2], 0, 0)
        heads_ref[...] = jnp.concatenate(
            [row_sum(thin[0].astype(full)), row_sum(thin[2].astype(full))], 0
        )
        grad_ref[...] = row_sum(wide[1].astype(full))
        cols_ref[...] = row_sum(thin[4].astype(full))
        own = rows_ref[:, last:].astype(full)
        own_ref[...] = sum(own[k * slots : (k + 1) * slots] for k in range(count))

    outputs = [
        ((3 * width, features), full),
        ((width, features), full),
        ((width, features), full),
        ((2, width), full),
        ((1, features), full),
        ((1, width), full),
        ((slots, total - last), full),
    ]
    return call_kernel(body, [operands], outputs, [], "message_weights", (), 3, 0)


def place_rows(target, value_of, mine, span, rows, near_count):
    for f in range(mine):
        for k in range(near_count):
            target[f * span + k * rows : f * span + (k + 1) * rows] = value_of(k, f).astype(full)


def frame_values(marks_ref, own_ref, came_ref, near_ref, mine):
    def value_of(k, f):
        if k == 0:
            return own_ref[marks_ref[2] * mine + f]
        if k == 2:
            return came_ref[(marks_ref[2] % 2) * mine + f]
        return near_ref[(k // 2) * mine + f]

    return value_of


def attn_heads(normed, pack, saved_ref, key_bias, mine):
    rows, _ = normed.shape
    span = rows // mine
    width = saved_ref.shape[2]
    extra = pack[4 * width : 4 * width + 16].astype(full)
    saved_ref[0] = (dot(normed, pack[:width], 1, 1) + extra[0:1, :width]).astype(low)
    saved_ref[1] = dot(normed, pack[width : 2 * width], 1, 1).astype(low)
    saved_ref[2] = (dot(normed, pack[2 * width : 3 * width], 1, 1) + extra[1:2, :width]).astype(low)
    for f in range(mine):
        at = slice(f * span, (f + 1) * span)
        query = saved_ref[0, at] * jnp.asarray(HEAD_DIM ** (-0.5), low)
        key, value = saved_ref[1, at], saved_ref[2, at]
        out = jnp.zeros((span, width), full)
        for j in range(width // HEAD_DIM):
            mask = lane_mask(width, j)
            scores = dot(jnp.where(mask, query, jnp.zeros_like(query)), key, 1, 1)
            scores = scores + key_bias
            exponent = jnp.exp(scores - jnp.max(scores, -1, keepdims=True))
            share = 1.0 / jnp.sum(exponent, -1, keepdims=True)
            out = jnp.where(mask, dot(exponent.astype(low), value) * share, out)
        saved_ref[3, at] = out.astype(low)
    return dot(saved_ref[3], pack[3 * width : 4 * width])


def attn_start(marks, frames, came, near, carried, norm, key_row, packs, mine, span, extras):
    _, rows, features = frames.shape
    width = features // 4
    groups = 4
    all_rows = groups * rows
    count = len(packs)

    def body(take, wait, send):
        marks_ref, own_ref, came_ref, near_ref, carried_ref, norm_ref, key_ref = take(7)
        pack_refs = take(count)
        joined_ref, normed_ref, total_ref, token_ref = take(4)
        saved_refs = take(count)
        token_ref[...] = jnp.zeros((8, 128), full)
        (joined,) = take(1)
        wait(own_ref, came_ref, near_ref)
        for f in range(mine):
            end = (f + 1) * span
            joined[f * span + all_rows : end] = jnp.zeros((span - all_rows, features), full)
            joined[f * span + all_rows : f * span + all_rows + 1] = carried_ref[f : f + 1]
        value_of = frame_values(marks_ref, own_ref, came_ref, near_ref, mine)
        place_rows(joined, value_of, mine, span, rows, groups)
        joined_ref[...] = joined[...].astype(low)
        unit, _ = unit_of(joined_ref[...].astype(full))
        normed_ref[...] = (unit * norm_ref[0:1] + norm_ref[1:2]).astype(low)
        send(joined_ref, normed_ref)
        for b in range(count):
            wait(pack_refs[b])
            part = attn_heads(normed_ref[...], pack_refs[b], saved_refs[b], key_ref[...], mine)
            send(saved_refs[b])
            total_ref[...] = total_ref[...] + part if b else part

    size = mine * span
    inputs = [marks, frames, came, near, carried, norm, key_row, *packs]
    outputs = [((size, features), low)] * 2 + [((size, features), full), ((8, 128), full)]
    outputs += [((4, size, width), low)] * count
    scratch = [pltpu.VMEM((size, features), full)]
    results = call_kernel(body, inputs, outputs, scratch, "attn_start", (0,), 9, size, extras)
    return results[:4], results[4:]


def attn_rest(marks, normed, total, key_row, halves, mine, extras):
    rows, features = normed.shape
    width = features // 4
    count = len(halves)

    def body(take, wait, send):
        marks_ref, normed_ref, total_in, key_ref = take(4)
        half_refs = [take(2) for _ in range(count)]
        total_ref, token_ref = take(2)
        pack_refs, saved_refs = take(count), take(count)
        token_ref[...] = jnp.zeros((8, 128), full)
        here = marks_ref[0]
        wait(normed_ref)
        for b in range(count):
            wait(*half_refs[b])
            size = half_refs[b][0].shape[0]
            for k, each in enumerate(half_refs[b]):
                pack_refs[b][pl.ds(pl.multiple_of((here ^ k) * size, 16), size)] = each[...]
            send(pack_refs[b])
            part = attn_heads(normed_ref[...], pack_refs[b], saved_refs[b], key_ref[...], mine)
            send(saved_refs[b])
            wait(total_in)
            total_ref[...] = (total_ref if b else total_in)[...] + part

    inputs = [marks, normed, total, key_row] + [each for pair in halves for each in pair]
    outputs = [((rows, features), full), ((8, 128), full)]
    outputs += [((2 * own.shape[0], features), low) for own, _ in halves]
    outputs += [((4, rows, width), low)] * count
    results = call_kernel(body, inputs, outputs, [], "attn_rest", (0,), 9, rows, extras)
    return results[:2], results[2 : 2 + count], results[2 + count :]


def out_blocks(own_ref, near_ref, far_ref, source, mine, span):
    rows = own_ref.shape[1]
    for f in range(mine):
        for k in range(4):
            value = source[f * span + k * rows : f * span + (k + 1) * rows].astype(low)
            if k < 2:
                (near_ref if k else own_ref)[f] = value
            else:
                far_ref[k - 2, f] = value


def mlp_step(start, carry, grad, consts, weights, biases, last, mine, rows, extras):
    first = carry is None
    total_rows, features = start[0].shape
    span = total_rows // mine
    size = biases[0].shape[1]
    count = len(weights)
    lengths = [[each.shape[0] for each in group] for group in weights]

    def body(take, wait, send):
        if first or last:
            joined_ref, total_ref, const_ref = take(3)
        if first:
            grad_sources = take(4)
        else:
            normed_ref, y_in, d_in, grad_ref = take(4)
        fc_bases = [take(len(group)) for group in lengths]
        fc_refs = [
            [ref.at[k] for ref, n in zip(refs, group) for k in range(n)]
            for refs, group in zip(fc_bases, lengths)
        ]
        bias_refs = take(count)
        if last:
            own_ref, near_ref, far_ref, mixed_ref, attn_ref, sums_ref = take(6)
        else:
            y_ref, d_ref = take(2)
        if first:
            normed_ref, grad_ref = take(2)
        w_refs, b_refs = take(count), take(count)
        if last:
            y_ref, d_ref = take(2)

        def mixed():
            return joined_ref[...].astype(full) + total_ref[...] + const_ref[0:1]

        if first:
            wait(*grad_sources)
            for f in range(mine):
                end = (f + 1) * span
                d_ref[f * span + 4 * rows : end] = jnp.zeros((span - 4 * rows, features), full)
            place_rows(d_ref, frame_values(*grad_sources, mine), mine, span, rows, 4)
            grad_ref[...] = d_ref[...].astype(low)
            wait(joined_ref, total_ref)
            unit, _ = unit_of(mixed())
            normed_ref[...] = (unit * const_ref[1:2] + const_ref[2:3]).astype(low)
            send(grad_ref, normed_ref)
        else:
            wait(normed_ref, grad_ref)
        normed = normed_ref[...]
        grad_rows = grad_ref[...]
        fresh = True
        for b in range(count):
            wait(*fc_bases[b])
            for c in range(len(fc_refs[b]) // 2):
                fc1, fc2 = fc_refs[b][2 * c][...], fc_refs[b][2 * c + 1][...]
                pre = dot(normed, fc1, 1, 1) + bias_refs[b][c : c + 1]
                gate = jax.nn.sigmoid(1.702 * pre)
                active = (pre * gate).astype(low)
                back = dot(grad_rows, fc2, 1, 1) * (gate + 1.702 * pre * gate * (1.0 - gate))
                back = back.astype(low)
                b_refs[b][c : c + 1] = row_sum(back.astype(full))
                y_part = dot(active, fc2)
                d_part = dot(back, fc1)
                if not fresh:
                    y_ref[...] += y_part
                    d_ref[...] += d_part
                elif first:
                    y_ref[...] = y_part
                    d_ref[...] = d_part
                else:
                    wait(y_in, d_in)
                    y_ref[...] = y_in[...] + y_part
                    d_ref[...] = d_in[...] + d_part
                fresh = False
                w_refs[b][2 * c] = dot(back, normed, 0, 0).astype(low)
                w_refs[b][2 * c + 1] = dot(active, grad_rows, 0, 0).astype(low)
            send(w_refs[b])
        if last:
            wait(joined_ref, total_ref)
            value = mixed()
            unit, inverse = unit_of(value)
            y_ref[...] = value + y_ref[...] + const_ref[3:4]
            out_blocks(own_ref, near_ref, far_ref, y_ref, mine, span)
            send(far_ref, near_ref, own_ref)
            grad_normed = d_ref[...]
            top = grad_rows.astype(full)
            grad_mixed = top + unit_backward(grad_normed * const_ref[1:2], unit, inverse)
            mixed_ref[...] = grad_mixed
            grad_attn = grad_mixed.astype(low)
            attn_ref[...] = grad_attn
            sums_ref[...] = jnp.concatenate(
                [
                    row_sum(grad_attn.astype(full)),
                    row_sum(grad_normed * unit),
                    row_sum(grad_normed),
                    row_sum(top),
                ],
                0,
            )

    big = ((total_rows, features), full)
    small = ((total_rows, features), low)
    inputs = [*start, consts] if first or last else []
    inputs += list(grad) if first else [*carry, grad]
    scalars = (3,) if first else ()
    inputs += [each for group in weights for each in group] + list(biases)
    if last:
        outputs = [((mine, rows, features), low)] * 2 + [((2, mine, rows, features), low)]
        outputs += [big, small, ((4, features), full)]
    else:
        outputs = [big, big]
    outputs += [small, small] if first else []
    lead = len(outputs)
    outputs += [((sum(group), size, features), low) for group in lengths]
    outputs += [(each.shape, full) for each in biases]
    scratch = [pltpu.VMEM((total_rows, features), full)] * 2 if last else []
    results = call_kernel(body, inputs, outputs, scratch, "mlp_step", scalars, 12, total_rows, extras, PINNED)
    return results[:lead], results[lead : lead + count], results[lead + count :]


def attn_backward(normed, grad, key_column, total, packs, saved, mine, frame_rows, ending, extras):
    rows, features = normed.shape
    span = rows // mine
    width = features // 4
    count = len(packs)
    first = total is None
    last = ending is not None

    def body(take, wait, send):
        normed_ref, grad_ref, key_ref = take(3)
        if not first:
            (total_in,) = take(1)
        if last:
            joined_ref, mixed_ref, norm_ref = take(3)
        pack_refs = take(count)
        saved_refs = take(count)
        q_refs, k_refs, v_refs, o_refs = [[each.at[k] for each in saved_refs] for k in range(4)]
        if last:
            own_ref, near_ref, far_ref, carried_ref, sums_ref = take(5)
        else:
            (total_ref,) = take(1)
        w_refs, b_refs = take(count), take(count)
        dq_ref, dk_ref, dv_ref, do_ref = take(4)
        if last:
            (total_ref,) = take(1)
        wait(normed_ref, grad_ref, key_ref)
        normed = normed_ref[...]
        grad = grad_ref[...]
        key_bias = key_ref[...]
        scale = HEAD_DIM ** (-0.5)
        for b in range(count):
            pack = pack_refs[b]
            wait(pack, saved_refs[b])
            do_ref[...] = dot(grad, pack[3 * width : 4 * width], 1, 1).astype(low)
            for f in range(mine):
                at = slice(f * span, (f + 1) * span)
                query = q_refs[b][at] * jnp.asarray(scale, low)
                key, value, grad_o = k_refs[b][at], v_refs[b][at], do_ref[at]
                grad_q = grad_k = grad_v = jnp.zeros((span, width), full)
                for j in range(width // HEAD_DIM):
                    mask = lane_mask(width, j)
                    one_query = jnp.where(mask, query, jnp.zeros_like(query))
                    one_grad = jnp.where(mask, grad_o, jnp.zeros_like(grad_o))
                    scores = dot(key, one_query, 1, 1) + key_bias
                    exponent = jnp.exp(scores - jnp.max(scores, 0, keepdims=True))
                    chances = exponent * (1.0 / row_sum(exponent))
                    grad_p = dot(value, one_grad, 1, 1)
                    grad_s = (chances * (grad_p - row_sum(chances * grad_p))).astype(low)
                    grad_v += dot(chances.astype(low), one_grad)
                    grad_k += dot(grad_s, one_query)
                    grad_q = jnp.where(mask, dot(grad_s, key, 0, 0), grad_q)
                dq_ref[at] = (grad_q * scale).astype(low)
                dk_ref[at] = grad_k.astype(low)
                dv_ref[at] = grad_v.astype(low)
            grads = (dq_ref[...], dk_ref[...], dv_ref[...])
            part = sum(dot(each, pack[k * width : (k + 1) * width]) for k, each in enumerate(grads))
            if b:
                total_ref[...] += part
            else:
                if not first:
                    wait(total_in)
                total_ref[...] = part if first else total_in[...] + part
            for k, each in enumerate(grads):
                w_refs[b][k] = dot(each, normed, 0, 0).astype(low)
            w_refs[b][3] = dot(o_refs[b][...], grad, 0, 0).astype(low)
            send(w_refs[b])
            b_refs[b][...] = jnp.concatenate(
                [row_sum(grads[0].astype(full)), row_sum(grads[2].astype(full))], 0
            )
        if last:
            wait(joined_ref, mixed_ref)
            unit, inverse = unit_of(joined_ref[...].astype(full))
            grad_normed = total_ref[...]
            grad_joined = unit_backward(grad_normed * norm_ref[0:1], unit, inverse)
            total_ref[...] = mixed_ref[...] + grad_joined
            all_rows = 4 * frame_rows
            for f in range(mine):
                at = f * span + all_rows
                carried_ref[f : f + 1] = total_ref[at : at + 1]
            out_blocks(own_ref, near_ref, far_ref, total_ref, mine, span)
            send(far_ref, near_ref, own_ref)
            sums_ref[...] = jnp.concatenate(
                [row_sum(grad_normed * unit), row_sum(grad_normed)], 0
            )

    inputs = [normed, grad, key_column] + ([] if first else [total]) + list(ending or ())
    inputs += [*packs, *saved]
    if last:
        outputs = [((mine, frame_rows, features), low)] * 2
        outputs += [((2, mine, frame_rows, features), low)]
        outputs += [((mine, features), full), ((2, features), full)]
    else:
        outputs = [((rows, features), full)]
    lead = len(outputs)
    outputs += [((4, width, features), low)] * count + [((2, width), full)] * count
    scratch = [pltpu.VMEM((rows, width), low)] * 4
    scratch += [pltpu.VMEM((rows, features), full)] if last else []
    results = call_kernel(body, inputs, outputs, scratch, "attn_backward", (), 9, rows, extras)
    grads = [(results[lead + b], results[lead + count + b]) for b in range(count)]
    return results[:lead], grads


def swap(value, axis, offset):
    size = lax.axis_size(axis)
    return lax.ppermute(value, axis, [(place, place ^ offset) for place in range(size)])


def pick(value, index, count, dimension=0):
    return lax.dynamic_slice_in_dim(value, index * count, count, dimension)


def add(*values):
    return sum(value.astype(full) for value in values).astype(low)


def hold(*values):
    return lax.optimization_barrier(values)


def tie(value, token):
    return value + token[:1, :1]


def everyone(value):
    size = lax.axis_size("heads")
    return [value] + [swap(value, "heads", k) for k in range(1, size)]


def by_place(pieces, here):
    stacked = jnp.stack(pieces)
    return [lax.dynamic_index_in_dim(stacked, here ^ k, 0, False) for k in range(len(pieces))]


def frame_pieces(frames, here, groups):
    mine = frames.shape[0] // groups
    return [pick(frames, here ^ k, mine) for k in range(groups)]


def send_each(pieces):
    return [swap(piece, "heads", k) if k else piece for k, piece in enumerate(pieces)]


def on_device(
    frames,
    out_grad,
    frame_tokens,
    frame_count,
    msg_fc_w,
    msg_fc_b,
    msg_norm_g,
    msg_norm_b,
    msg_qkv_w,
    msg_qkv_b,
    msg_out_w,
    msg_out_b,
    norm1_g,
    norm1_b,
    attn_qkv_w,
    attn_qkv_b,
    attn_out_w,
    attn_out_b,
    norm2_g,
    norm2_b,
    fc1_w,
    fc1_b,
    fc2_w,
    fc2_b,
):
    _, slots, rows, features = frames.shape
    groups = lax.axis_size("heads")
    videos = lax.axis_size("videos")
    here = lax.axis_index("heads")
    video = lax.axis_index("videos")
    bit = video % 2
    far = groups // 2
    mine = slots // groups
    span = -(-(rows * groups + 1) // 16) * 16
    tail = span - rows * groups
    width = msg_fc_w.shape[1]
    units = fc1_w.shape[1]
    half = units // 2
    quick = videos == 8
    pair_bit = (video // 2) % 2
    frames = frames[0]
    out_grad = out_grad[0]
    marks = [bit, pair_bit, here, here ^ 1, here % 2, (here // 2) ^ 1]
    marks = jnp.stack(marks).astype(jnp.int32)
    stack = lambda *vectors: jnp.stack(vectors).astype(full)
    link = lambda value: swap(value, "heads", far)
    side = lambda value: swap(value, "heads", 1)
    pair = lambda value: swap(value, "videos", 1)
    two = range(mine)
    far_rows = lambda value: [[(value, k, 0, 0, 0, 0, 0, far * mine)] for k in range(far * mine)]
    near_rows = lambda value, came: [[(value, k, 0, 0, 0, mine)] for k in two] + [
        [(came, mine + k, 0, 0, 0, 0, -mine)] for k in two
    ]

    leads = everyone(frames[:, 0, :])
    row_send, _ = combine(marks, [each for each in far_rows(frames)])
    row_came = link(row_send)
    leading, fc_part = message_start(
        marks, leads, msg_fc_w.T, msg_fc_b[None].astype(full), [row_send]
    )
    columns = everyone(fc_part)
    wide = lambda value: jnp.pad(value, ((0, 0), (0, features - value.shape[1])))
    extra = jnp.concatenate(
        [wide(attn_qkv_b), wide(fc1_b[None]), jnp.zeros((29, features), low)], 0
    )
    pack, pack_send, fcs, fc_send_1, fc_send_2 = prepare(
        marks,
        attn_qkv_w.transpose(0, 2, 1).reshape(3 * width, features),
        attn_out_w,
        extra,
        fc1_w,
        fc2_w,
        [fc_part],
    )
    pack_own = link(pack_send)
    message = jnp.concatenate(by_place(columns, here), 1)
    msg_norm = stack(msg_norm_g, msg_norm_b)
    msg_key = jnp.where(jnp.arange(slots) < frame_count[0], 0.0, -1e30).astype(full)[None]
    msg_qkv = msg_qkv_w.transpose(0, 2, 1).reshape(3 * width, features)
    msg_in, msg_saved, msg_part = message_forward(
        message, msg_norm, msg_qkv, msg_out_w, msg_qkv_b.astype(full), msg_key, [pack_send]
    )
    msg_pieces = frame_pieces(msg_part, here, groups)
    msg_rows = send_each(msg_pieces)
    row_next, token = combine(marks, near_rows(frames, row_came), extras=msg_pieces)
    row_near = side(row_next)
    pack_near = side(pack)
    grad_send, token = combine(marks, far_rows(out_grad), extras=[token])
    carried = tie(pick(message + msg_out_b, here, mine) + sum(msg_rows), token)

    places = jnp.concatenate([(here ^ k) * rows + jnp.arange(rows) for k in range(groups)])
    seen = jnp.concatenate([places < frame_tokens[0], jnp.arange(tail) == 0])
    key_bias = jnp.where(seen, 0.0, -1e30).astype(full)
    norm = stack(norm1_g, norm1_b)
    pack_own, carried = hold(pack_own, carried)
    pack_other, pack_own_3 = pair(pack_own), side(pack_own)
    grad_came = link(grad_send)
    (joined, normed, total, token), saved = attn_start(
        marks,
        frames,
        row_came,
        row_near,
        carried,
        norm,
        key_bias[None],
        [pack, pack_near],
        mine,
        span,
        [pack_own],
    )
    fc_own_1 = link(fc_send_1)
    token, pack_other = hold(token, pack_other)
    pack_other_3 = side(pack_other)
    grad_next, _ = combine(marks, near_rows(out_grad, grad_came), extras=[token])
    grad_near = side(grad_next)
    fc_near = side(fcs)
    halves = [(pack_own, pack_other), (pack_own_3, pack_other_3)]
    (total, token), far_packs, rest = attn_rest(
        marks, normed, total, key_bias[None], halves, mine, [grad_next]
    )
    saved += rest
    packs = [pack, pack_near, *far_packs]
    token, fc_own_1 = hold(token, fc_own_1)
    fc_own_2, fc_other_1, fc_own_31 = link(fc_send_2), pair(fc_own_1), side(fc_own_1)

    consts = stack(attn_out_b, norm2_g, norm2_b, fc2_b)
    bias = [each[4 * width + 2].reshape(2, half).astype(full) for each in packs]
    order = lambda value: jnp.concatenate([pick(value, bit, 1), pick(value, 1 - bit, 1)], 0)
    bias = bias[:2] + [order(each) for each in bias[2:]]
    parts = [[each[:1] for each in bias[:1:-1]], [each[1:] for each in bias[:1:-1]]]
    start = (joined, total)
    sources = (marks, out_grad, grad_came, grad_near)
    (y_sum, d_sum, normed_two, grad_top), (w_0,), (b_0,) = mlp_step(
        start, None, sources, consts, [[fcs]], bias[:1], False, mine, rows, [token]
    )
    b_0, fc_own_2, fc_other_1 = hold(b_0, fc_own_2, fc_other_1)
    fc_other_2, fc_own_32 = pair(fc_own_2), side(fc_own_2)
    fc_other_31 = side(fc_other_1)
    carry = (normed_two, y_sum, d_sum)
    (y_sum, d_sum), (w_1,), (b_1,) = mlp_step(
        start, carry, grad_top, consts, [[fc_near]], bias[1:2], False, mine, rows, []
    )
    b_1, parts[0][0], fc_other_2 = hold(b_1, parts[0][0], fc_other_2)
    fc_other_32, w_1_came = side(fc_other_2), side(w_1)
    carry = (normed_two, y_sum, d_sum)
    units_own = [[fc_own_31, fc_own_32], [fc_own_1, fc_own_2]]
    (y_sum, d_sum), (w_3a, w_2a), (b_3a, b_2a) = mlp_step(
        start, carry, grad_top, consts, units_own, parts[0], False, mine, rows, []
    )
    w_3a_came = side(w_3a)

    near = lambda weight: [(w_0, weight, 2), (w_1_came, weight, 2)]
    near_other = lambda weight: [(w_0, 2 + weight, -2), (w_1_came, 2 + weight, -2)]
    sum_of = lambda index, *arrays: [(array, index) for array in arrays]
    by_bit = lambda index, *arrays: [(array, index, 1) for array in arrays]
    by_other = lambda index, *arrays: [(array, index + 1, -1) for array in arrays]
    token = w_3a
    if quick:
        send_2a, token = combine(marks, [near_other(1)], extras=[w_3a])
        came_2a = pair(send_2a)
    carry = (normed_two, y_sum, d_sum)
    units_other = [[fc_other_31, fc_other_32], [fc_other_1, fc_other_2]]
    ends, (w_3b, w_2b), (b_3b, b_2b) = mlp_step(
        start, carry, grad_top, consts, units_other, parts[1], True, mine, rows, [token]
    )
    out_own, out_near, out_far, grad_mixed, grad_attn, two_sums = ends
    column = key_bias[:, None]
    ending = (joined, grad_mixed, norm)

    def back(block, total, last, extras):
        results, ((weights, sums),) = attn_backward(
            normed,
            grad_attn,
            column,
            total,
            [packs[block]],
            [saved[block]],
            mine,
            rows,
            ending if last else None,
            extras,
        )
        return results, weights, sums

    w_3b_came = side(w_3b)
    token = w_3b
    extras = []
    if quick:
        send_1a, token = combine(marks, [sum_of(0, w_2a, w_3a_came)], extras=[w_3b])
        came_1a = link(send_1a)
        extras = [token, came_2a]
    (d_total,), g_1, s_1 = back(1, None, False, extras)
    g_1_came = side(g_1)
    if quick:
        send_1b, send_2b, token = combine(
            marks, [sum_of(0, w_2b, w_3b_came)], [sum_of(1, w_2b, w_3b_came)], extras=[g_1]
        )
        came_1b, came_2b = link(send_1b), pair(send_2b)
        extras = [token, came_1a]
    (d_total,), g_3, s_3 = back(3, d_total, False, extras)
    g_3_came = side(g_3)
    quarters = lambda value: value.reshape(2 * value.shape[0], -1, features)
    quarter = lambda pieces: [(quarters(array), 2 * k, 0, 1) for array, k in pieces]
    quarter_other = lambda pieces: [(quarters(array), 2 * k + 1, 0, -1) for array, k in pieces]
    if quick:
        send_1c, send_2c, keep, token = combine(
            marks,
            [near_other(0) + sum_of(0, came_1b)],
            [sum_of(1, w_2a, w_3a_came) + sum_of(0, came_2b)],
            [near(0) + sum_of(0, came_1a), near(1) + sum_of(0, came_2a)],
            extras=[g_3],
        )
        came_1c, came_2c = pair(send_1c), link(send_2c)
        extras = [token]
    (d_total,), g_2, s_2 = back(2, d_total, False, extras)
    if quick:
        far_a, far_b, token = combine(
            marks,
            [sum_of(0, g_2, g_3_came), sum_of(1, g_2, g_3_came)],
            [by_other(2, g_2, g_3_came)],
        )
        far_a_came, far_b_came = link(far_a), pair(far_b)
        extras = [token]
    by_blocks = lambda value: value.reshape(-1, rows, features)
    out_send, token = combine(
        marks, [[(by_blocks(out_far), k)] for k in range(2 * mine)], extras=[g_2, *extras]
    )
    out_came = link(out_send.reshape(out_far.shape))
    extras = [token]
    if quick:
        fc_parts = [[(keep, 0), (came_1c, 0)], [(keep, 1), (came_2c, 0)]]
        fc_out, fc_keep, token = combine(
            marks,
            [quarter_other(part) for part in fc_parts],
            [quarter(part) for part in fc_parts],
            extras=[token],
        )
        fc_came = swap(fc_out, "videos", 2)
        extras = [token]
    ends, g_0, s_0 = back(0, d_total, True, extras)
    row_own, row_near, row_far, grad_carried, one_sums = ends

    token = jnp.zeros((8, 128), full)
    if quick:
        attn_out, far_b, attn_keep, token = combine(
            marks,
            [by_other(0, g_0, g_1_came, far_a_came), by_other(2, g_0, g_1_came)],
            [by_bit(2, g_2, g_3_came) + sum_of(0, far_b_came)],
            [by_bit(0, g_0, g_1_came, far_a_came), by_bit(2, g_0, g_1_came)],
        )
        attn_came, far_b_came = pair(attn_out), link(far_b)
        fc_quarter, token = combine(
            marks, [sum_of(0, fc_keep, fc_came), sum_of(1, fc_keep, fc_came)], extras=[token]
        )
        fc_came = swap(fc_quarter, "videos", 4)
    grad_message = lax.all_gather(tie(grad_carried, token), "heads", axis=0, tiled=True)
    msg_stacked, msg_norm_part = message_backward(
        grad_message, msg_saved, msg_qkv, msg_out_w, msg_key, []
    )
    bundle = message_bundle(
        marks,
        msg_norm_part,
        one_sums,
        two_sums,
        [b_0, b_1, b_2a, b_2b, b_3a, b_3b],
        [s_0, s_1, s_2, s_3],
    )
    bundles = lax.all_gather(bundle, "heads")
    rows_out, token = combine(
        marks, [[(by_blocks(row_far), k)] for k in range(2 * mine)], extras=[bundles]
    )
    rows_came = link(rows_out.reshape(row_far.shape))
    if quick:
        attn_parts = [
            [(attn_keep, 0), (attn_came, 0)],
            [(attn_keep, 1), (attn_came, 1), (far_b_came, 0)],
        ]
        attn_out, attn_keep, token = combine(
            marks,
            [quarter_other(part) for part in attn_parts],
            [quarter(part) for part in attn_parts],
            extras=[token],
        )
        attn_came = swap(attn_out, "videos", 2)

    field = -(-width // 128) * 128
    operands, leading_part = message_finish(
        marks,
        bundles,
        grad_message,
        message,
        msg_norm,
        msg_in,
        leading,
        msg_stacked,
        msg_saved,
        msg_fc_w.T,
        field,
        [token],
    )
    operands = operands.astype(low)[None]
    if quick:
        came = pair(operands)
        attn_quarter, token = combine(
            marks,
            [sum_of(0, attn_keep, attn_came), sum_of(1, attn_keep, attn_came)],
            extras=[operands],
        )
        attn_came = swap(attn_quarter, "videos", 4)
        fc_quarter, token = combine(
            marks,
            [sum_of(0, fc_quarter, fc_came), sum_of(1, fc_quarter, fc_came)],
            extras=[token],
        )
        fc_second, fc_third = swap(fc_quarter, "videos", 2), pair(fc_quarter)
        token, came = hold(token, came)
        operands = jnp.concatenate([operands, came], 0)
        came = swap(operands, "videos", 2)
        token, came, leading_part, fc_second, fc_third = hold(
            token, came, leading_part, fc_second, fc_third
        )
        fc_fourth = pair(fc_second)
        operands = jnp.concatenate([operands, came], 0)
        came = swap(operands, "videos", 4)
    else:
        operands = lax.all_gather(operands, "videos", axis=0, tiled=True)
    leading_grad = jnp.sum(lax.all_gather(leading_part, "heads"), 0)
    out_came, rows_came, leading_grad = hold(out_came, rows_came, leading_grad)
    rows_near = [side(each) for each in (row_near, rows_came[1], out_near, out_came[1])]
    if quick:
        attn_quarter, token = combine(
            marks,
            [sum_of(0, attn_quarter, attn_came), sum_of(1, attn_quarter, attn_came)],
            extras=[leading_grad],
        )
        attn_second, attn_third = swap(attn_quarter, "videos", 2), pair(attn_quarter)
        token, came, fc_fourth = hold(token, came, fc_fourth)
        operands = jnp.concatenate([operands, came], 0)
    weights = message_weights(
        operands.reshape(-1, operands.shape[2]), features, width, field, videos
    )
    qkv_msg, msg_out_w_grad, fc_msg, msg_qkv_b_grad, all_grad, all_cols, own = weights

    arrange = lambda pieces: jnp.concatenate(by_place(pieces, here), 0)
    mixed_out = arrange([out_own, rows_near[2], out_came[0], rows_near[3]])
    frames_grad = arrange([row_own, rows_near[0], rows_came[0], rows_near[1]]).astype(full)
    owner = (here == 0).astype(full)
    frames_grad = frames_grad.at[:, 0, :].add(leading_grad * owner)
    if quick:
        attn_second, msg_out_w_grad = hold(attn_second, msg_out_w_grad)
        attn_fourth = pair(attn_second)
        fc1_total, fc2_total = spread(
            [fc_quarter, fc_second, fc_third, fc_fourth], marks, False
        )
        qkv_total, out_total = spread(
            [attn_quarter, attn_second, attn_third, attn_fourth], marks, True
        )
    else:
        w_2 = order(jnp.stack([w_2a, w_2b])).reshape(w_0.shape)
        w_3 = order(jnp.stack([w_3a_came, w_3b_came])).reshape(w_0.shape)
        fc_total = add(w_0, w_1_came, link(add(w_2, w_3)))
        attn_total = add(g_0, g_1_came, link(add(g_2, g_3_came)))
        fc_total, attn_total = lax.psum((fc_total, attn_total), "videos")
        fc1_total, fc2_total = [
            fc_total[k::2].reshape(units, features).astype(full) for k in range(2)
        ]
        attn_total = attn_total.astype(full)
        qkv_total, out_total = attn_total[:3].reshape(-1, features), attn_total[3]


    six = own[:6, :width]
    more = own[:4, 256 : 256 + width]
    cut = lambda value: lax.dynamic_slice_in_dim(value, here * width, width, value.ndim - 1)
    turn = lambda value: value.reshape(3, width, features).transpose(0, 2, 1)
    return (
        mixed_out[None],
        frames_grad[None],
        fc_msg.T,
        all_cols[0],
        more[0],
        more[1],
        turn(qkv_msg),
        msg_qkv_b_grad,
        msg_out_w_grad,
        cut(all_grad)[0],
        six[0],
        six[1],
        turn(qkv_total),
        more[2:],
        out_total,
        six[2],
        six[3],
        six[4],
        fc1_total.T,
        own[6:, :half].reshape(units),
        fc2_total,
        six[5],
    )


def solution(mesh):
    placed = (
        P("videos", None, "heads", None),
        P("videos", None, "heads", None),
        P("videos"),
        P("videos"),
        P(None, "heads"),
        P("heads"),
        P(),
        P(),
        P(None, None, "heads"),
        P(None, "heads"),
        P("heads", None),
        P(),
        P(),
        P(),
        P(None, None, "heads"),
        P(None, "heads"),
        P("heads", None),
        P(),
        P(),
        P(),
        P(None, "heads"),
        P("heads"),
        P("heads", None),
        P(),
    )
    return jax.shard_map(
        on_device,
        mesh=mesh,
        in_specs=placed,
        out_specs=(
            P("videos", None, "heads", None),
            P("videos", None, "heads", None),
            P(None, "heads"),
            P("heads"),
            P("heads"),
            P("heads"),
            P(None, None, "heads"),
            P(None, "heads"),
            P("heads", None),
            P("heads"),
            P("heads"),
            P("heads"),
            P(None, None, "heads"),
            P(None, "heads"),
            P("heads", None),
            P("heads"),
            P("heads"),
            P("heads"),
            P(None, "heads"),
            P("heads"),
            P("heads", None),
            P("heads"),
        ),
        check_vma=False,
    )
```

```python
import math

import jax
import jax.numpy as jnp
from jax import lax
from jax.experimental import pallas as pl
from jax.experimental.pallas import tpu as pltpu
from jax.sharding import PartitionSpec as P

HEAD_DIM = 64


epsilon = 1e-05

low = jnp.bfloat16
full = jnp.float32
VMEM_LIMIT = 30 * 1024 * 1024

RATE = 6e9


def norm_forward(value, gains, offset):
    average = jnp.mean(value, -1, keepdims=True)
    centered = value - average
    spread = jnp.mean(centered * centered, -1, keepdims=True)
    inverse = lax.rsqrt(spread + epsilon)
    unit = centered * inverse
    return (unit * gains.astype(jnp.float32) + offset.astype(jnp.float32), unit, inverse)


def norm_backward(gradient, unit, inverse, gains):
    scaled = gradient * gains.astype(jnp.float32)
    average = jnp.mean(scaled, -1, keepdims=True)
    second = jnp.mean(scaled * unit, -1, keepdims=True)
    return inverse * (scaled - average - unit * second)


def split_heads(tensors):
    return tuple(
        (
            tensor.reshape(tensor.shape[:-1] + (tensor.shape[-1] // HEAD_DIM, HEAD_DIM))
            for tensor in tensors
        )
    )


def project(normed, weight, biases):
    stacked = jnp.einsum("...d,cde->c...e", normed, weight, preferred_element_type=jnp.float32)
    return (
        (stacked[0] + biases[0]).astype(jnp.bfloat16),
        stacked[1].astype(jnp.bfloat16),
        (stacked[2] + biases[1]).astype(jnp.bfloat16),
    )


def attend_forward(queries, key_rows, values, keymask):
    scale_factor = HEAD_DIM ** (-0.5)
    scores = (
        jnp.einsum("bqhe,bkhe->bhqk", queries, key_rows, preferred_element_type=jnp.float32)
        * scale_factor
    )
    scores = jnp.where(keymask, scores, -1e30)
    largest = jnp.max(scores, -1, keepdims=True)
    exponent = jnp.exp(scores - largest)
    totals = jnp.sum(exponent, -1, keepdims=True)
    chances = exponent / totals
    output = jnp.einsum(
        "bhqk,bkhe->bqhe", chances.astype(jnp.bfloat16), values, preferred_element_type=jnp.float32
    )
    return (output.astype(jnp.bfloat16), largest + jnp.log(totals))


def attend_backward(queries, key_rows, values, keymask, log_total, grad_heads):
    scale_factor = HEAD_DIM ** (-0.5)
    scores = (
        jnp.einsum("bqhe,bkhe->bhqk", queries, key_rows, preferred_element_type=jnp.float32)
        * scale_factor
    )
    scores = jnp.where(keymask, scores, -1e30)
    chances = jnp.exp(scores - log_total)
    grad_chances = jnp.einsum(
        "bqhe,bkhe->bhqk", grad_heads, values, preferred_element_type=jnp.float32
    )
    deltas = jnp.sum(chances * grad_chances, -1, keepdims=True)
    grad_scores = (chances * (grad_chances - deltas)).astype(jnp.bfloat16)
    grad_query = (
        jnp.einsum("bhqk,bkhe->bqhe", grad_scores, key_rows, preferred_element_type=jnp.float32)
        * scale_factor
    ).astype(jnp.bfloat16)
    grad_key = (
        jnp.einsum("bhqk,bqhe->bkhe", grad_scores, queries, preferred_element_type=jnp.float32)
        * scale_factor
    ).astype(jnp.bfloat16)
    grad_value = jnp.einsum(
        "bhqk,bqhe->bkhe",
        chances.astype(jnp.bfloat16),
        grad_heads,
        preferred_element_type=jnp.float32,
    ).astype(jnp.bfloat16)
    return (grad_query, grad_key, grad_value)


PINNED = True


def dot(left, right, left_dim=1, right_dim=0):
    return lax.dot_general(
        left, right, (((left_dim,), (right_dim,)), ((), ())), preferred_element_type=full
    )


def unit_of(value):
    centered = value - jnp.mean(value, -1, keepdims=True)
    inverse = lax.rsqrt(jnp.mean(centered * centered, -1, keepdims=True) + epsilon)
    return centered * inverse, inverse


def unit_backward(scaled, unit, inverse):
    average = jnp.mean(scaled, -1, keepdims=True)
    second = jnp.mean(scaled * unit, -1, keepdims=True)
    return inverse * (scaled - average - unit * second)


def row_sum(value):
    return jnp.sum(value, 0, keepdims=True)


def lane_mask(width, head):
    lane = lax.broadcasted_iota(jnp.int32, (1, width), 1)
    return (lane >= head * HEAD_DIM) & (lane < (head + 1) * HEAD_DIM)


def call_kernel(body, inputs, outputs, scratch, name, scalars=(), micros=3, loose=None, extras=(), pinned=True, whole=False):
    def large(shape, dtype):
        if loose == 0 or (len(shape) == 2 and shape[0] == loose):
            return False
        return jnp.dtype(dtype).itemsize * math.prod(shape) > 2**17

    big_in = [
        (whole and k not in scalars) or (pinned and large(each.shape, each.dtype))
        for k, each in enumerate(inputs)
    ]
    big_out = [large(*each) for each in outputs]
    count = len(inputs) + len(outputs)

    def kernel(*refs):
        refs = refs[: len(inputs)] + refs[len(inputs) + len(extras) :]
        outer, spare = refs[:count], list(refs[count:])
        queue, coming, going = [], {}, []
        in_marks, out_marks = spare[-2:]
        targets = {}
        for k, ref in enumerate(outer):
            is_input = k < len(inputs)
            n = k if is_input else k - len(inputs)
            if not (big_in[n] if is_input else big_out[n]):
                queue.append(ref)
                continue
            buffer = spare.pop(len(scratch))
            queue.append(buffer)
            if is_input:
                copy = pltpu.make_async_copy(ref, buffer, in_marks.at[n])
                copy.start()
                coming[id(buffer)] = copy
            else:
                targets[id(buffer)] = pltpu.make_async_copy(buffer, ref, out_marks.at[n])
        queue += spare[: len(scratch)]
        handed = list(queue)

        def wait(*each):
            for ref in each:
                copy = coming.pop(id(ref), None)
                if copy is not None:
                    copy.wait()

        def send(*each):
            for ref in each:
                copy = targets.pop(id(ref), None)
                if copy is not None:
                    copy.start()
                    going.append(copy)

        body(lambda k: [queue.pop(0) for _ in range(k)], wait, send)
        wait(*handed)
        send(*handed)
        for copy in going:
            copy.wait()

    def spec(big, k=None):
        if k in scalars:
            return pl.BlockSpec(memory_space=pltpu.SMEM)
        return pl.BlockSpec(memory_space=pltpu.HBM if big else pltpu.VMEM)

    buffers = [pltpu.VMEM(each.shape, each.dtype) for each, big in zip(inputs, big_in) if big]
    buffers += [pltpu.VMEM(*each) for each, big in zip(outputs, big_out) if big]
    marks = [pltpu.SemaphoreType.DMA((len(inputs),)), pltpu.SemaphoreType.DMA((len(outputs),))]
    return list(
        pl.pallas_call(
            kernel,
            out_shape=[jax.ShapeDtypeStruct(*each) for each in outputs],
            in_specs=[spec(big, k) for k, big in enumerate(big_in)]
            + [pl.BlockSpec(memory_space=pl.ANY)] * len(extras),
            out_specs=[spec(big) for big in big_out],
            scratch_shapes=list(scratch) + buffers + marks,
            compiler_params=pltpu.CompilerParams(vmem_limit_bytes=VMEM_LIMIT),
            cost_estimate=pl.CostEstimate(
                flops=int(micros * RATE), bytes_accessed=1024, transcendentals=0
            ),
            name=name,
        )(*inputs, *extras)
    )


def combine(marks, *outputs, extras=()):
    terms = [term for output in outputs for slot in output for term in slot]
    _, rows, features = terms[0][0].shape
    chunk = rows // 2 if rows >= 192 else rows

    def kernel(_, *refs):
        queue = list(refs)
        sums = [
            [sum(queue.pop(0)[0].astype(full) for _ in slot) for slot in output]
            for output in outputs
        ]
        for out, values in zip(queue[len(extras) :], sums):
            for k, value in enumerate(values):
                out[k] = value.astype(low)
        queue[-1][...] = jnp.zeros((8, 128), full)

    def place(_, base, *steps):
        return lambda c, s: (base + sum(step * s[k] for k, step in enumerate(steps) if step), c, 0)

    return pl.pallas_call(
        kernel,
        grid_spec=pltpu.PrefetchScalarGridSpec(
            num_scalar_prefetch=1,
            grid=(rows // chunk,),
            in_specs=[pl.BlockSpec((1, chunk, features), place(*term)) for term in terms]
            + [pl.BlockSpec(memory_space=pl.ANY)] * len(extras),
            out_specs=[
                pl.BlockSpec((len(output), chunk, features), lambda c, s: (0, c, 0))
                for output in outputs
            ]
            + [pl.BlockSpec((8, 128), lambda c, s: (0, 0))],
        ),
        out_shape=[jax.ShapeDtypeStruct((len(each), rows, features), low) for each in outputs]
        + [jax.ShapeDtypeStruct((8, 128), full)],
        compiler_params=pltpu.CompilerParams(vmem_limit_bytes=VMEM_LIMIT),
        cost_estimate=pl.CostEstimate(flops=1024, bytes_accessed=1024, transcendentals=0),
        name="combine",
    )(marks, *[term[0] for term in terms], *extras)


def spread(pieces, marks, split):
    _, rows, features = pieces[0].shape

    def body(take, wait, send):
        (mark_ref,) = take(1)
        piece_refs = take(4)
        first_ref, second_ref = take(2)
        for k, piece in enumerate(piece_refs):
            wait(piece)
            outer, inner = mark_ref[0] ^ (k // 2), mark_ref[1] ^ (k % 2)
            begin = pl.multiple_of((outer * 2 + inner) * rows, 8)
            first_ref[pl.ds(begin, rows)] = piece[0].astype(full)
            if not split:
                second_ref[pl.ds(begin, rows)] = piece[1].astype(full)
            else:

                @pl.when(outer == 0)
                def _(piece=piece, begin=begin):
                    first_ref[pl.ds(4 * rows + begin, rows)] = piece[1].astype(full)

                @pl.when(outer == 1)
                def _(piece=piece, inner=inner):
                    at = pl.ds(pl.multiple_of(inner * rows, 8), rows)
                    second_ref[at] = piece[1].astype(full)

    sizes = (6, 2) if split else (4, 4)
    outputs = [((size * rows, features), full) for size in sizes]
    return call_kernel(body, [marks, *pieces], outputs, [], "spread", (0,), 0.01, 0)


def prepare(marks, qkv, out, extra, fc1, fc2, extras):
    width, features = out.shape
    units = fc2.shape[0]
    half = units // 2
    size = 4 * width + extra.shape[0]

    def body(take, wait, send):
        mark_ref, qkv_ref, out_ref, extra_ref, fc1_ref, fc2_ref = take(6)
        pack_ref, half_ref, fcs_ref, first_ref, second_ref = take(5)
        wait(qkv_ref, out_ref, extra_ref)
        pack_ref[: 3 * width] = qkv_ref[...]
        pack_ref[3 * width : 4 * width] = out_ref[...]
        pack_ref[4 * width :] = extra_ref[...]
        here = mark_ref[0]
        half_ref[...] = pack_ref[pl.ds(pl.multiple_of(here * (size // 2), 16), size // 2)]
        send(pack_ref, half_ref)
        wait(fc1_ref, fc2_ref)
        for k in range(2):
            fcs_ref[2 * k] = fc1_ref[:, k * half : (k + 1) * half].T
            fcs_ref[2 * k + 1] = fc2_ref[k * half : (k + 1) * half]
        first_ref[0] = fcs_ref[2 * here]
        second_ref[0] = fcs_ref[2 * here + 1]

    outputs = [((size, features), low), ((size // 2, features), low)]
    outputs += [((4, half, features), low)] + [((1, half, features), low)] * 2
    inputs = [marks, qkv, out, extra, fc1, fc2]
    return call_kernel(body, inputs, outputs, [], "prepare", (0,), extras=extras)


def message_start(marks, leads, weight, bias, extras):
    slots, _ = leads[0].shape
    width = weight.shape[0]

    def body(take, wait, send):
        (mark_ref,) = take(1)
        lead_refs = take(len(leads))
        weight_ref, bias_ref = take(2)
        lead_ref, part_ref = take(2)
        here = mark_ref[2]
        lead = lead_refs[0][...].astype(full)
        for k in range(1, len(leads)):
            lead = jnp.where(here == k, lead_refs[k][...].astype(full), lead)
        lead_ref[...] = lead
        part_ref[...] = dot(lead.astype(low), weight_ref[...], 1, 1) + bias_ref[...]

    outputs = [(leads[0].shape, full), ((slots, width), full)]
    inputs = [marks, *leads, weight, bias]
    return call_kernel(body, inputs, outputs, [], "message_start", (0,), 0.01, 0, extras)


def message_forward(message, norm, qkv, out, bias, key_row, extras):
    slots, features = message.shape
    width = out.shape[0]

    def body(take, wait, send):
        message_ref, norm_ref, qkv_ref, out_ref, bias_ref, key_ref = take(6)
        normed_ref, saved_ref, part_ref = take(3)
        wait(message_ref, qkv_ref, out_ref)
        unit, _ = unit_of(message_ref[...])
        normed = (unit * norm_ref[0:1] + norm_ref[1:2]).astype(low)
        normed_ref[...] = normed.astype(full)
        query, key, value = [
            dot(normed, qkv_ref[k * width : (k + 1) * width], 1, 1) for k in range(3)
        ]
        query = (query + bias_ref[0:1]).astype(low)
        key = key.astype(low)
        value = (value + bias_ref[1:2]).astype(low)
        result = jnp.zeros((slots, width), full)
        for j in range(width // HEAD_DIM):
            mask = lane_mask(width, j)
            scaled = query.astype(full) * HEAD_DIM ** (-0.5)
            one = jnp.where(mask, scaled, jnp.zeros_like(scaled)).astype(low)
            scores = dot(one, key, 1, 1) + key_ref[...]
            exponent = jnp.exp(scores - jnp.max(scores, -1, keepdims=True))
            chances = exponent / jnp.sum(exponent, -1, keepdims=True)
            result = jnp.where(mask, dot(chances.astype(low), value), result)
        result = result.astype(low)
        for k, each in enumerate((query, key, value, result)):
            saved_ref[k] = each.astype(full)
        part_ref[...] = dot(result, out_ref[...])

    outputs = [((slots, features), full), ((4, slots, width), full), ((slots, features), full)]
    inputs = [message, norm, qkv, out, bias, key_row]
    return call_kernel(body, inputs, outputs, [], "message_forward", (), 0.01, 0, extras)


def message_backward(grad_message, saved, qkv, out, key_row, extras):
    slots, features = grad_message.shape
    width = out.shape[0]

    def body(take, wait, send):
        grad_ref, saved_ref, qkv_ref, out_ref, key_ref = take(5)
        stacked_ref, part_ref = take(2)
        wait(saved_ref, qkv_ref, out_ref)
        grad_o = dot(grad_ref[...].astype(low), out_ref[...], 1, 1).astype(low).astype(full)
        scaled = saved_ref[0] * HEAD_DIM ** (-0.5)
        key, value = saved_ref[1].astype(low), saved_ref[2].astype(low)
        grad_q = grad_k = grad_v = jnp.zeros((slots, width), full)
        for j in range(width // HEAD_DIM):
            mask = lane_mask(width, j)
            one_query = jnp.where(mask, scaled, jnp.zeros_like(scaled)).astype(low)
            one_grad = jnp.where(mask, grad_o, jnp.zeros_like(grad_o)).astype(low)
            scores = dot(one_query, key, 1, 1) + key_ref[...]
            exponent = jnp.exp(scores - jnp.max(scores, -1, keepdims=True))
            chances = exponent / jnp.sum(exponent, -1, keepdims=True)
            grad_p = dot(one_grad, value, 1, 1)
            grad_s = chances * (grad_p - jnp.sum(chances * grad_p, -1, keepdims=True))
            grad_s = grad_s.astype(low)
            grad_v += dot(chances.astype(low), one_grad, 0, 0)
            grad_k += dot(grad_s, one_query, 0, 0)
            grad_q = jnp.where(mask, dot(grad_s, key), grad_q)
        grads = [each.astype(low) for each in (grad_q * HEAD_DIM ** (-0.5), grad_k, grad_v)]
        for k, each in enumerate(grads):
            stacked_ref[k] = each.astype(full)
        part_ref[...] = sum(
            dot(each, qkv_ref[k * width : (k + 1) * width]) for k, each in enumerate(grads)
        )

    outputs = [((3, slots, width), full), ((slots, features), full)]
    inputs = [grad_message, saved, qkv, out, key_row]
    return call_kernel(body, inputs, outputs, [], "message_backward", (), 0.01, 0, extras)


def message_bundle(marks, part, one_sums, two_sums, hidden, heads):
    slots, features = part.shape
    width = heads[0].shape[1]
    half = features // 2

    def body(take, wait, send):
        mark_ref, part_ref, one_ref, two_ref = take(4)
        near_refs, far_refs, head_refs = take(2), take(4), take(4)
        (out_ref,) = take(1)
        wait(part_ref, one_ref, two_ref, *near_refs, *far_refs, *head_refs)
        out_ref[...] = jnp.zeros(out_ref.shape, full)
        out_ref[:slots] = part_ref[...]
        out_ref[slots : slots + 2] = one_ref[...]
        out_ref[slots + 2 : slots + 6] = two_ref[...]
        bit, here = mark_ref[0], mark_ref[2]
        for k in range(4):
            if k < 2:
                first, second = near_refs[k][0:1], near_refs[k][1:2]
            else:
                own, other = far_refs[2 * k - 4][...], far_refs[2 * k - 3][...]
                first, second = jnp.where(bit == 0, own, other), jnp.where(bit == 0, other, own)
            row = pl.ds(slots + 6 + (here ^ k), 1)
            out_ref[row, :half] = first
            out_ref[row, half:] = second
            row = pl.ds(slots + 10 + (here ^ k), 1)
            out_ref[row, :width] = head_refs[k][0:1]
            out_ref[row, 256 : 256 + width] = head_refs[k][1:2]

    inputs = [marks, part, one_sums, two_sums, *hidden, *heads]
    outputs = [((slots + 16, features), full)]
    return call_kernel(body, inputs, outputs, [], "message_bundle", (0,), 0.01, 0, whole=True)[0]


def message_finish(marks, bundles, grad_message, message, norm, normed, lead, stacked, saved, weight, field, extras):
    slots, features = message.shape
    width = weight.shape[0]
    groups = features // width

    def body(take, wait, send):
        mark_ref, bundle_ref, grad_ref, message_ref, norm_ref, normed_ref = take(6)
        lead_ref, stacked_ref, saved_ref, weight_ref = take(4)
        out_ref, part_ref = take(2)
        here = mark_ref[2]
        bundle = sum(bundle_ref[k] for k in range(groups))

        def cut(value):
            result = value[:, :width]
            for k in range(1, groups):
                result = jnp.where(here == k, value[:, k * width : (k + 1) * width], result)
            return result

        def own_row(first):
            result = bundle[first : first + 1]
            for k in range(1, groups):
                result = jnp.where(here == k, bundle[first + k : first + k + 1], result)
            return result

        grad_normed = bundle[:slots]
        unit, inverse = unit_of(message_ref[...])
        grad = grad_ref[...]
        columns = cut(grad + unit_backward(grad_normed * norm_ref[0:1], unit, inverse)).astype(low)
        part_ref[...] = dot(columns, weight_ref[...])
        at = 0
        for value in (normed_ref[...], grad, lead_ref[...]):
            out_ref[:, at : at + features] = value
            at += features
        for value in (stacked_ref[0], stacked_ref[1], stacked_ref[2], saved_ref[3], columns):
            out_ref[:, at : at + field] = jnp.zeros((slots, field), full)
            out_ref[:, at : at + width] = value.astype(full)
            at += field
        out_ref[:, at:] = jnp.zeros((slots, 512), full)
        out_ref[0:6, at : at + width] = cut(bundle[slots : slots + 6])
        units, heads = own_row(slots + 6), own_row(slots + 10)
        half = features // 2
        out_ref[6:7, at : at + half] = units[:, :half]
        out_ref[7:8, at : at + half] = units[:, half:]
        side = at + 256
        out_ref[0:1, side : side + width] = cut(row_sum(grad_normed * unit))
        out_ref[1:2, side : side + width] = cut(row_sum(grad_normed))
        out_ref[2:3, side : side + width] = heads[:, :width]
        out_ref[3:4, side : side + width] = heads[:, 256 : 256 + width]

    inputs = [marks, bundles, grad_message, message, norm, normed, lead, stacked, saved, weight]
    outputs = [((slots, 3 * features + 5 * field + 512), full), ((slots, features), full)]
    return call_kernel(body, inputs, outputs, [], "message_finish", (0,), 0.01, 0, extras)


def message_weights(operands, features, width, field, count):
    rows, total = operands.shape
    slots = rows // count
    starts = [k * features for k in range(3)] + [3 * features + k * field for k in range(5)]
    last = 3 * features + 5 * field

    def body(take, wait, send):
        (rows_ref,) = take(1)
        wait(rows_ref)
        qkv_ref, out_ref, fc_ref, heads_ref, grad_ref, cols_ref, own_ref = take(7)
        wide = [rows_ref[:, at : at + features] for at in starts[:3]]
        thin = [rows_ref[:, at : at + width] for at in starts[3:]]
        for k in range(3):
            qkv_ref[k * width : (k + 1) * width] = dot(thin[k], wide[0], 0, 0)
        out_ref[...] = dot(thin[3], wide[1], 0, 0)
        fc_ref[...] = dot(thin[4], wide[2], 0, 0)
        heads_ref[...] = jnp.concatenate(
            [row_sum(thin[0].astype(full)), row_sum(thin[2].astype(full))], 0
        )
        grad_ref[...] = row_sum(wide[1].astype(full))
        cols_ref[...] = row_sum(thin[4].astype(full))
        own = rows_ref[:, last:].astype(full)
        own_ref[...] = sum(own[k * slots : (k + 1) * slots] for k in range(count))

    outputs = [
        ((3 * width, features), full),
        ((width, features), full),
        ((width, features), full),
        ((2, width), full),
        ((1, features), full),
        ((1, width), full),
        ((slots, total - last), full),
    ]
    return call_kernel(body, [operands], outputs, [], "message_weights", (), 3, 0)


def place_rows(target, value_of, mine, span, rows, near_count):
    for f in range(mine):
        for k in range(near_count):
            target[f * span + k * rows : f * span + (k + 1) * rows] = value_of(k, f).astype(full)


def frame_values(marks_ref, own_ref, came_ref, near_ref, mine):
    def value_of(k, f):
        if k == 0:
            return own_ref[marks_ref[2] * mine + f]
        if k == 2:
            return came_ref[(marks_ref[2] % 2) * mine + f]
        return near_ref[(k // 2) * mine + f]

    return value_of


def attn_heads(normed, pack, saved_ref, key_bias, mine):
    rows, _ = normed.shape
    span = rows // mine
    width = saved_ref.shape[2]
    extra = pack[4 * width : 4 * width + 16].astype(full)
    saved_ref[0] = (dot(normed, pack[:width], 1, 1) + extra[0:1, :width]).astype(low)
    saved_ref[1] = dot(normed, pack[width : 2 * width], 1, 1).astype(low)
    saved_ref[2] = (dot(normed, pack[2 * width : 3 * width], 1, 1) + extra[1:2, :width]).astype(low)
    for f in range(mine):
        at = slice(f * span, (f + 1) * span)
        query = saved_ref[0, at] * jnp.asarray(HEAD_DIM ** (-0.5), low)
        key, value = saved_ref[1, at], saved_ref[2, at]
        out = jnp.zeros((span, width), full)
        for j in range(width // HEAD_DIM):
            mask = lane_mask(width, j)
            scores = dot(jnp.where(mask, query, jnp.zeros_like(query)), key, 1, 1)
            scores = scores + key_bias
            exponent = jnp.exp(scores - jnp.max(scores, -1, keepdims=True))
            share = 1.0 / jnp.sum(exponent, -1, keepdims=True)
            out = jnp.where(mask, dot(exponent.astype(low), value) * share, out)
        saved_ref[3, at] = out.astype(low)
    return dot(saved_ref[3], pack[3 * width : 4 * width])


def attn_start(marks, frames, came, near, carried, norm, key_row, packs, mine, span, extras):
    _, rows, features = frames.shape
    width = features // 4
    groups = 4
    all_rows = groups * rows
    count = len(packs)

    def body(take, wait, send):
        marks_ref, own_ref, came_ref, near_ref, carried_ref, norm_ref, key_ref = take(7)
        pack_refs = take(count)
        joined_ref, normed_ref, total_ref, token_ref = take(4)
        saved_refs = take(count)
        token_ref[...] = jnp.zeros((8, 128), full)
        (joined,) = take(1)
        wait(own_ref, came_ref, near_ref)
        for f in range(mine):
            end = (f + 1) * span
            joined[f * span + all_rows : end] = jnp.zeros((span - all_rows, features), full)
            joined[f * span + all_rows : f * span + all_rows + 1] = carried_ref[f : f + 1]
        value_of = frame_values(marks_ref, own_ref, came_ref, near_ref, mine)
        place_rows(joined, value_of, mine, span, rows, groups)
        joined_ref[...] = joined[...].astype(low)
        unit, _ = unit_of(joined_ref[...].astype(full))
        normed_ref[...] = (unit * norm_ref[0:1] + norm_ref[1:2]).astype(low)
        send(joined_ref, normed_ref)
        for b in range(count):
            wait(pack_refs[b])
            part = attn_heads(normed_ref[...], pack_refs[b], saved_refs[b], key_ref[...], mine)
            send(saved_refs[b])
            total_ref[...] = total_ref[...] + part if b else part

    size = mine * span
    inputs = [marks, frames, came, near, carried, norm, key_row, *packs]
    outputs = [((size, features), low)] * 2 + [((size, features), full), ((8, 128), full)]
    outputs += [((4, size, width), low)] * count
    scratch = [pltpu.VMEM((size, features), full)]
    results = call_kernel(body, inputs, outputs, scratch, "attn_start", (0,), 9, size, extras)
    return results[:4], results[4:]


def attn_rest(marks, normed, total, key_row, halves, mine, extras):
    rows, features = normed.shape
    width = features // 4
    count = len(halves)

    def body(take, wait, send):
        marks_ref, normed_ref, total_in, key_ref = take(4)
        half_refs = [take(2) for _ in range(count)]
        total_ref, token_ref = take(2)
        pack_refs, saved_refs = take(count), take(count)
        token_ref[...] = jnp.zeros((8, 128), full)
        here = marks_ref[0]
        wait(normed_ref)
        for b in range(count):
            wait(*half_refs[b])
            size = half_refs[b][0].shape[0]
            for k, each in enumerate(half_refs[b]):
                pack_refs[b][pl.ds(pl.multiple_of((here ^ k) * size, 16), size)] = each[...]
            send(pack_refs[b])
            part = attn_heads(normed_ref[...], pack_refs[b], saved_refs[b], key_ref[...], mine)
            send(saved_refs[b])
            wait(total_in)
            total_ref[...] = (total_ref if b else total_in)[...] + part

    inputs = [marks, normed, total, key_row] + [each for pair in halves for each in pair]
    outputs = [((rows, features), full), ((8, 128), full)]
    outputs += [((2 * own.shape[0], features), low) for own, _ in halves]
    outputs += [((4, rows, width), low)] * count
    results = call_kernel(body, inputs, outputs, [], "attn_rest", (0,), 9, rows, extras)
    return results[:2], results[2 : 2 + count], results[2 + count :]


def out_blocks(own_ref, near_ref, far_ref, source, mine, span):
    rows = own_ref.shape[1]
    for f in range(mine):
        for k in range(4):
            value = source[f * span + k * rows : f * span + (k + 1) * rows].astype(low)
            if k < 2:
                (near_ref if k else own_ref)[f] = value
            else:
                far_ref[k - 2, f] = value


def mlp_step(start, carry, grad, consts, weights, biases, last, mine, rows, extras):
    first = carry is None
    total_rows, features = start[0].shape
    span = total_rows // mine
    size = biases[0].shape[1]
    count = len(weights)
    lengths = [[each.shape[0] for each in group] for group in weights]

    def body(take, wait, send):
        if first or last:
            joined_ref, total_ref, const_ref = take(3)
        if first:
            grad_sources = take(4)
        else:
            normed_ref, y_in, d_in, grad_ref = take(4)
        fc_bases = [take(len(group)) for group in lengths]
        fc_refs = [
            [ref.at[k] for ref, n in zip(refs, group) for k in range(n)]
            for refs, group in zip(fc_bases, lengths)
        ]
        bias_refs = take(count)
        if last:
            own_ref, near_ref, far_ref, mixed_ref, attn_ref, sums_ref = take(6)
        else:
            y_ref, d_ref = take(2)
        if first:
            normed_ref, grad_ref = take(2)
        w_refs, b_refs = take(count), take(count)
        if last:
            y_ref, d_ref = take(2)

        def mixed():
            return joined_ref[...].astype(full) + total_ref[...] + const_ref[0:1]

        if first:
            wait(*grad_sources)
            for f in range(mine):
                end = (f + 1) * span
                d_ref[f * span + 4 * rows : end] = jnp.zeros((span - 4 * rows, features), full)
            place_rows(d_ref, frame_values(*grad_sources, mine), mine, span, rows, 4)
            grad_ref[...] = d_ref[...].astype(low)
            wait(joined_ref, total_ref)
            unit, _ = unit_of(mixed())
            normed_ref[...] = (unit * const_ref[1:2] + const_ref[2:3]).astype(low)
            send(grad_ref, normed_ref)
        else:
            wait(normed_ref, grad_ref)
        normed = normed_ref[...]
        grad_rows = grad_ref[...]
        fresh = True
        for b in range(count):
            wait(*fc_bases[b])
            for c in range(len(fc_refs[b]) // 2):
                fc1, fc2 = fc_refs[b][2 * c][...], fc_refs[b][2 * c + 1][...]
                pre = dot(normed, fc1, 1, 1) + bias_refs[b][c : c + 1]
                gate = jax.nn.sigmoid(1.702 * pre)
                active = (pre * gate).astype(low)
                back = dot(grad_rows, fc2, 1, 1) * (gate + 1.702 * pre * gate * (1.0 - gate))
                back = back.astype(low)
                b_refs[b][c : c + 1] = row_sum(back.astype(full))
                y_part = dot(active, fc2)
                d_part = dot(back, fc1)
                if not fresh:
                    y_ref[...] += y_part
                    d_ref[...] += d_part
                elif first:
                    y_ref[...] = y_part
                    d_ref[...] = d_part
                else:
                    wait(y_in, d_in)
                    y_ref[...] = y_in[...] + y_part
                    d_ref[...] = d_in[...] + d_part
                fresh = False
                w_refs[b][2 * c] = dot(back, normed, 0, 0).astype(low)
                w_refs[b][2 * c + 1] = dot(active, grad_rows, 0, 0).astype(low)
            send(w_refs[b])
        if last:
            wait(joined_ref, total_ref)
            value = mixed()
            unit, inverse = unit_of(value)
            y_ref[...] = value + y_ref[...] + const_ref[3:4]
            out_blocks(own_ref, near_ref, far_ref, y_ref, mine, span)
            send(far_ref, near_ref, own_ref)
            grad_normed = d_ref[...]
            top = grad_rows.astype(full)
            grad_mixed = top + unit_backward(grad_normed * const_ref[1:2], unit, inverse)
            mixed_ref[...] = grad_mixed
            grad_attn = grad_mixed.astype(low)
            attn_ref[...] = grad_attn
            sums_ref[...] = jnp.concatenate(
                [
                    row_sum(grad_attn.astype(full)),
                    row_sum(grad_normed * unit),
                    row_sum(grad_normed),
                    row_sum(top),
                ],
                0,
            )

    big = ((total_rows, features), full)
    small = ((total_rows, features), low)
    inputs = [*start, consts] if first or last else []
    inputs += list(grad) if first else [*carry, grad]
    scalars = (3,) if first else ()
    inputs += [each for group in weights for each in group] + list(biases)
    if last:
        outputs = [((mine, rows, features), low)] * 2 + [((2, mine, rows, features), low)]
        outputs += [big, small, ((4, features), full)]
    else:
        outputs = [big, big]
    outputs += [small, small] if first else []
    lead = len(outputs)
    outputs += [((sum(group), size, features), low) for group in lengths]
    outputs += [(each.shape, full) for each in biases]
    scratch = [pltpu.VMEM((total_rows, features), full)] * 2 if last else []
    results = call_kernel(body, inputs, outputs, scratch, "mlp_step", scalars, 12, total_rows, extras, PINNED)
    return results[:lead], results[lead : lead + count], results[lead + count :]


def attn_backward(normed, grad, key_column, total, packs, saved, mine, frame_rows, ending, extras):
    rows, features = normed.shape
    span = rows // mine
    width = features // 4
    count = len(packs)
    first = total is None
    last = ending is not None

    def body(take, wait, send):
        normed_ref, grad_ref, key_ref = take(3)
        if not first:
            (total_in,) = take(1)
        if last:
            joined_ref, mixed_ref, norm_ref = take(3)
        pack_refs = take(count)
        saved_refs = take(count)
        q_refs, k_refs, v_refs, o_refs = [[each.at[k] for each in saved_refs] for k in range(4)]
        if last:
            own_ref, near_ref, far_ref, carried_ref, sums_ref = take(5)
        else:
            (total_ref,) = take(1)
        w_refs, b_refs = take(count), take(count)
        dq_ref, dk_ref, dv_ref, do_ref = take(4)
        if last:
            (total_ref,) = take(1)
        wait(normed_ref, grad_ref, key_ref)
        normed = normed_ref[...]
        grad = grad_ref[...]
        key_bias = key_ref[...]
        scale = HEAD_DIM ** (-0.5)
        for b in range(count):
            pack = pack_refs[b]
            wait(pack, saved_refs[b])
            do_ref[...] = dot(grad, pack[3 * width : 4 * width], 1, 1).astype(low)
            for f in range(mine):
                at = slice(f * span, (f + 1) * span)
                query = q_refs[b][at] * jnp.asarray(scale, low)
                key, value, grad_o = k_refs[b][at], v_refs[b][at], do_ref[at]
                grad_q = grad_k = grad_v = jnp.zeros((span, width), full)
                for j in range(width // HEAD_DIM):
                    mask = lane_mask(width, j)
                    one_query = jnp.where(mask, query, jnp.zeros_like(query))
                    one_grad = jnp.where(mask, grad_o, jnp.zeros_like(grad_o))
                    scores = dot(key, one_query, 1, 1) + key_bias
                    exponent = jnp.exp(scores - jnp.max(scores, 0, keepdims=True))
                    chances = exponent * (1.0 / row_sum(exponent))
                    grad_p = dot(value, one_grad, 1, 1)
                    grad_s = (chances * (grad_p - row_sum(chances * grad_p))).astype(low)
                    grad_v += dot(chances.astype(low), one_grad)
                    grad_k += dot(grad_s, one_query)
                    grad_q = jnp.where(mask, dot(grad_s, key, 0, 0), grad_q)
                dq_ref[at] = (grad_q * scale).astype(low)
                dk_ref[at] = grad_k.astype(low)
                dv_ref[at] = grad_v.astype(low)
            grads = (dq_ref[...], dk_ref[...], dv_ref[...])
            part = sum(dot(each, pack[k * width : (k + 1) * width]) for k, each in enumerate(grads))
            if b:
                total_ref[...] += part
            else:
                if not first:
                    wait(total_in)
                total_ref[...] = part if first else total_in[...] + part
            for k, each in enumerate(grads):
                w_refs[b][k] = dot(each, normed, 0, 0).astype(low)
            w_refs[b][3] = dot(o_refs[b][...], grad, 0, 0).astype(low)
            send(w_refs[b])
            b_refs[b][...] = jnp.concatenate(
                [row_sum(grads[0].astype(full)), row_sum(grads[2].astype(full))], 0
            )
        if last:
            wait(joined_ref, mixed_ref)
            unit, inverse = unit_of(joined_ref[...].astype(full))
            grad_normed = total_ref[...]
            grad_joined = unit_backward(grad_normed * norm_ref[0:1], unit, inverse)
            total_ref[...] = mixed_ref[...] + grad_joined
            all_rows = 4 * frame_rows
            for f in range(mine):
                at = f * span + all_rows
                carried_ref[f : f + 1] = total_ref[at : at + 1]
            out_blocks(own_ref, near_ref, far_ref, total_ref, mine, span)
            send(far_ref, near_ref, own_ref)
            sums_ref[...] = jnp.concatenate(
                [row_sum(grad_normed * unit), row_sum(grad_normed)], 0
            )

    inputs = [normed, grad, key_column] + ([] if first else [total]) + list(ending or ())
    inputs += [*packs, *saved]
    if last:
        outputs = [((mine, frame_rows, features), low)] * 2
        outputs += [((2, mine, frame_rows, features), low)]
        outputs += [((mine, features), full), ((2, features), full)]
    else:
        outputs = [((rows, features), full)]
    lead = len(outputs)
    outputs += [((4, width, features), low)] * count + [((2, width), full)] * count
    scratch = [pltpu.VMEM((rows, width), low)] * 4
    scratch += [pltpu.VMEM((rows, features), full)] if last else []
    results = call_kernel(body, inputs, outputs, scratch, "attn_backward", (), 9, rows, extras)
    grads = [(results[lead + b], results[lead + count + b]) for b in range(count)]
    return results[:lead], grads


def swap(value, axis, offset):
    size = lax.axis_size(axis)
    return lax.ppermute(value, axis, [(place, place ^ offset) for place in range(size)])


def pick(value, index, count, dimension=0):
    return lax.dynamic_slice_in_dim(value, index * count, count, dimension)


def add(*values):
    return sum(value.astype(full) for value in values).astype(low)


def hold(*values):
    return lax.optimization_barrier(values)


def tie(value, token):
    return value + token[:1, :1]


def everyone(value):
    size = lax.axis_size("heads")
    return [value] + [swap(value, "heads", k) for k in range(1, size)]


def by_place(pieces, here):
    stacked = jnp.stack(pieces)
    return [lax.dynamic_index_in_dim(stacked, here ^ k, 0, False) for k in range(len(pieces))]


def frame_pieces(frames, here, groups):
    mine = frames.shape[0] // groups
    return [pick(frames, here ^ k, mine) for k in range(groups)]


def send_each(pieces):
    return [swap(piece, "heads", k) if k else piece for k, piece in enumerate(pieces)]


def on_device(
    frames,
    out_grad,
    frame_tokens,
    frame_count,
    msg_fc_w,
    msg_fc_b,
    msg_norm_g,
    msg_norm_b,
    msg_qkv_w,
    msg_qkv_b,
    msg_out_w,
    msg_out_b,
    norm1_g,
    norm1_b,
    attn_qkv_w,
    attn_qkv_b,
    attn_out_w,
    attn_out_b,
    norm2_g,
    norm2_b,
    fc1_w,
    fc1_b,
    fc2_w,
    fc2_b,
):
    _, slots, rows, features = frames.shape
    groups = lax.axis_size("heads")
    videos = lax.axis_size("videos")
    here = lax.axis_index("heads")
    video = lax.axis_index("videos")
    bit = video % 2
    far = groups // 2
    mine = slots // groups
    span = -(-(rows * groups + 1) // 16) * 16
    tail = span - rows * groups
    width = msg_fc_w.shape[1]
    units = fc1_w.shape[1]
    half = units // 2
    quick = videos == 8
    pair_bit = (video // 2) % 2
    frames = frames[0]
    out_grad = out_grad[0]
    marks = [bit, pair_bit, here, here ^ 1, here % 2, (here // 2) ^ 1]
    marks = jnp.stack(marks).astype(jnp.int32)
    stack = lambda *vectors: jnp.stack(vectors).astype(full)
    link = lambda value: swap(value, "heads", far)
    side = lambda value: swap(value, "heads", 1)
    pair = lambda value: swap(value, "videos", 1)
    two = range(mine)
    far_rows = lambda value: [[(value, k, 0, 0, 0, 0, 0, far * mine)] for k in range(far * mine)]
    near_rows = lambda value, came: [[(value, k, 0, 0, 0, mine)] for k in two] + [
        [(came, mine + k, 0, 0, 0, 0, -mine)] for k in two
    ]

    leads = everyone(frames[:, 0, :])
    row_send, _ = combine(marks, [each for each in far_rows(frames)])
    row_came = link(row_send)
    leading, fc_part = message_start(
        marks, leads, msg_fc_w.T, msg_fc_b[None].astype(full), [row_send]
    )
    columns = everyone(fc_part)
    wide = lambda value: jnp.pad(value, ((0, 0), (0, features - value.shape[1])))
    extra = jnp.concatenate(
        [wide(attn_qkv_b), wide(fc1_b[None]), jnp.zeros((29, features), low)], 0
    )
    pack, pack_send, fcs, fc_send_1, fc_send_2 = prepare(
        marks,
        attn_qkv_w.transpose(0, 2, 1).reshape(3 * width, features),
        attn_out_w,
        extra,
        fc1_w,
        fc2_w,
        [fc_part],
    )
    pack_own = link(pack_send)
    message = jnp.concatenate(by_place(columns, here), 1)
    msg_norm = stack(msg_norm_g, msg_norm_b)
    msg_key = jnp.where(jnp.arange(slots) < frame_count[0], 0.0, -1e30).astype(full)[None]
    msg_qkv = msg_qkv_w.transpose(0, 2, 1).reshape(3 * width, features)
    msg_in, msg_saved, msg_part = message_forward(
        message, msg_norm, msg_qkv, msg_out_w, msg_qkv_b.astype(full), msg_key, [pack_send]
    )
    msg_pieces = frame_pieces(msg_part, here, groups)
    msg_rows = send_each(msg_pieces)
    row_next, token = combine(marks, near_rows(frames, row_came), extras=msg_pieces)
    row_near = side(row_next)
    pack_near = side(pack)
    grad_send, token = combine(marks, far_rows(out_grad), extras=[token])
    carried = tie(pick(message + msg_out_b, here, mine) + sum(msg_rows), token)

    places = jnp.concatenate([(here ^ k) * rows + jnp.arange(rows) for k in range(groups)])
    seen = jnp.concatenate([places < frame_tokens[0], jnp.arange(tail) == 0])
    key_bias = jnp.where(seen, 0.0, -1e30).astype(full)
    norm = stack(norm1_g, norm1_b)
    pack_own, carried = hold(pack_own, carried)
    pack_other, pack_own_3 = pair(pack_own), side(pack_own)
    grad_came = link(grad_send)
    (joined, normed, total, token), saved = attn_start(
        marks,
        frames,
        row_came,
        row_near,
        carried,
        norm,
        key_bias[None],
        [pack, pack_near],
        mine,
        span,
        [pack_own],
    )
    fc_own_1 = link(fc_send_1)
    token, pack_other = hold(token, pack_other)
    pack_other_3 = side(pack_other)
    grad_next, _ = combine(marks, near_rows(out_grad, grad_came), extras=[token])
    grad_near = side(grad_next)
    fc_near = side(fcs)
    halves = [(pack_own, pack_other), (pack_own_3, pack_other_3)]
    (total, token), far_packs, rest = attn_rest(
        marks, normed, total, key_bias[None], halves, mine, [grad_next]
    )
    saved += rest
    packs = [pack, pack_near, *far_packs]
    token, fc_own_1 = hold(token, fc_own_1)
    fc_own_2, fc_other_1, fc_own_31 = link(fc_send_2), pair(fc_own_1), side(fc_own_1)

    consts = stack(attn_out_b, norm2_g, norm2_b, fc2_b)
    bias = [each[4 * width + 2].reshape(2, half).astype(full) for each in packs]
    order = lambda value: jnp.concatenate([pick(value, bit, 1), pick(value, 1 - bit, 1)], 0)
    bias = bias[:2] + [order(each) for each in bias[2:]]
    parts = [[each[:1] for each in bias[:1:-1]], [each[1:] for each in bias[:1:-1]]]
    start = (joined, total)
    sources = (marks, out_grad, grad_came, grad_near)
    (y_sum, d_sum, normed_two, grad_top), (w_0,), (b_0,) = mlp_step(
        start, None, sources, consts, [[fcs]], bias[:1], False, mine, rows, [token]
    )
    b_0, fc_own_2, fc_other_1 = hold(b_0, fc_own_2, fc_other_1)
    fc_other_2, fc_own_32 = pair(fc_own_2), side(fc_own_2)
    fc_other_31 = side(fc_other_1)
    carry = (normed_two, y_sum, d_sum)
    (y_sum, d_sum), (w_1,), (b_1,) = mlp_step(
        start, carry, grad_top, consts, [[fc_near]], bias[1:2], False, mine, rows, []
    )
    b_1, parts[0][0], fc_other_2 = hold(b_1, parts[0][0], fc_other_2)
    fc_other_32, w_1_came = side(fc_other_2), side(w_1)
    carry = (normed_two, y_sum, d_sum)
    units_own = [[fc_own_31, fc_own_32], [fc_own_1, fc_own_2]]
    (y_sum, d_sum), (w_3a, w_2a), (b_3a, b_2a) = mlp_step(
        start, carry, grad_top, consts, units_own, parts[0], False, mine, rows, []
    )
    w_3a_came = side(w_3a)

    near = lambda weight: [(w_0, weight, 2), (w_1_came, weight, 2)]
    near_other = lambda weight: [(w_0, 2 + weight, -2), (w_1_came, 2 + weight, -2)]
    sum_of = lambda index, *arrays: [(array, index) for array in arrays]
    by_bit = lambda index, *arrays: [(array, index, 1) for array in arrays]
    by_other = lambda index, *arrays: [(array, index + 1, -1) for array in arrays]
    token = w_3a
    if quick:
        send_2a, token = combine(marks, [near_other(1)], extras=[w_3a])
        came_2a = pair(send_2a)
    carry = (normed_two, y_sum, d_sum)
    units_other = [[fc_other_31, fc_other_32], [fc_other_1, fc_other_2]]
    ends, (w_3b, w_2b), (b_3b, b_2b) = mlp_step(
        start, carry, grad_top, consts, units_other, parts[1], True, mine, rows, [token]
    )
    out_own, out_near, out_far, grad_mixed, grad_attn, two_sums = ends
    column = key_bias[:, None]
    ending = (joined, grad_mixed, norm)

    def back(block, total, last, extras):
        results, ((weights, sums),) = attn_backward(
            normed,
            grad_attn,
            column,
            total,
            [packs[block]],
            [saved[block]],
            mine,
            rows,
            ending if last else None,
            extras,
        )
        return results, weights, sums

    w_3b_came = side(w_3b)
    token = w_3b
    extras = []
    if quick:
        send_1a, token = combine(marks, [sum_of(0, w_2a, w_3a_came)], extras=[w_3b])
        came_1a = link(send_1a)
        extras = [token, came_2a]
    (d_total,), g_1, s_1 = back(1, None, False, extras)
    g_1_came = side(g_1)
    if quick:
        send_1b, send_2b, token = combine(
            marks, [sum_of(0, w_2b, w_3b_came)], [sum_of(1, w_2b, w_3b_came)], extras=[g_1]
        )
        came_1b, came_2b = link(send_1b), pair(send_2b)
        extras = [token, came_1a]
    (d_total,), g_3, s_3 = back(3, d_total, False, extras)
    g_3_came = side(g_3)
    quarters = lambda value: value.reshape(2 * value.shape[0], -1, features)
    quarter = lambda pieces: [(quarters(array), 2 * k, 0, 1) for array, k in pieces]
    quarter_other = lambda pieces: [(quarters(array), 2 * k + 1, 0, -1) for array, k in pieces]
    if quick:
        send_1c, send_2c, keep, token = combine(
            marks,
            [near_other(0) + sum_of(0, came_1b)],
            [sum_of(1, w_2a, w_3a_came) + sum_of(0, came_2b)],
            [near(0) + sum_of(0, came_1a), near(1) + sum_of(0, came_2a)],
            extras=[g_3],
        )
        came_1c, came_2c = pair(send_1c), link(send_2c)
        extras = [token]
    (d_total,), g_2, s_2 = back(2, d_total, False, extras)
    if quick:
        far_a, far_b, token = combine(
            marks,
            [sum_of(0, g_2, g_3_came), sum_of(1, g_2, g_3_came)],
            [by_other(2, g_2, g_3_came)],
        )
        far_a_came, far_b_came = link(far_a), pair(far_b)
        extras = [token]
    by_blocks = lambda value: value.reshape(-1, rows, features)
    out_send, token = combine(
        marks, [[(by_blocks(out_far), k)] for k in range(2 * mine)], extras=[g_2, *extras]
    )
    out_came = link(out_send.reshape(out_far.shape))
    extras = [token]
    if quick:
        fc_parts = [[(keep, 0), (came_1c, 0)], [(keep, 1), (came_2c, 0)]]
        fc_out, fc_keep, token = combine(
            marks,
            [quarter_other(part) for part in fc_parts],
            [quarter(part) for part in fc_parts],
            extras=[token],
        )
        fc_came = swap(fc_out, "videos", 2)
        extras = [token]
    ends, g_0, s_0 = back(0, d_total, True, extras)
    row_own, row_near, row_far, grad_carried, one_sums = ends

    token = jnp.zeros((8, 128), full)
    if quick:
        fc_quarter, token = combine(
            marks, [sum_of(0, fc_keep, fc_came), sum_of(1, fc_keep, fc_came)], extras=[g_0]
        )
        fc_came = swap(fc_quarter, "videos", 4)
        attn_out, far_b, attn_keep, token = combine(
            marks,
            [by_other(0, g_0, g_1_came, far_a_came), by_other(2, g_0, g_1_came)],
            [by_bit(2, g_2, g_3_came) + sum_of(0, far_b_came)],
            [by_bit(0, g_0, g_1_came, far_a_came), by_bit(2, g_0, g_1_came)],
            extras=[token],
        )
        attn_came, far_b_came = pair(attn_out), link(far_b)
    grad_message = lax.all_gather(tie(grad_carried, token), "heads", axis=0, tiled=True)
    msg_stacked, msg_norm_part = message_backward(
        grad_message, msg_saved, msg_qkv, msg_out_w, msg_key, []
    )
    bundle = message_bundle(
        marks,
        msg_norm_part,
        one_sums,
        two_sums,
        [b_0, b_1, b_2a, b_2b, b_3a, b_3b],
        [s_0, s_1, s_2, s_3],
    )
    bundles = lax.all_gather(bundle, "heads")
    rows_out, token = combine(
        marks, [[(by_blocks(row_far), k)] for k in range(2 * mine)], extras=[bundles]
    )
    rows_came = link(rows_out.reshape(row_far.shape))
    if quick:
        attn_parts = [
            [(attn_keep, 0), (attn_came, 0)],
            [(attn_keep, 1), (attn_came, 1), (far_b_came, 0)],
        ]
        attn_out, attn_keep, token = combine(
            marks,
            [quarter_other(part) for part in attn_parts],
            [quarter(part) for part in attn_parts],
            extras=[token],
        )
        attn_came = swap(attn_out, "videos", 2)

    field = -(-width // 128) * 128
    operands, leading_part = message_finish(
        marks,
        bundles,
        grad_message,
        message,
        msg_norm,
        msg_in,
        leading,
        msg_stacked,
        msg_saved,
        msg_fc_w.T,
        field,
        [token],
    )
    operands = operands.astype(low)[None]
    if quick:
        came = pair(operands)
        attn_quarter, token = combine(
            marks,
            [sum_of(0, attn_keep, attn_came), sum_of(1, attn_keep, attn_came)],
            extras=[operands],
        )
        attn_came = swap(attn_quarter, "videos", 4)
        fc_quarter, token = combine(
            marks,
            [sum_of(0, fc_quarter, fc_came), sum_of(1, fc_quarter, fc_came)],
            extras=[token],
        )
        fc_second, fc_third = swap(fc_quarter, "videos", 2), pair(fc_quarter)
        token, came = hold(token, came)
        operands = jnp.concatenate([operands, came], 0)
        came = swap(operands, "videos", 2)
        token, came, leading_part, fc_second, fc_third = hold(
            token, came, leading_part, fc_second, fc_third
        )
        fc_fourth = pair(fc_second)
        operands = jnp.concatenate([operands, came], 0)
        came = swap(operands, "videos", 4)
    else:
        operands = lax.all_gather(operands, "videos", axis=0, tiled=True)
    leading_grad = jnp.sum(lax.all_gather(leading_part, "heads"), 0)
    out_came, rows_came, leading_grad = hold(out_came, rows_came, leading_grad)
    rows_near = [side(each) for each in (row_near, rows_came[1], out_near, out_came[1])]
    if quick:
        attn_quarter, token = combine(
            marks,
            [sum_of(0, attn_quarter, attn_came), sum_of(1, attn_quarter, attn_came)],
            extras=[leading_grad],
        )
        attn_second, attn_third = swap(attn_quarter, "videos", 2), pair(attn_quarter)
        token, came, fc_fourth = hold(token, came, fc_fourth)
        operands = jnp.concatenate([operands, came], 0)
    weights = message_weights(
        operands.reshape(-1, operands.shape[2]), features, width, field, videos
    )
    qkv_msg, msg_out_w_grad, fc_msg, msg_qkv_b_grad, all_grad, all_cols, own = weights

    arrange = lambda pieces: jnp.concatenate(by_place(pieces, here), 0)
    mixed_out = arrange([out_own, rows_near[2], out_came[0], rows_near[3]])
    frames_grad = arrange([row_own, rows_near[0], rows_came[0], rows_near[1]]).astype(full)
    owner = (here == 0).astype(full)
    frames_grad = frames_grad.at[:, 0, :].add(leading_grad * owner)
    if quick:
        attn_second, msg_out_w_grad = hold(attn_second, msg_out_w_grad)
        attn_fourth = pair(attn_second)
        fc1_total, fc2_total = spread(
            [fc_quarter, fc_second, fc_third, fc_fourth], marks, False
        )
        qkv_total, out_total = spread(
            [attn_quarter, attn_second, attn_third, attn_fourth], marks, True
        )
    else:
        w_2 = order(jnp.stack([w_2a, w_2b])).reshape(w_0.shape)
        w_3 = order(jnp.stack([w_3a_came, w_3b_came])).reshape(w_0.shape)
        fc_total = add(w_0, w_1_came, link(add(w_2, w_3)))
        attn_total = add(g_0, g_1_came, link(add(g_2, g_3_came)))
        fc_total, attn_total = lax.psum((fc_total, attn_total), "videos")
        fc1_total, fc2_total = [
            fc_total[k::2].reshape(units, features).astype(full) for k in range(2)
        ]
        attn_total = attn_total.astype(full)
        qkv_total, out_total = attn_total[:3].reshape(-1, features), attn_total[3]


    six = own[:6, :width]
    more = own[:4, 256 : 256 + width]
    cut = lambda value: lax.dynamic_slice_in_dim(value, here * width, width, value.ndim - 1)
    turn = lambda value: value.reshape(3, width, features).transpose(0, 2, 1)
    return (
        mixed_out[None],
        frames_grad[None],
        fc_msg.T,
        all_cols[0],
        more[0],
        more[1],
        turn(qkv_msg),
        msg_qkv_b_grad,
        msg_out_w_grad,
        cut(all_grad)[0],
        six[0],
        six[1],
        turn(qkv_total),
        more[2:],
        out_total,
        six[2],
        six[3],
        six[4],
        fc1_total.T,
        own[6:, :half].reshape(units),
        fc2_total,
        six[5],
    )


def solution(mesh):
    placed = (
        P("videos", None, "heads", None),
        P("videos", None, "heads", None),
        P("videos"),
        P("videos"),
        P(None, "heads"),
        P("heads"),
        P(),
        P(),
        P(None, None, "heads"),
        P(None, "heads"),
        P("heads", None),
        P(),
        P(),
        P(),
        P(None, None, "heads"),
        P(None, "heads"),
        P("heads", None),
        P(),
        P(),
        P(),
        P(None, "heads"),
        P("heads"),
        P("heads", None),
        P(),
    )
    return jax.shard_map(
        on_device,
        mesh=mesh,
        in_specs=placed,
        out_specs=(
            P("videos", None, "heads", None),
            P("videos", None, "heads", None),
            P(None, "heads"),
            P("heads"),
            P("heads"),
            P("heads"),
            P(None, None, "heads"),
            P(None, "heads"),
            P("heads", None),
            P("heads"),
            P("heads"),
            P("heads"),
            P(None, None, "heads"),
            P(None, "heads"),
            P("heads", None),
            P("heads"),
            P("heads"),
            P("heads"),
            P(None, "heads"),
            P("heads"),
            P("heads", None),
            P("heads"),
        ),
        check_vma=False,
    )
```
